128 devices in a mesh: tm: 4 (over y), height: 16 (over z, x_hi, core), section: 2 (over x_lo).
Axes of the slice: x: 4 (x_hi: 2, x_lo: 2; x = x_hi * 2 + x_lo), y: 4, z: 4, core: 2. Of those that a mesh axis runs over, the one named last changes fastest.
Arguments:
- video: bfloat16 [4, 16, 4, 64, 1280], P('tm', 'height'), may hold values from -6 to 6
- target: bfloat16 [4, 16, 4, 64, 1280], P('tm', 'height'), may hold values from -6 to 6
- gain: float32 [1280], replicated, may hold values from 0.25 to 1.75
- w_qkv: bfloat16 [1280, 3, 1280], P(None, None, 'section')
- w_out: bfloat16 [1280, 1280], P('section'), may hold values from -0.8984375 to 0.8984375
- neighbours: int32 [4, 16, 4, 8], P('tm', 'height'), may hold values from 0 to 255, as said below
- counts: int32 [4, 16, 4], P('tm', 'height'), may hold values from 1 to 64, as said below
Outputs:
- video_grad: bfloat16 [4, 16, 4, 64, 1280], P('tm', 'height', None, None, 'section')
The draws below stay inside these ranges and needn't reach their ends.
Inputs may be any that keep to these rules, and one draw needn't show every extreme that they name: `neighbours`: row i lists 8 different tube ids; the first is tube i itself, the others lie inside the clip within one tube of i along each of time, height and width. `counts`: tubes in the last height row or the last width column may be partial; all other tubes are full.
All inputs are finite; a program needn't handle non-finite values.
Results may differ from the reference program's by a relative error of at most 0.015.
Values may be sent and summed in bfloat16 or wider, within the bound.
No kernel may reach another device: no remote copies, remote signals or barrier semaphores. Data moves between devices by JAX's collectives and lax.ppermute only.
A program may use at most 192 MiB of HBM per device.

```python
import jax
import jax.numpy as jnp
import numpy as np
from jax import lax

D = 1280
HEAD_DIM = 80
TUBE = 64
NB = 8
TW = 4
NT = 4
NH = 16
HW = 1280


def draw_w_qkv(key, part):
    first = jax.random.fold_in(key, 0)
    base = jax.random.normal(first, (D, 3, HW), jnp.float32) * D ** (-0.5)
    return base.astype(jnp.bfloat16)


def draw_neighbours(key, part):
    offsets = np.array([(a, b, c) for a in (-1, 0, 1) for b in (-1, 0, 1) for c in (-1, 0, 1) if (a, b, c) != (0, 0, 0)], np.int32)
    t_pos = jnp.arange(NT, dtype=jnp.int32)[:, None, None, None]
    h_pos = jnp.arange(NH, dtype=jnp.int32)[None, :, None, None]
    w_pos = jnp.arange(TW, dtype=jnp.int32)[None, None, :, None]
    t_near = t_pos + offsets[:, 0]
    h_near = h_pos + offsets[:, 1]
    w_near = w_pos + offsets[:, 2]
    inside = (t_near >= 0) & (t_near < NT) & (h_near >= 0) & (h_near < NH) & (w_near >= 0) & (w_near < TW)
    noise = jax.random.randint(key, (NT, NH, TW, 26), 0, 1024)
    score = noise * 32 + jnp.arange(26, dtype=jnp.int32) + inside.astype(jnp.int32) * 65536
    order = jnp.argsort(-score, axis=-1)[..., :NB - 1]
    ids_all = (t_near * NH + h_near) * TW + w_near
    chosen = jnp.take_along_axis(jnp.broadcast_to(ids_all, (NT, NH, TW, 26)), order, axis=-1)
    itself = jnp.broadcast_to((t_pos * NH + h_pos) * TW + w_pos, (NT, NH, TW, 1))
    return jnp.concatenate([itself, chosen], axis=-1).astype(jnp.int32)


def draw_counts(key, part):
    ragged = jax.random.randint(key, (NT, NH, TW), 1, TUBE + 1)
    h_pos = jnp.arange(NH, dtype=jnp.int32)[None, :, None]
    w_pos = jnp.arange(TW, dtype=jnp.int32)[None, None, :]
    edge = (h_pos == NH - 1) | (w_pos == TW - 1)
    return jnp.where(edge, ragged, TUBE).astype(jnp.int32)


def steps_of(key, dims, cuts, low, top_value):
    def one(position, parts):
        steps = jax.random.uniform(jax.random.fold_in(jax.random.fold_in(key, 6), position), (parts,), jnp.float32, low / len(cuts), top_value / len(cuts))
        return jnp.repeat(jnp.exp(steps), dims[position] // parts).reshape((-1,) + (1,) * (len(dims) - position - 1))

    level = one(*cuts[0])
    for cut in cuts[1:]:
        level = level * one(*cut)
    return level


def scatter_about(rng, extent, scale, reach, cuts=(), kind=jnp.bfloat16):
    level = steps_of(rng, extent, cuts, -0.22, 0.18) if cuts else 1.0
    drawn = jax.random.normal(rng, extent, jnp.float32) * scale * level
    return jnp.minimum(jnp.maximum(drawn, -reach), reach).astype(kind)


def setup_inputs(seed: int = 0) -> dict:
    key_list = jax.random.split(jax.random.key(seed), 8)
    video = scatter_about(key_list[0], (NT, NH, TW, TUBE, D), 1.0, 6.0, ((0, 4), (1, 16)))
    target = scatter_about(key_list[1], (NT, NH, TW, TUBE, D), 1.0, 6.0, ((0, 4), (1, 16)))
    gain = jnp.clip(1.0 + 0.15 * jax.random.normal(key_list[2], (D,), jnp.float32), 0.25, 1.75)
    w_qkv = draw_w_qkv(jax.random.fold_in(key_list[7], 71), 0)
    w_out = scatter_about(key_list[4], (HW, D), 0.15, 0.8984375, ((0, 2),))
    neighbours = draw_neighbours(jax.random.fold_in(key_list[7], 71), 0)
    counts = draw_counts(jax.random.fold_in(key_list[7], 71), 0)
    return {"video": video, "target": target, "gain": gain, "w_qkv": w_qkv, "w_out": w_out, "neighbours": neighbours, "counts": counts}


def reduced_precision(value):
    return lax.optimization_barrier(value.astype(jnp.bfloat16)).astype(jnp.float32)

def attention_probs(query, keys, near_live):
    scores = jnp.einsum('nqhe,nkhe->nhqk', query, keys, precision=lax.Precision.HIGHEST) * HEAD_DIM ** (-0.5)
    scores = jnp.where(near_live[:, None, None, :] > 0, scores, -1e+30)
    top = lax.optimization_barrier(jnp.max(scores, axis=-1, keepdims=True))
    expd = jnp.exp(scores - top)
    return expd / lax.optimization_barrier(jnp.sum(expd, axis=-1, keepdims=True))

def reference(video, target, gain, w_qkv, w_out, neighbours, counts):
    nt, nh, nw, tube, width = video.shape
    feats = w_qkv.shape[2]
    heads = feats // HEAD_DIM
    nblist = neighbours.shape[3]
    tubes = nt * nh * nw
    per_row = nh * nw
    xf = video.astype(jnp.float32)
    centred_input = xf - lax.optimization_barrier(jnp.mean(xf, axis=-1, keepdims=True))
    inverse_deviation = lax.rsqrt(lax.optimization_barrier(jnp.mean(centred_input * centred_input, axis=-1, keepdims=True)) + 1e-06)
    standardized_input = centred_input * inverse_deviation
    normalized_rows = reduced_precision(standardized_input * gain)
    wq = w_qkv.astype(jnp.float32)
    proj = reduced_precision(jnp.einsum('thwpd,dcj->thwpcj', normalized_rows, wq, precision=lax.Precision.HIGHEST))
    flat_proj = proj.reshape(tubes, tube, 3, feats)
    flat_kv = flat_proj[:, :, 1:, :]
    positions = lax.broadcasted_iota(jnp.int32, (nt, nh, nw, tube), 3)
    live = (positions < counts[..., None].astype(jnp.int32)).astype(jnp.float32).reshape(tubes, tube)
    ids = neighbours.reshape(tubes, nblist).astype(jnp.int32)
    x_rows = xf.reshape(tubes, tube, width)
    goal_rows = target.astype(jnp.float32).reshape(tubes, tube, width)
    w_o = w_out.astype(jnp.float32)

    def row_step(carry, row):
        start = (row * per_row).astype(jnp.int32)
        query = lax.dynamic_slice_in_dim(flat_proj, start, per_row, 0)[:, :, 0].reshape(per_row, tube, heads, HEAD_DIM)
        row_ids = lax.dynamic_slice_in_dim(ids, start, per_row, 0)
        near = flat_kv[row_ids]
        keys = near[:, :, :, 0].reshape(per_row, nblist * tube, heads, HEAD_DIM)
        values = near[:, :, :, 1].reshape(per_row, nblist * tube, heads, HEAD_DIM)
        near_live = live[row_ids].reshape(per_row, nblist * tube)
        probs = attention_probs(query, keys, near_live)
        probs_low = reduced_precision(probs)
        attended = reduced_precision(jnp.einsum('nhqk,nkhe->nqhe', probs_low, values, precision=lax.Precision.HIGHEST))
        mixed = jnp.dot(attended.reshape(per_row * tube, feats), w_o, precision=lax.Precision.HIGHEST)
        x_here = lax.dynamic_slice_in_dim(x_rows, start, per_row, 0).reshape(per_row * tube, width)
        goal_here = lax.dynamic_slice_in_dim(goal_rows, start, per_row, 0).reshape(per_row * tube, width)
        valid = lax.dynamic_slice_in_dim(live, start, per_row, 0).reshape(per_row * tube, 1)
        grad_feat = jnp.where(valid > 0, 2.0 * (x_here + mixed - goal_here), 0.0)
        grad_low = reduced_precision(grad_feat)
        d_att = reduced_precision(jnp.dot(grad_low, w_o.T, precision=lax.Precision.HIGHEST)).reshape(per_row, tube, heads, HEAD_DIM)
        d_prob = jnp.einsum('nqhe,nkhe->nhqk', d_att, values, precision=lax.Precision.HIGHEST)
        inner = lax.optimization_barrier(jnp.sum(d_prob * probs, axis=-1, keepdims=True))
        d_score = reduced_precision(probs * (d_prob - inner) * HEAD_DIM ** (-0.5))
        d_query = reduced_precision(jnp.einsum('nhqk,nkhe->nqhe', d_score, keys, precision=lax.Precision.HIGHEST))
        d_keys = jnp.einsum('nhqk,nqhe->nkhe', d_score, query, precision=lax.Precision.HIGHEST)
        d_values = jnp.einsum('nhqk,nqhe->nkhe', probs_low, d_att, precision=lax.Precision.HIGHEST)
        pieces = jnp.stack([d_keys.reshape(per_row, nblist, tube, feats), d_values.reshape(per_row, nblist, tube, feats)], axis=3)
        carry = carry.at[row_ids.reshape(-1)].add(pieces.reshape(per_row * nblist, tube, 2, feats))
        return (carry, (d_query.reshape(per_row, tube, feats), grad_feat))
    start_grad = jnp.zeros((tubes, tube, 2, feats), jnp.float32)
    kv_grad, (all_dq, all_grad) = lax.scan(row_step, start_grad, jnp.arange(nt, dtype=jnp.int32))
    kv_low = reduced_precision(kv_grad)
    d_proj = jnp.concatenate([all_dq.reshape(tubes, tube, 1, feats), kv_low], axis=2).reshape(nt, nh, nw, tube, 3, feats)
    d_normed = jnp.einsum('thwpcj,dcj->thwpd', d_proj, wq, precision=lax.Precision.HIGHEST)
    scaled_gradient = d_normed * gain
    correction_term = (scaled_gradient - lax.optimization_barrier(jnp.mean(scaled_gradient, axis=-1, keepdims=True)) - standardized_input * lax.optimization_barrier(jnp.mean(scaled_gradient * standardized_input, axis=-1, keepdims=True))) * inverse_deviation
    total = correction_term + all_grad.reshape(nt, nh, nw, tube, width)
    return total.astype(jnp.bfloat16)
```

```python
import functools
import math

import jax
import jax.numpy as jnp
from jax import lax
from jax.experimental import pallas as pl
from jax.experimental.pallas import tpu as pltpu
from jax.sharding import PartitionSpec as P

HEAD_DIM = 80
SCALE = HEAD_DIM ** (-0.5)
LOG2_SCALE = SCALE * math.log2(math.e)
BF16 = jnp.bfloat16
F32 = jnp.float32
MIB = 1 << 20
GROUPS = ((0, 3, 0, 256), (3, 2, 128, 384), (5, 3, 384, 256))
CHUNK = 4
STAT_ROWS = 32

NT_DIMS = (((1,), (1,)), ((), ()))


def dot(a, b):
    return jnp.dot(a, b, preferred_element_type=F32)


def dot_nt(a, b):
    return lax.dot_general(a, b, NT_DIMS, preferred_element_type=F32)


def head_mask(head, first_lane, rows, lanes):
    lane = lax.broadcasted_iota(jnp.int32, (rows, lanes), 1) + first_lane
    return (lane >= head * HEAD_DIM) & (lane < (head + 1) * HEAD_DIM)


def spread(x, group):
    h0, nh, l0, wd = group
    zero = jnp.zeros_like(x)
    return jnp.concatenate(
        [jnp.where(head_mask(h, l0, x.shape[0], wd), x, zero) for h in range(h0, h0 + nh)], axis=0
    )


def gather_heads(y, group, rows):
    h0, nh, l0, wd = group
    total = jnp.zeros((rows, wd), y.dtype)
    for k in range(nh):
        total = jnp.where(head_mask(h0 + k, l0, rows, wd), y[k * rows : (k + 1) * rows], total)
    return total


def add_group(ref, rows, value, group):
    h0, nh, l0, wd = group
    ref[rows, l0 : l0 + wd] = ref[rows, l0 : l0 + wd] + value


def project_body(n, aliased, *refs):
    xs = refs[:n]
    gain_ref, w_ref = refs[n : n + 2]
    out_ref, x_scr = refs[n + 2 + aliased :]
    step = pl.program_id(0)
    for k in range(n):

        @pl.when(step == k)
        def _():
            x_scr[...] = xs[k][...]

    x = x_scr[...].astype(F32)
    centred = x - jnp.mean(x, axis=-1, keepdims=True)
    inverse = lax.rsqrt(jnp.mean(centred * centred, axis=-1, keepdims=True) + 1e-06)
    normed = (centred * inverse * gain_ref[...]).astype(BF16)
    feats = w_ref.shape[1] // 3
    for c in range(3):
        cols = slice(c * feats, (c + 1) * feats)
        out_ref[0, :, cols] = dot(normed, w_ref[:, cols]).astype(BF16)


def project(blocks, first, gain, w, buf=None):
    n = len(blocks)
    rows, width = blocks[0].shape
    cols = w.shape[1]
    aliased = int(buf is not None)
    whole = lambda a: pl.BlockSpec(a.shape, lambda i: (0,) * a.ndim)
    return pl.pallas_call(
        functools.partial(project_body, n, aliased),
        grid=(n,),
        in_specs=[whole(b) for b in blocks]
        + [whole(gain), whole(w)]
        + [pl.BlockSpec(memory_space=pl.ANY)] * aliased,
        out_specs=pl.BlockSpec((1, rows, cols), lambda i: (i + first, 0, 0)),
        out_shape=jax.ShapeDtypeStruct((9, rows, cols), BF16),
        scratch_shapes=[pltpu.VMEM((rows, width), BF16)],
        input_output_aliases={n + 2: 0} if aliased else {},
        compiler_params=pltpu.CompilerParams(vmem_limit_bytes=32 * MIB),
        cost_estimate=pl.CostEstimate(
            flops=2 * n * rows * width * cols, bytes_accessed=2 * width * cols + 4 * n * rows * width, transcendentals=0
        ),
        name=f"project{first}",
    )(*blocks, gain, w, *([buf] if aliased else []))


def start_kv(local_ref, qkv_ref, kv_scr, sem, tubes, nb):
    feats = kv_scr.shape[2] // 2

    @pl.when(pl.program_id(0) == 0)
    def _():
        for i in range(tubes):
            for n in range(nb):
                pltpu.make_async_copy(
                    qkv_ref.at[local_ref[i * nb + n], :, feats:],
                    kv_scr.at[i, n * 64 : (n + 1) * 64, :],
                    sem.at[i],
                ).start()


def wait_kv(kv_scr, sem, i):
    pltpu.make_async_copy(kv_scr.at[i], kv_scr.at[i], sem.at[i]).wait()


def forward_body(local_ref, count_ref, qkv_ref, q_ref, w_out_ref, part_ref, o_ref, p_ref, lse_ref, kv_scr, att_scr, sem):
    tubes, keys, feats2 = kv_scr.shape
    feats = feats2 // 2
    nb = keys // 64
    i = pl.program_id(0)
    start_kv(local_ref, qkv_ref, kv_scr, sem, tubes, nb)
    lane = lax.broadcasted_iota(jnp.int32, (1, keys), 1)
    slot, place = lane // 64, lane % 64
    limit = jnp.zeros((1, keys), jnp.int32)
    for n in range(nb):
        limit = jnp.where(slot == n, count_ref[local_ref[i * nb + n]], limit)
    live = place < limit
    wait_kv(kv_scr, sem, i)
    o_ref[...] = jnp.zeros_like(o_ref)
    pick = lax.broadcasted_iota(jnp.int32, (64, 128), 0) == lax.broadcasted_iota(jnp.int32, (64, 128), 1) % 64
    for group in GROUPS:
        h0, nh, l0, wd = group
        window = slice(l0, l0 + wd)
        q = spread(q_ref[:, window], group)
        s = dot_nt(q, kv_scr[i, :, window]) * LOG2_SCALE
        s = jnp.where(live, s, -1e30)
        top = jnp.max(s, axis=-1, keepdims=True)
        e = jnp.exp2(s - top)
        total = jnp.sum(e, axis=-1, keepdims=True)
        p = (e * (1.0 / total)).astype(BF16)
        p_ref[0, h0 * 64 : (h0 + nh) * 64, :] = p
        o = dot(p, kv_scr[i, :, feats + l0 : feats + l0 + wd])
        add_group(o_ref, slice(None), gather_heads(o, group, 64), group)
        lse = top + jnp.log2(total)
        for k in range(nh):
            column = jnp.broadcast_to(lse[k * 64 : (k + 1) * 64], (64, 128))
            lse_ref[0, h0 + k : h0 + k + 1, :] = jnp.sum(jnp.where(pick, column, 0.0), axis=0, keepdims=True)
    att_scr[pl.ds(i * 64, 64), :] = o_ref[...].astype(BF16)

    @pl.when(i == tubes - 1)
    def _():
        part_ref[...] = dot(att_scr[...], w_out_ref[...]).astype(BF16)


def attend_forward(local, counts, qkv, w_out):
    slots, _, cols = qkv.shape
    feats = cols // 3
    tubes, nb = 4, local.shape[0] // 4
    keys = nb * 64
    rows = tubes * 64
    heads = feats // HEAD_DIM
    width = w_out.shape[1]
    return pl.pallas_call(
        forward_body,
        grid_spec=pltpu.PrefetchScalarGridSpec(
            num_scalar_prefetch=2,
            grid=(tubes,),
            in_specs=[
                pl.BlockSpec(memory_space=pl.ANY),
                pl.BlockSpec((pl.squeezed, 64, feats), lambda i, *_: (i, 0, 0)),
                pl.BlockSpec((feats, width), lambda i, *_: (0, 0)),
            ],
            out_specs=[
                pl.BlockSpec((rows, width), lambda i, *_: (0, 0)),
                pl.BlockSpec((64, feats), lambda i, *_: (i, 0)),
                pl.BlockSpec((1, heads * 64, keys), lambda i, *_: (i, 0, 0)),
                pl.BlockSpec((1, heads, 128), lambda i, *_: (i, 0, 0)),
            ],
            scratch_shapes=[
                pltpu.VMEM((tubes, keys, 2 * feats), BF16),
                pltpu.VMEM((rows, feats), BF16),
                pltpu.SemaphoreType.DMA((tubes,)),
            ],
        ),
        out_shape=[
            jax.ShapeDtypeStruct((rows, width), BF16),
            jax.ShapeDtypeStruct((rows, feats), F32),
            jax.ShapeDtypeStruct((tubes, heads * 64, keys), BF16),
            jax.ShapeDtypeStruct((tubes, heads, 128), F32),
        ],
        compiler_params=pltpu.CompilerParams(vmem_limit_bytes=32 * MIB),
        cost_estimate=pl.CostEstimate(
            flops=4 * rows * heads * keys * 256, bytes_accessed=10 * MIB, transcendentals=rows * heads * keys
        ),
        name="attend_forward",
    )(local, counts, qkv, qkv, w_out)


def parts_of(x, n):
    out = []
    for _ in range(n):
        piece = x.astype(BF16)
        out.append(piece)
        x = x - piece.astype(F32)
    return out


def middle_body(count_ref, sec_ref, mine_ref, other_ref, video_ref, target_ref, w_out_ref, o_ref, lse_ref, pay_ref, g_ref):
    rows, width = video_ref.shape
    feats = w_out_ref.shape[0]
    heads = feats // HEAD_DIM
    tubes = rows // 64
    row = lax.broadcasted_iota(jnp.int32, (rows, 1), 0)
    limit = jnp.zeros((rows, 1), jnp.int32)
    for i in range(tubes):
        limit = jnp.where(row // 64 == i, count_ref[i], limit)
    valid = row % 64 < limit
    mixed = mine_ref[...].astype(F32) + other_ref[...].astype(F32)
    g = jnp.where(valid, 2.0 * (video_ref[...].astype(F32) + mixed - target_ref[...].astype(F32)), 0.0)
    half = width // 2
    g_ref[...] = jnp.where(sec_ref[0] == 0, g[:, :half], g[:, half:])
    d_att = dot_nt(g.astype(BF16), w_out_ref[...]).astype(BF16)
    pay_ref[:rows] = d_att
    prod = d_att.astype(F32) * o_ref[...]
    head = lax.broadcasted_iota(jnp.int32, (heads, feats), 0)
    lane = lax.broadcasted_iota(jnp.int32, (heads, feats), 1)
    ones = ((lane >= head * HEAD_DIM) & (lane < (head + 1) * HEAD_DIM)).astype(F32)
    inner = []
    for i in range(tubes):
        one = prod[i * 64 : (i + 1) * 64]
        inner.append(
            lax.dot_general(
                ones,
                jnp.concatenate([one, one], axis=0),
                NT_DIMS,
                precision=lax.Precision.HIGHEST,
                preferred_element_type=F32,
            )
        )
    inner = jnp.concatenate(inner, axis=0)
    lse = lse_ref[...].reshape(tubes * heads, 128)
    for k, piece in enumerate(parts_of(lse, 3) + parts_of(inner, 2)):
        pay_ref[rows:, k * 128 : (k + 1) * 128] = piece


def middle(counts, sec, mine, other, video, target, w_out, o, lse):
    rows, width = video.shape
    feats = w_out.shape[0]
    vmem = pl.BlockSpec(memory_space=pltpu.VMEM)
    smem = pl.BlockSpec(memory_space=pltpu.SMEM)
    return pl.pallas_call(
        middle_body,
        in_specs=[smem, smem] + [vmem] * 7,
        out_specs=[vmem, vmem],
        out_shape=[
            jax.ShapeDtypeStruct((rows + STAT_ROWS, feats), BF16),
            jax.ShapeDtypeStruct((rows, width // 2), F32),
        ],
        compiler_params=pltpu.CompilerParams(vmem_limit_bytes=32 * MIB),
        cost_estimate=pl.CostEstimate(flops=2 * rows * width * feats, bytes_accessed=6 * MIB, transcendentals=0),
        name="middle",
    )(counts, sec, mine, other, video, target, w_out, o, lse)


def query_body(local_ref, qkv_ref, p_ref, pay_ref, dq_ref, kv_scr, dq_scr, sem):
    tubes, keys, feats2 = kv_scr.shape
    feats = feats2 // 2
    i = pl.program_id(0)
    start_kv(local_ref, qkv_ref, kv_scr, sem, tubes, keys // 64)
    wait_kv(kv_scr, sem, i)
    dq_scr[...] = jnp.zeros_like(dq_scr)
    for group in GROUPS:
        h0, nh, l0, wd = group
        window = slice(l0, l0 + wd)
        d_att = spread(pay_ref[pl.ds(i * 64, 64), window], group)
        d_prob = dot_nt(d_att, kv_scr[i, :, feats + l0 : feats + l0 + wd])
        p = p_ref[0, h0 * 64 : (h0 + nh) * 64, :].astype(F32)
        inner = jnp.sum(d_prob * p, axis=-1, keepdims=True)
        d_score = (p * (d_prob - inner) * SCALE).astype(BF16)
        add_group(dq_scr, slice(None), gather_heads(dot(d_score, kv_scr[i, :, window]), group, 64), group)
    dq_ref[...] = dq_scr[...].astype(BF16)


def query_grad(local, qkv, p, pay):
    cols = qkv.shape[2]
    feats = cols // 3
    tubes, rows_h, keys = p.shape
    return pl.pallas_call(
        query_body,
        grid_spec=pltpu.PrefetchScalarGridSpec(
            num_scalar_prefetch=1,
            grid=(tubes,),
            in_specs=[
                pl.BlockSpec(memory_space=pl.ANY),
                pl.BlockSpec((1, rows_h, keys), lambda i, *_: (i, 0, 0)),
                pl.BlockSpec(pay.shape, lambda i, *_: (0, 0)),
            ],
            out_specs=pl.BlockSpec((64, feats), lambda i, *_: (i, 0)),
            scratch_shapes=[
                pltpu.VMEM((tubes, keys, 2 * feats), BF16),
                pltpu.VMEM((64, feats), F32),
                pltpu.SemaphoreType.DMA((tubes,)),
            ],
        ),
        out_shape=jax.ShapeDtypeStruct((tubes * 64, feats), BF16),
        compiler_params=pltpu.CompilerParams(vmem_limit_bytes=32 * MIB),
        cost_estimate=pl.CostEstimate(flops=4 * tubes * rows_h * keys * 256, bytes_accessed=10 * MIB, transcendentals=0),
        name="query_grad",
    )(local, qkv, p, pay)


def key_body(
    list_ref, n_ref, count_ref, sec_ref, qkv_ref, w_ref, *rest
):
    pays = rest[:9]
    video_ref, gain_ref, dq_ref, g_ref, send_ref, keep_ref = rest[9:15]
    q_scr, kv_scr, pay_scr, w_scr, lse_scr, inner_scr, qc_scr, dc_scr, grad_scr, dproj_scr, sem = rest[15:]
    tubes = kv_scr.shape[0]
    feats = q_scr.shape[2]
    rows = tubes * 64
    most = list_ref.shape[0] // tubes
    w_copy = pltpu.make_async_copy(w_ref, w_scr, sem.at[0])
    q_copy = pltpu.make_async_copy(qkv_ref.at[:, :, :feats], q_scr, sem.at[1])
    kv_copy = pltpu.make_async_copy(qkv_ref.at[:tubes, :, feats:], kv_scr, sem.at[2])
    pay_copies = [pltpu.make_async_copy(pays[k], pay_scr.at[k], sem.at[3 + k]) for k in range(9)]
    for c in pay_copies + [q_copy, kv_copy, w_copy]:
        c.start()
    for k, c in enumerate(pay_copies):
        c.wait()
        parts = [pay_scr[k, rows:, j * 128 : (j + 1) * 128].astype(F32) for j in range(5)]
        lse_scr[k * tubes : (k + 1) * tubes] = (parts[0] + parts[1] + parts[2]).reshape(tubes, -1, 128)
        inner_scr[k * tubes : (k + 1) * tubes] = (parts[3] + parts[4]).reshape(tubes, -1, 128)
    q_copy.wait()
    kv_copy.wait()
    low = lax.broadcasted_iota(jnp.int32, (8, 128), 1) < 64
    key_row = lax.broadcasted_iota(jnp.int32, (64, 1), 0)
    grad_scr[...] = jnp.zeros_like(grad_scr)

    def tube(j, carry):
        alive = key_row < count_ref[j]

        def chunk(c, carry):
            lses, inners = [], []
            for t in range(CHUNK):
                place = c * CHUNK + t
                i = list_ref[j * most + jnp.minimum(place, most - 1)]
                slot, w = i // tubes, i % tubes
                qc_scr[t * 64 : (t + 1) * 64, :] = q_scr[i]
                dc_scr[t * 64 : (t + 1) * 64, :] = pay_scr[slot, pl.ds(pl.multiple_of(w * 64, 64), 64), :]
                lses.append(jnp.where(place < n_ref[j], lse_scr[i], 1e30))
                inners.append(inner_scr[i])
            lse = jnp.concatenate([jnp.where(low, lses[t], lses[t + 1]) for t in range(0, CHUNK, 2)], axis=1)
            inner = jnp.concatenate([jnp.where(low, inners[t], inners[t + 1]) for t in range(0, CHUNK, 2)], axis=1)
            for group in GROUPS:
                h0, nh, l0, wd = group
                window = slice(l0, l0 + wd)
                k = spread(kv_scr[j, :, window], group)
                v = spread(kv_scr[j, :, feats + l0 : feats + l0 + wd], group)
                qc, dc = qc_scr[:, window], dc_scr[:, window]
                s = dot_nt(k, qc) * LOG2_SCALE
                d_prob = dot_nt(v, dc)
                p, d_score = [], []
                for m in range(nh):
                    part = slice(m * 64, (m + 1) * 64)
                    head = slice(h0 + m, h0 + m + 1)
                    one = jnp.where(alive, jnp.exp2(s[part] - lse[head]), 0.0)
                    p.append(one.astype(BF16))
                    d_score.append((one * (d_prob[part] - inner[head]) * SCALE).astype(BF16))
                d_key = dot(jnp.concatenate(d_score, axis=0), qc)
                d_value = dot(jnp.concatenate(p, axis=0), dc)
                block = pl.ds(pl.multiple_of(j * 64, 64), 64)
                grad_scr[block, window] += gather_heads(d_key, group, 64)
                there = slice(feats + l0, feats + l0 + wd)
                grad_scr[block, there] += gather_heads(d_value, group, 64)
            return carry

        return lax.fori_loop(0, (n_ref[j] + CHUNK - 1) // CHUNK, chunk, carry)

    lax.fori_loop(0, tubes, tube, 0)
    dproj_scr[:, :feats] = dq_ref[...]
    dproj_scr[:, feats:] = grad_scr[...].astype(BF16)
    w_copy.wait()
    x = video_ref[...].astype(F32)
    centred = x - jnp.mean(x, axis=-1, keepdims=True)
    inverse = lax.rsqrt(jnp.mean(centred * centred, axis=-1, keepdims=True) + 1e-06)
    xhat = centred * inverse
    scaled = dot_nt(dproj_scr[...], w_scr[...]) * gain_ref[...]
    out = (
        scaled
        - jnp.mean(scaled, axis=-1, keepdims=True)
        - xhat * jnp.mean(scaled * xhat, axis=-1, keepdims=True)
    ) * inverse
    half = out.shape[1] // 2
    first = sec_ref[0] == 0
    send_ref[...] = jnp.where(first, out[:, half:], out[:, :half]).astype(BF16)
    keep_ref[...] = jnp.where(first, out[:, :half], out[:, half:]) + g_ref[...]


def key_grad(lists, lengths, counts, sec, qkv, w, pays, video, gain, dq, g):
    cols = qkv.shape[2]
    feats = cols // 3
    rows, width = video.shape
    tubes = rows // 64
    heads = feats // HEAD_DIM
    vmem = pl.BlockSpec(memory_space=pltpu.VMEM)
    smem = pl.BlockSpec(memory_space=pltpu.SMEM)
    hbm = pl.BlockSpec(memory_space=pl.ANY)
    return pl.pallas_call(
        key_body,
        in_specs=[smem] * 4 + [hbm] * 11 + [vmem] * 4,
        out_specs=[vmem, vmem],
        out_shape=[
            jax.ShapeDtypeStruct((rows, width // 2), BF16),
            jax.ShapeDtypeStruct((rows, width // 2), F32),
        ],
        scratch_shapes=[
            pltpu.VMEM((9 * tubes, 64, feats), BF16),
            pltpu.VMEM((tubes, 64, 2 * feats), BF16),
            pltpu.VMEM((9, rows + STAT_ROWS, feats), BF16),
            pltpu.VMEM(w.shape, BF16),
            pltpu.VMEM((9 * tubes, heads, 128), F32),
            pltpu.VMEM((9 * tubes, heads, 128), F32),
            pltpu.VMEM((CHUNK * 64, feats), BF16),
            pltpu.VMEM((CHUNK * 64, feats), BF16),
            pltpu.VMEM((rows, 2 * feats), F32),
            pltpu.VMEM((rows, 3 * feats), BF16),
            pltpu.SemaphoreType.DMA((12,)),
        ],
        compiler_params=pltpu.CompilerParams(vmem_limit_bytes=40 * MIB),
        cost_estimate=pl.CostEstimate(flops=12 * 10**9, bytes_accessed=16 * MIB, transcendentals=10**6),
        name="key_grad",
    )(lists, lengths, counts, sec, qkv, w, *pays, video, gain, dq, g)


def per_device(video, target, gain, w_qkv, w_out, neighbours, counts):
    tt, th, tw, tube, width = video.shape
    feats = w_qkv.shape[2]
    nb = neighbours.shape[3]
    rows = tt * th * tw * tube
    n_t, n_h = lax.axis_size("tm"), lax.axis_size("height")
    t_here, h_here, sec = lax.axis_index("tm"), lax.axis_index("height"), lax.axis_index("section")
    later = [(i, i + 1) for i in range(n_t - 1)]
    earlier = [(i + 1, i) for i in range(n_t - 1)]
    off_chip = [p for h in range(1, n_h - 1, 2) for p in ((h, h + 1), (h + 1, h))]
    on_chip = [(h, h ^ 1) for h in range(n_h)]
    swap = [(0, 1), (1, 0)]

    def from_before(x):
        return lax.ppermute(x, "tm", later)

    def from_after(x):
        return lax.ppermute(x, "tm", earlier)

    def from_off(x):
        return lax.ppermute(x, "height", off_chip)

    def from_mate(x):
        return lax.ppermute(x, "height", on_chip)

    def halo(x):
        off = from_off(x)
        before, after = from_before(x), from_after(x)
        return (x, before, after, off), (from_mate(x), from_mate(before), from_mate(after)), (from_before(off), from_after(off))

    video = video.reshape(rows, width)
    target = target.reshape(rows, width)
    gain = gain.reshape(1, width)
    w = w_qkv.reshape(width, 3 * feats)

    near, mates, corners = halo(video)
    qkv = project([near[0]], 0, gain, w)
    qkv = project([*near[1:], mates[0]], 1, gain, w, qkv)
    qkv = project([*mates[1:], *corners], 5, gain, w, qkv)
    qkv = qkv.reshape(9 * tw, tube, 3 * feats)

    meta = jnp.concatenate(
        [neighbours.reshape(tw, nb) + 1, counts.reshape(tw, 1), jnp.zeros((tw, 16 - nb - 1), jnp.int32)], axis=1
    )
    three = jnp.stack([meta, from_before(meta), from_after(meta)])
    off_meta, mate_meta = from_off(three), from_mate(three)
    meta = jnp.concatenate([three, off_meta[:1], mate_meta, off_meta[1:]]).reshape(9 * tw, 16)
    listed = meta[:, :nb] - 1
    count_all = meta[:, nb]

    ids = listed[:tw]
    t_of, h_of, w_of = ids // (n_h * tw), ids // tw % n_h, ids % tw
    step = jnp.where(t_of == t_here, 0, jnp.where(t_of < t_here, 1, 2))
    slot = jnp.where(
        h_of == h_here, step, jnp.where(h_of == h_here + 1 - 2 * (h_here % 2), 4 + step, jnp.where(step == 0, 3, 6 + step))
    )
    local = (slot * tw + w_of).reshape(tw * nb)
    own_ids = (t_here * n_h + h_here) * tw + jnp.arange(tw, dtype=jnp.int32)
    names = jnp.any(listed[None] == own_ids[:, None, None], axis=2)
    where = jnp.arange(9 * tw, dtype=jnp.int32)
    rank = jnp.sum(names[:, None, :] & (where[None, :] < where[:, None])[None], axis=2)
    lengths = jnp.sum(names, axis=1).astype(jnp.int32)
    most = 28
    hit = names[:, None, :] & (rank[:, None, :] == jnp.arange(most)[None, :, None])
    lists = jnp.sum(jnp.where(hit, where, 0), axis=2).astype(jnp.int32).reshape(tw * most)
    sec = sec.reshape(1).astype(jnp.int32)
    own_counts = count_all[:tw]

    part, o, p, lse = attend_forward(local, count_all, qkv, w_out)
    other = lax.ppermute(part, "section", swap)
    pay, g = middle(own_counts, sec, part, other, video, target, w_out, o, lse)
    near, mates, corners = halo(pay)
    dq = query_grad(local, qkv, p, pay)
    send, keep = key_grad(lists, lengths, own_counts, sec, qkv, w, [*near, *mates, *corners], video, gain, dq, g)
    got = lax.ppermute(send, "section", swap)
    return (keep + got.astype(F32)).astype(BF16).reshape(tt, th, tw, tube, width // 2)


def solution(mesh):
    in_specs = (
        P("tm", "height", None, None, None),
        P("tm", "height", None, None, None),
        P(),
        P(None, None, "section"),
        P("section", None),
        P("tm", "height", None, None),
        P("tm", "height", None),
    )
    out_specs = P("tm", "height", None, None, "section")
    return jax.shard_map(
        per_device, mesh=mesh, in_specs=in_specs, out_specs=out_specs, check_vma=False
    )
```

```python
import functools
import math

import jax
import jax.numpy as jnp
from jax import lax
from jax.experimental import pallas as pl
from jax.experimental.pallas import tpu as pltpu
from jax.sharding import PartitionSpec as P

HEAD_DIM = 80
SCALE = HEAD_DIM ** (-0.5)
LOG2_SCALE = SCALE * math.log2(math.e)
BF16 = jnp.bfloat16
F32 = jnp.float32
MIB = 1 << 20
GROUPS = ((0, 3, 0, 256), (3, 2, 128, 384), (5, 3, 384, 256))
NEAR_CHUNK, LAST_CHUNK = 8, 2
STAT_ROWS = 32
BLOCKS = 12
SMALL = pl.CostEstimate(flops=1, bytes_accessed=1, transcendentals=0)
VMEM_LIMIT = 60 * MIB

NT_DIMS = (((1,), (1,)), ((), ()))


def dot(a, b):
    return jnp.dot(a, b, preferred_element_type=F32)


def dot_nt(a, b):
    return lax.dot_general(a, b, NT_DIMS, preferred_element_type=F32)


def head_row(head, first_lane, lanes):
    lane = lax.broadcasted_iota(jnp.int32, (1, lanes), 1) + first_lane
    return jnp.where((lane >= head * HEAD_DIM) & (lane < (head + 1) * HEAD_DIM), 1.0, 0.0).astype(F32)


def spread(x, group):
    h0, nh, l0, wd = group
    out = []
    for h in range(h0, h0 + nh):
        mask = jnp.broadcast_to(head_row(h, l0, wd), (16, wd)).astype(BF16)
        out += [x[r : r + 16] * mask for r in range(0, x.shape[0], 16)]
    return jnp.concatenate(out, axis=0)


def gather_heads(y, group, rows):
    h0, nh, l0, wd = group
    total = y[:rows] * head_row(h0, l0, wd)
    for k in range(1, nh):
        total = total + y[k * rows : (k + 1) * rows] * head_row(h0 + k, l0, wd)
    return total


def add_group(ref, rows, value, group):
    h0, nh, l0, wd = group
    ref[rows, l0 : l0 + wd] = ref[rows, l0 : l0 + wd] + value


def normalize(x):
    centred = x - jnp.mean(x, axis=-1, keepdims=True)
    inverse = lax.rsqrt(jnp.mean(centred * centred, axis=-1, keepdims=True) + 1e-06)
    return centred * inverse, inverse


def project_near_body(n, *refs):
    xs = refs[:n]
    gain_ref, w_ref = refs[n : n + 2]
    kv_ref, q_ref, x_scr = refs[n + 3 :]
    rows = xs[0].shape[0]
    step = pl.program_id(0)

    @pl.when(step == 0)
    def _():
        for k in range(n):
            x_scr[k * rows : (k + 1) * rows] = (normalize(xs[k][...].astype(F32))[0] * gain_ref[...]).astype(BF16)

    @pl.when(step > 0)
    def _():
        kv_ref[...] = dot(x_scr[...], w_ref[...]).astype(BF16).reshape(q_ref.shape)

    @pl.when(step == 0)
    def _():
        q_ref[...] = dot(x_scr[...], w_ref[...]).astype(BF16).reshape(q_ref.shape)


def whole(a):
    return pl.BlockSpec(a.shape, lambda i: (0,) * a.ndim)


def project_near(blocks, first, gain, w, buf):
    n = len(blocks)
    rows, width = blocks[0].shape
    feats = w.shape[2]
    return pl.pallas_call(
        functools.partial(project_near_body, n),
        grid=(3,),
        in_specs=[whole(b) for b in blocks]
        + [whole(gain), pl.BlockSpec((pl.squeezed, width, feats), lambda i: (i, 0, 0))]
        + [pl.BlockSpec(memory_space=pl.ANY)],
        out_specs=[
            pl.BlockSpec((n, rows, feats), lambda i: (first // n, 0, jnp.maximum(i - 1, 0))),
            pl.BlockSpec((n, rows, feats), lambda i: (0, 0, 0)),
        ],
        out_shape=[jax.ShapeDtypeStruct(buf.shape, BF16), jax.ShapeDtypeStruct((n, rows, feats), BF16)],
        scratch_shapes=[pltpu.VMEM((n * rows, width), BF16)],
        input_output_aliases={n + 2: 0},
        compiler_params=pltpu.CompilerParams(vmem_limit_bytes=VMEM_LIMIT),
        cost_estimate=SMALL,
        name="project_near",
    )(*blocks, gain, w, buf)


def project_own_body(x_ref, gain_ref, w_ref, kv_ref, q_ref, x_scr):
    step = pl.program_id(0)

    @pl.when(step == 0)
    def _():
        x_scr[...] = (normalize(x_ref[...].astype(F32))[0] * gain_ref[...]).astype(BF16)

    @pl.when(step < 2)
    def _():
        kv_ref[0] = dot(x_scr[...], w_ref[...]).astype(BF16)

    @pl.when(step == 2)
    def _():
        q_ref[...] = dot(x_scr[...], w_ref[...]).astype(BF16)


def project_own(x, gain, w):
    rows, width = x.shape
    feats = w.shape[2]
    return pl.pallas_call(
        project_own_body,
        grid=(3,),
        in_specs=[whole(x), whole(gain), pl.BlockSpec((pl.squeezed, width, feats), lambda i: ((i + 1) % 3, 0, 0))],
        out_specs=[
            pl.BlockSpec((1, rows, feats), lambda i: (0, 0, jnp.minimum(i, 1))),
            pl.BlockSpec((rows, feats), lambda i: (0, 0)),
        ],
        out_shape=[
            jax.ShapeDtypeStruct((BLOCKS, rows, 2 * feats), BF16),
            jax.ShapeDtypeStruct((rows, feats), BF16),
        ],
        scratch_shapes=[pltpu.VMEM((rows, width), BF16)],
        compiler_params=pltpu.CompilerParams(vmem_limit_bytes=VMEM_LIMIT),
        cost_estimate=SMALL,
        name="project_own",
    )(x, gain, w)


def project_queries_body(n, *refs):
    xs = refs[:n]
    gain_ref, w_ref, out_ref, x_scr = refs[n:]
    step = pl.program_id(0)
    for k in range(n):

        @pl.when(step == k)
        def _():
            x_scr[...] = xs[k][...]

    normed = (normalize(x_scr[...].astype(F32))[0] * gain_ref[...]).astype(BF16)
    out_ref[0] = dot(normed, w_ref[...]).astype(BF16)


def project_queries(blocks, gain, w):
    n = len(blocks)
    rows, width = blocks[0].shape
    feats = w.shape[2]
    return pl.pallas_call(
        functools.partial(project_queries_body, n),
        grid=(n,),
        in_specs=[whole(b) for b in blocks] + [whole(gain), pl.BlockSpec((pl.squeezed, width, feats), lambda i: (0, 0, 0))],
        out_specs=pl.BlockSpec((1, rows, feats), lambda i: (i, 0, 0)),
        out_shape=jax.ShapeDtypeStruct((n, rows, feats), BF16),
        scratch_shapes=[pltpu.VMEM((rows, width), BF16)],
        compiler_params=pltpu.CompilerParams(vmem_limit_bytes=VMEM_LIMIT),
        cost_estimate=SMALL,
        name="project_queries",
    )(*blocks, gain, w)


def lay_out_keys(local_ref, all_scr, kv_scr, i):
    nb = kv_scr.shape[1] // 64
    for n in range(nb):
        kv_scr[i, n * 64 : (n + 1) * 64, :] = all_scr[local_ref[i * nb + n]]


def forward_body(
    local_ref, count_ref, x0_ref, x1_ref, gain_ref, w_ref, kv_ref, q_ref, w_out_ref,
    part_ref, o_ref, lse_ref, p_ref, far_ref,
    x_scr, n_scr, w_scr, wo_scr, q_scr, all_scr, kv_scr, p_scr, sem, p_sem,
):
    tubes, keys, feats2 = kv_scr.shape
    feats = feats2 // 2
    nb = keys // 64
    rows = tubes * 64
    copies = [
        pltpu.make_async_copy(x0_ref, x_scr.at[:rows], sem.at[0]),
        pltpu.make_async_copy(x1_ref, x_scr.at[rows:], sem.at[1]),
        pltpu.make_async_copy(w_ref.at[1], w_scr.at[0], sem.at[2]),
        pltpu.make_async_copy(w_ref.at[2], w_scr.at[1], sem.at[3]),
        pltpu.make_async_copy(q_ref, q_scr, sem.at[4]),
        pltpu.make_async_copy(w_out_ref, wo_scr, sem.at[5]),
        pltpu.make_async_copy(kv_ref.at[:tubes], all_scr.at[:tubes], sem.at[6]),
        pltpu.make_async_copy(kv_ref.at[6 * tubes :], all_scr.at[tubes : 7 * tubes], sem.at[7]),
    ]
    for k in (0, 1, 2, 3, 6, 7, 4, 5):
        copies[k].start()
    for k in range(2):
        copies[k].wait()
        half = slice(k * rows, (k + 1) * rows)
        n_scr[half] = (normalize(x_scr[half].astype(F32))[0] * gain_ref[...]).astype(BF16)
    for k in range(2):
        copies[2 + k].wait()
        out = dot(n_scr[...], w_scr[k]).astype(BF16).reshape(2 * tubes, 64, feats)
        all_scr[7 * tubes :, :, k * feats : (k + 1) * feats] = out
    far_copy = pltpu.make_async_copy(all_scr.at[7 * tubes :], far_ref, sem.at[8])
    far_copy.start()
    for k in (6, 7, 4):
        copies[k].wait()
    lane = lax.broadcasted_iota(jnp.int32, (1, keys), 1)
    slot, place = lane // 64, lane % 64
    pick = lax.broadcasted_iota(jnp.int32, (64, 128), 0) == lax.broadcasted_iota(jnp.int32, (64, 128), 1) % 64
    o_ref[...] = jnp.zeros_like(o_ref)

    def tube(i):
        limit = jnp.zeros((1, keys), jnp.int32)
        for n in range(nb):
            limit = jnp.where(slot == n, count_ref[local_ref[i * nb + n]], limit)
        live = place < limit
        here = slice(i * 64, (i + 1) * 64)
        lay_out_keys(local_ref, all_scr, kv_scr, i)
        for group in GROUPS:
            h0, nh, l0, wd = group
            window = slice(l0, l0 + wd)
            q = spread(q_scr[here, window], group)
            s = dot_nt(q, kv_scr[i, :, window]) * LOG2_SCALE
            s = jnp.where(live, s, -1e30)
            top = jnp.max(s, axis=-1, keepdims=True)
            e = jnp.exp2(s - top)
            total = jnp.sum(e, axis=-1, keepdims=True)
            p = (e * (1.0 / total)).astype(BF16)
            p_scr[i, h0 * 64 : (h0 + nh) * 64, :] = p
            o = dot(p, kv_scr[i, :, feats + l0 : feats + l0 + wd])
            o_ref[here, window] += gather_heads(o, group, 64)
            lse = top + jnp.log2(total)
            for k in range(nh):
                column = jnp.broadcast_to(lse[k * 64 : (k + 1) * 64], (64, 128))
                lse_ref[i, h0 + k : h0 + k + 1, :] = jnp.sum(jnp.where(pick, column, 0.0), axis=0, keepdims=True)
        pltpu.make_async_copy(p_scr.at[i], p_ref.at[i], p_sem.at[i]).start()

    for i in range(tubes):
        tube(i)
    copies[5].wait()
    part_ref[...] = dot(o_ref[...].astype(BF16), wo_scr[...]).astype(BF16)
    far_copy.wait()
    for i in range(tubes):
        pltpu.make_async_copy(p_scr.at[i], p_ref.at[i], p_sem.at[i]).wait()


def attend_forward(local, counts, x0, x1, gain, w, kv, q, w_out):
    rows, feats = q.shape
    tubes = rows // 64
    nb = local.shape[0] // tubes
    keys = nb * 64
    heads = feats // HEAD_DIM
    width = w_out.shape[1]
    vmem = pl.BlockSpec(memory_space=pltpu.VMEM)
    smem = pl.BlockSpec(memory_space=pltpu.SMEM)
    hbm = pl.BlockSpec(memory_space=pl.ANY)
    return pl.pallas_call(
        forward_body,
        in_specs=[smem, smem, hbm, hbm, vmem, hbm, hbm, hbm, hbm],
        out_specs=[vmem, vmem, vmem, hbm, hbm],
        out_shape=[
            jax.ShapeDtypeStruct((rows, width), BF16),
            jax.ShapeDtypeStruct((rows, feats), F32),
            jax.ShapeDtypeStruct((tubes, heads, 128), F32),
            jax.ShapeDtypeStruct((tubes, heads * 64, keys), BF16),
            jax.ShapeDtypeStruct((2 * tubes, 64, 2 * feats), BF16),
        ],
        scratch_shapes=[
            pltpu.VMEM((2 * rows, width), BF16),
            pltpu.VMEM((2 * rows, width), BF16),
            pltpu.VMEM((2, width, feats), BF16),
            pltpu.VMEM((feats, width), BF16),
            pltpu.VMEM((rows, feats), BF16),
            pltpu.VMEM((9 * tubes, 64, 2 * feats), BF16),
            pltpu.VMEM((tubes, keys, 2 * feats), BF16),
            pltpu.VMEM((tubes, heads * 64, keys), BF16),
            pltpu.SemaphoreType.DMA((9,)),
            pltpu.SemaphoreType.DMA((tubes,)),
        ],
        compiler_params=pltpu.CompilerParams(vmem_limit_bytes=VMEM_LIMIT),
        cost_estimate=SMALL,
        name="attend_forward",
    )(local, counts, x0, x1, gain, w, kv, q, w_out)


def parts_of(x, n):
    out = []
    for _ in range(n):
        piece = x.astype(BF16)
        out.append(piece)
        x = x - piece.astype(F32)
    return out


def middle_body(
    count_ref, sec_ref, mine_hbm, other_hbm, video_hbm, target_hbm, w_out_hbm, o_hbm, lse_ref, pay_ref, g_ref,
    mine_ref, other_ref, video_ref, target_ref, w_out_ref, o_ref, sem,
):
    rows, width = video_ref.shape
    feats = w_out_ref.shape[0]
    pairs = [
        (mine_hbm, mine_ref),
        (other_hbm, other_ref),
        (video_hbm, video_ref),
        (target_hbm, target_ref),
        (w_out_hbm, w_out_ref),
        (o_hbm, o_ref),
    ]
    copies = [pltpu.make_async_copy(*pair, sem.at[k]) for k, pair in enumerate(pairs)]
    for c in copies:
        c.start()
    heads = feats // HEAD_DIM
    tubes = rows // 64
    row = lax.broadcasted_iota(jnp.int32, (rows, 1), 0)
    limit = jnp.zeros((rows, 1), jnp.int32)
    for i in range(tubes):
        limit = jnp.where(row // 64 == i, count_ref[i], limit)
    valid = row % 64 < limit
    for c in copies[:4]:
        c.wait()
    mixed = mine_ref[...].astype(F32) + other_ref[...].astype(F32)
    g = jnp.where(valid, 2.0 * (video_ref[...].astype(F32) + mixed - target_ref[...].astype(F32)), 0.0)
    half = width // 2
    g_ref[...] = jnp.where(sec_ref[0] == 0, g[:, :half], g[:, half:])
    copies[4].wait()
    d_att = dot_nt(g.astype(BF16), w_out_ref[...]).astype(BF16)
    copies[5].wait()
    pay_ref[:rows] = d_att
    prod = d_att.astype(F32) * o_ref[...]
    head = lax.broadcasted_iota(jnp.int32, (heads, feats), 0)
    lane = lax.broadcasted_iota(jnp.int32, (heads, feats), 1)
    ones = ((lane >= head * HEAD_DIM) & (lane < (head + 1) * HEAD_DIM)).astype(F32)
    inner = []
    for i in range(tubes):
        one = prod[i * 64 : (i + 1) * 64]
        inner.append(
            lax.dot_general(
                ones,
                jnp.concatenate([one, one], axis=0),
                NT_DIMS,
                precision=lax.Precision.HIGHEST,
                preferred_element_type=F32,
            )
        )
    inner = jnp.concatenate(inner, axis=0)
    lse = lse_ref[...].reshape(tubes * heads, 128)
    for k, piece in enumerate(parts_of(lse, 3) + parts_of(inner, 2)):
        pay_ref[rows:, k * 128 : (k + 1) * 128] = piece


def middle(counts, sec, mine, other, video, target, w_out, o, lse):
    rows, width = video.shape
    feats = w_out.shape[0]
    vmem = pl.BlockSpec(memory_space=pltpu.VMEM)
    smem = pl.BlockSpec(memory_space=pltpu.SMEM)
    return pl.pallas_call(
        middle_body,
        in_specs=[smem, smem] + [pl.BlockSpec(memory_space=pl.ANY)] * 6 + [vmem],
        out_specs=[vmem, vmem],
        out_shape=[
            jax.ShapeDtypeStruct((rows + STAT_ROWS, feats), BF16),
            jax.ShapeDtypeStruct((rows, width // 2), F32),
        ],
        scratch_shapes=[pltpu.VMEM((rows, width), BF16)] * 4
        + [pltpu.VMEM((feats, width), BF16), pltpu.VMEM((rows, feats), F32), pltpu.SemaphoreType.DMA((6,))],
        compiler_params=pltpu.CompilerParams(vmem_limit_bytes=VMEM_LIMIT),
        cost_estimate=SMALL,
        name="middle",
    )(counts, sec, mine, other, video, target, w_out, o, lse)


def key_pass(
    list_ref, n_ref, count_ref, q_scr, kv_scr, pay_scr, lse_scr, inner_scr, qc_scr, dc_scr, km_scr, vm_scr, dk_scr, dv_scr, grad_scr
):
    tubes = kv_scr.shape[0]
    size = qc_scr.shape[0] // 64
    feats = q_scr.shape[2]
    most = list_ref.shape[0] // tubes
    low = lax.broadcasted_iota(jnp.int32, (8, 128), 1) < 64
    key_row = lax.broadcasted_iota(jnp.int32, (64, 1), 0)

    def tube(j, carry):
        alive = key_row < count_ref[j]
        block = pl.ds(pl.multiple_of(j * 64, 64), 64)
        for group in GROUPS:
            h0, nh, l0, wd = group
            these = slice(h0 * 64, (h0 + nh) * 64)
            km_scr[these, :wd] = spread(kv_scr[j, :, l0 : l0 + wd], group)
            vm_scr[these, :wd] = spread(kv_scr[j, :, feats + l0 : feats + l0 + wd], group)
        dk_scr[...] = jnp.zeros_like(dk_scr)
        dv_scr[...] = jnp.zeros_like(dv_scr)

        def chunk(c, carry):
            lses, inners = [], []
            for t in range(size):
                place = c * size + t
                i = list_ref[j * most + jnp.minimum(place, most - 1)]
                slot, w = i // tubes, i % tubes
                qc_scr[t * 64 : (t + 1) * 64, :] = q_scr[i]
                dc_scr[t * 64 : (t + 1) * 64, :] = pay_scr[slot, pl.ds(pl.multiple_of(w * 64, 64), 64), :]
                lses.append(jnp.where(place < n_ref[j], lse_scr[i], 1e30))
                inners.append(inner_scr[i])
            lse = jnp.concatenate([jnp.where(low, lses[t], lses[t + 1]) for t in range(0, size, 2)], axis=1)
            inner = jnp.concatenate([jnp.where(low, inners[t], inners[t + 1]) for t in range(0, size, 2)], axis=1)
            for group in GROUPS:
                h0, nh, l0, wd = group
                window = slice(l0, l0 + wd)
                these = slice(h0 * 64, (h0 + nh) * 64)
                qc, dc = qc_scr[:, window], dc_scr[:, window]
                s = dot_nt(km_scr[these, :wd], qc)
                d_prob = dot_nt(vm_scr[these, :wd], dc)
                p, d_score = [], []
                for m in range(nh):
                    part = slice(m * 64, (m + 1) * 64)
                    head = slice(h0 + m, h0 + m + 1)
                    one = jnp.where(alive, jnp.exp2(s[part] * LOG2_SCALE - lse[head]), 0.0)
                    p.append(one.astype(BF16))
                    d_score.append((one * (d_prob[part] - inner[head])).astype(BF16))
                dk_scr[these, :wd] += dot(jnp.concatenate(d_score, axis=0), qc)
                dv_scr[these, :wd] += dot(jnp.concatenate(p, axis=0), dc)
            return carry

        lax.fori_loop(0, (n_ref[j] + size - 1) // size, chunk, carry)
        for group in GROUPS:
            h0, nh, l0, wd = group
            these = slice(h0 * 64, (h0 + nh) * 64)
            grad_scr[block, l0 : l0 + wd] += gather_heads(dk_scr[these, :wd], group, 64) * SCALE
            grad_scr[block, feats + l0 : feats + l0 + wd] += gather_heads(dv_scr[these, :wd], group, 64)
        return carry

    lax.fori_loop(0, tubes, tube, 0)


def stats_of(pay_scr, k, rows, tubes, lse_scr, inner_scr):
    parts = [pay_scr[k, rows:, j * 128 : (j + 1) * 128].astype(F32) for j in range(5)]
    lse_scr[k * tubes : (k + 1) * tubes] = (parts[0] + parts[1] + parts[2]).reshape(tubes, -1, 128)
    inner_scr[k * tubes : (k + 1) * tubes] = (parts[3] + parts[4]).reshape(tubes, -1, 128)


def query_body(local_ref, pay_ref, kv_ref, far_ref, p_ref, dq_ref, all_scr, kv_scr, p_scr, pay_scr, dq_scr, sem, p_sem):
    tubes, keys, feats2 = kv_scr.shape
    feats = feats2 // 2
    pay_copy = pltpu.make_async_copy(pay_ref, pay_scr, sem.at[0])
    p_copies = [pltpu.make_async_copy(p_ref.at[i], p_scr.at[i], p_sem.at[i]) for i in range(tubes)]
    copies = [
        pltpu.make_async_copy(kv_ref.at[:tubes], all_scr.at[:tubes], sem.at[1]),
        pltpu.make_async_copy(kv_ref.at[6 * tubes :], all_scr.at[tubes : 7 * tubes], sem.at[2]),
        pltpu.make_async_copy(far_ref, all_scr.at[7 * tubes :], sem.at[3]),
    ]
    for c in copies + [pay_copy] + p_copies:
        c.start()
    for c in copies:
        c.wait()
    dq_scr[...] = jnp.zeros_like(dq_scr)
    pay_copy.wait()
    for i in range(tubes):
        here = slice(i * 64, (i + 1) * 64)
        lay_out_keys(local_ref, all_scr, kv_scr, i)
        p_copies[i].wait()
        for group in GROUPS:
            h0, nh, l0, wd = group
            window = slice(l0, l0 + wd)
            d_att = spread(pay_scr[here, window], group)
            d_prob = dot_nt(d_att, kv_scr[i, :, feats + l0 : feats + l0 + wd])
            p = p_scr[i, h0 * 64 : (h0 + nh) * 64, :].astype(F32)
            inner = jnp.sum(d_prob * p, axis=-1, keepdims=True)
            d_score = (p * (d_prob - inner)).astype(BF16)
            dq_scr[here, window] += gather_heads(dot(d_score, kv_scr[i, :, window]), group, 64)
    dq_ref[...] = (dq_scr[...] * SCALE).astype(BF16)


def query_grad(local, pay, kv, far, p):
    feats = pay.shape[1]
    tubes, _, keys = p.shape
    vmem = pl.BlockSpec(memory_space=pltpu.VMEM)
    smem = pl.BlockSpec(memory_space=pltpu.SMEM)
    hbm = pl.BlockSpec(memory_space=pl.ANY)
    return pl.pallas_call(
        query_body,
        in_specs=[smem] + [hbm] * 4,
        out_specs=vmem,
        out_shape=jax.ShapeDtypeStruct((tubes * 64, feats), BF16),
        scratch_shapes=[
            pltpu.VMEM((9 * tubes, 64, 2 * feats), BF16),
            pltpu.VMEM((tubes, keys, 2 * feats), BF16),
            pltpu.VMEM(p.shape, BF16),
            pltpu.VMEM(pay.shape, BF16),
            pltpu.VMEM((tubes * 64, feats), F32),
            pltpu.SemaphoreType.DMA((4,)),
            pltpu.SemaphoreType.DMA((tubes,)),
        ],
        compiler_params=pltpu.CompilerParams(vmem_limit_bytes=VMEM_LIMIT),
        cost_estimate=SMALL,
        name="query_grad",
    )(local, pay, kv, far, p)


def key_near_body(n, list_ref, n_ref, count_ref, own_q_ref, q_ref, kv_ref, w_ref, dq_ref, *rest):
    pays = rest[:n]
    grad_ref, base_ref, w_scr, dq_scr, q_scr, kv_scr, pay_scr, *scr, sem = rest[n:]
    lse_scr, inner_scr = scr[:2]
    tubes = kv_scr.shape[0]
    rows = tubes * 64
    pay_copies = [pltpu.make_async_copy(pays[k], pay_scr.at[k], sem.at[k]) for k in range(n)]
    first = [
        pltpu.make_async_copy(dq_ref, dq_scr, sem.at[n + 4]),
        pltpu.make_async_copy(w_ref.at[0], w_scr, sem.at[n]),
    ]
    copies = [
        pltpu.make_async_copy(own_q_ref, q_scr.at[:tubes], sem.at[n + 1]),
        pltpu.make_async_copy(q_ref.at[: (n - 1) * tubes], q_scr.at[tubes:], sem.at[n + 2]),
        pltpu.make_async_copy(kv_ref.at[:tubes], kv_scr, sem.at[n + 3]),
    ]
    for c in first + pay_copies + copies:
        c.start()
    grad_ref[...] = jnp.zeros_like(grad_ref)
    for c in first:
        c.wait()
    base_ref[...] = dot_nt(dq_scr[...], w_scr[...])
    for k in range(n):
        pay_copies[k].wait()
        stats_of(pay_scr, k, rows, tubes, lse_scr, inner_scr)
    for c in copies:
        c.wait()
    key_pass(list_ref, n_ref, count_ref, q_scr, kv_scr, pay_scr, *scr, grad_ref)


def key_scratch(n, tubes, feats, size):
    rows = tubes * 64
    heads = feats // HEAD_DIM
    return [
        pltpu.VMEM((n * tubes, 64, feats), BF16),
        pltpu.VMEM((tubes, 64, 2 * feats), BF16),
        pltpu.VMEM((n, rows + STAT_ROWS, feats), BF16),
        pltpu.VMEM((n * tubes, heads, 128), F32),
        pltpu.VMEM((n * tubes, heads, 128), F32),
        pltpu.VMEM((size * 64, feats), BF16),
        pltpu.VMEM((size * 64, feats), BF16),
        pltpu.VMEM((heads * 64, 384), BF16),
        pltpu.VMEM((heads * 64, 384), BF16),
        pltpu.VMEM((heads * 64, 384), F32),
        pltpu.VMEM((heads * 64, 384), F32),
    ]


def key_near(lists, lengths, counts, own_q, q, kv, w, dq, pays):
    rows, feats = dq.shape
    width = w.shape[1]
    tubes = rows // 64
    n = len(pays)
    vmem = pl.BlockSpec(memory_space=pltpu.VMEM)
    smem = pl.BlockSpec(memory_space=pltpu.SMEM)
    hbm = pl.BlockSpec(memory_space=pl.ANY)
    return pl.pallas_call(
        functools.partial(key_near_body, n),
        in_specs=[smem] * 3 + [hbm] * (5 + n),
        out_specs=[vmem, vmem],
        out_shape=[
            jax.ShapeDtypeStruct((rows, 2 * feats), F32),
            jax.ShapeDtypeStruct((rows, width), F32),
        ],
        scratch_shapes=[pltpu.VMEM((width, feats), BF16), pltpu.VMEM((rows, feats), BF16)]
        + key_scratch(n, tubes, feats, NEAR_CHUNK)
        + [pltpu.SemaphoreType.DMA((n + 5,))],
        compiler_params=pltpu.CompilerParams(vmem_limit_bytes=VMEM_LIMIT),
        cost_estimate=SMALL,
        name="key_near",
    )(lists, lengths, counts, own_q, q, kv, w, dq, *pays)


def key_last_body(n, first, list_ref, n_ref, count_ref, sec_ref, q_ref, kv_ref, w_ref, acc_ref, *rest):
    pays = rest[:n]
    video_ref, gain_ref, base_ref, g_ref, send_ref, keep_ref = rest[n : n + 6]
    q_scr, kv_scr, pay_scr, *scr, w_scr, grad_scr, x_scr, base_scr, g_scr, sem = rest[n + 6 :]
    lse_scr, inner_scr = scr[:2]
    tubes = kv_scr.shape[0]
    rows = tubes * 64
    feats = q_scr.shape[2]
    q_copy = pltpu.make_async_copy(q_ref.at[first * tubes : (first + n) * tubes], q_scr, sem.at[0])
    kv_copy = pltpu.make_async_copy(kv_ref.at[:tubes], kv_scr, sem.at[1])
    acc_copy = pltpu.make_async_copy(acc_ref, grad_scr, sem.at[2])
    w_copy = pltpu.make_async_copy(w_ref.at[1:], w_scr, sem.at[3])
    x_copy = pltpu.make_async_copy(video_ref, x_scr, sem.at[4])
    base_copy = pltpu.make_async_copy(base_ref, base_scr, sem.at[5])
    g_copy = pltpu.make_async_copy(g_ref, g_scr, sem.at[6])
    pay_copies = [pltpu.make_async_copy(pays[k], pay_scr.at[k], sem.at[7 + k]) for k in range(n)]
    for c in pay_copies + [q_copy, kv_copy, acc_copy, w_copy, x_copy, base_copy, g_copy]:
        c.start()
    for k, c in enumerate(pay_copies):
        c.wait()
        stats_of(pay_scr, k, rows, tubes, lse_scr, inner_scr)
    q_copy.wait()
    kv_copy.wait()
    acc_copy.wait()
    key_pass(list_ref, n_ref, count_ref, q_scr, kv_scr, pay_scr, *scr, grad_scr)
    d_proj = grad_scr[...].astype(BF16)
    x_copy.wait()
    xhat, inverse = normalize(x_scr[...].astype(F32))
    w_copy.wait()
    base_copy.wait()
    g_copy.wait()
    d_normed = base_scr[...] + dot_nt(d_proj[:, :feats], w_scr[0]) + dot_nt(d_proj[:, feats:], w_scr[1])
    scaled = d_normed * gain_ref[...]
    out = (
        scaled
        - jnp.mean(scaled, axis=-1, keepdims=True)
        - xhat * jnp.mean(scaled * xhat, axis=-1, keepdims=True)
    ) * inverse
    half = out.shape[1] // 2
    lower = sec_ref[0] == 0
    send_ref[...] = jnp.where(lower, out[:, half:], out[:, :half]).astype(BF16)
    keep_ref[...] = jnp.where(lower, out[:, :half], out[:, half:]) + g_scr[...]


def key_last(first, lists, lengths, counts, sec, q, kv, w, acc, pays, video, gain, base, g):
    rows, width = video.shape
    feats = q.shape[2]
    tubes = rows // 64
    n = len(pays)
    vmem = pl.BlockSpec(memory_space=pltpu.VMEM)
    smem = pl.BlockSpec(memory_space=pltpu.SMEM)
    hbm = pl.BlockSpec(memory_space=pl.ANY)
    return pl.pallas_call(
        functools.partial(key_last_body, n, first),
        in_specs=[smem] * 4 + [hbm] * (5 + n) + [vmem] + [hbm] * 2,
        out_specs=[vmem, vmem],
        out_shape=[
            jax.ShapeDtypeStruct((rows, width // 2), BF16),
            jax.ShapeDtypeStruct((rows, width // 2), F32),
        ],
        scratch_shapes=key_scratch(n, tubes, feats, LAST_CHUNK)
        + [
            pltpu.VMEM((2, width, feats), BF16),
            pltpu.VMEM((rows, 2 * feats), F32),
            pltpu.VMEM((rows, width), BF16),
            pltpu.VMEM((rows, width), F32),
            pltpu.VMEM((rows, width // 2), F32),
            pltpu.SemaphoreType.DMA((7 + n,)),
        ],
        compiler_params=pltpu.CompilerParams(vmem_limit_bytes=VMEM_LIMIT),
        cost_estimate=SMALL,
        name="key_last",
    )(lists, lengths, counts, sec, q, kv, w, acc, *pays, video, gain, base, g)


def per_device(video, target, gain, w_qkv, w_out, neighbours, counts):
    tt, th, tw, tube, width = video.shape
    feats = w_qkv.shape[2]
    nb = neighbours.shape[3]
    rows = tt * th * tw * tube
    n_t, n_h = lax.axis_size("tm"), lax.axis_size("height")
    t_here, h_here, sec = lax.axis_index("tm"), lax.axis_index("height"), lax.axis_index("section")
    off_chip = [p for h in range(1, n_h - 1, 2) for p in ((h, h + 1), (h + 1, h))]
    on_chip = [(h, h ^ 1) for h in range(n_h)]
    pair_times = [(t, t ^ 1) for t in range(n_t)]
    other_times = [p for t in range(1, n_t - 1, 2) for p in ((t, t + 1), (t + 1, t))]
    swap = [(0, 1), (1, 0)]

    def from_pair(x):
        return lax.ppermute(x, "tm", pair_times)

    def from_other(x):
        return lax.ppermute(x, "tm", other_times)

    def from_off(x):
        return lax.ppermute(x, "height", off_chip)

    def from_mate(x):
        return lax.ppermute(x, "height", on_chip)

    video = video.reshape(rows, width)
    target = target.reshape(rows, width)
    gain = gain.reshape(1, width)
    w = jnp.transpose(w_qkv, (1, 0, 2))

    off, mate, pair, other = from_off(video), from_mate(video), from_pair(video), from_other(video)
    meta = jnp.concatenate(
        [neighbours.reshape(tw, nb) + 1, counts.reshape(tw, 1), jnp.zeros((tw, 16 - nb - 1), jnp.int32)], axis=1
    )
    own_video, meta, _ = lax.optimization_barrier((video, meta, mate))
    kv, own_q = project_own(own_video, gain, w)
    three = jnp.stack([meta, from_pair(meta), from_other(meta)])
    off_meta, mate_meta = from_off(three), from_mate(three)
    off, off_meta, mate_meta, kv = lax.optimization_barrier((off, off_meta, mate_meta, kv))
    corners = from_pair(off), from_other(off)
    mates = mate, from_mate(pair), from_mate(other)
    kv, near_q = project_near((pair, other, off, *mates), 6, gain, w, kv)
    kv = kv.reshape(BLOCKS * tw, tube, 2 * feats)

    meta = jnp.concatenate([three, off_meta[:1], mate_meta, off_meta[1:]]).reshape(9 * tw, 16)
    listed = meta[:, :nb] - 1
    count_q = meta[:, nb].reshape(9, tw)
    count_all = count_q.reshape(9 * tw)

    ids = neighbours.reshape(tw, nb)
    t_of, h_of, w_of = ids // (n_h * tw), ids // tw % n_h, ids % tw
    step = jnp.where(t_of == t_here, 0, jnp.where(t_of == t_here + 1 - 2 * (t_here % 2), 1, 2))
    slot = jnp.where(
        h_of == h_here,
        step,
        jnp.where(h_of == h_here + 1 - 2 * (h_here % 2), 4 + step, jnp.where(step == 0, 3, 6 + step)),
    )
    local = (slot * tw + w_of).reshape(tw * nb)
    own_ids = (t_here * n_h + h_here) * tw + jnp.arange(tw, dtype=jnp.int32)
    names = jnp.any(listed[None] == own_ids[:, None, None], axis=2)

    def listing(first, last, most):
        named = names[:, first:last]
        where = jnp.arange(last - first, dtype=jnp.int32)
        rank = jnp.sum(named[:, None, :] & (where[None, :] < where[:, None])[None], axis=2)
        hit = named[:, None, :] & (rank[:, None, :] == jnp.arange(most)[None, :, None])
        places = jnp.sum(jnp.where(hit, where, 0), axis=2).astype(jnp.int32).reshape(tw * most)
        return places, jnp.sum(named, axis=1).astype(jnp.int32)

    near_list, near_n = listing(0, 7 * tw, 24)
    last_list, last_n = listing(7 * tw, 9 * tw, 8)
    sec = sec.reshape(1).astype(jnp.int32)
    own_counts = counts.reshape(tw)

    part, o, lse, p, far = attend_forward(local, count_all, *corners, gain, w, kv, own_q, w_out)
    other = lax.ppermute(part, "section", swap)
    part, videos = lax.optimization_barrier((part, corners))
    far_q = project_queries(videos, gain, w).reshape(2 * tw, tube, feats)
    other, far_q, near_list, near_n, last_list, last_n = lax.optimization_barrier(
        (other, far_q, near_list, near_n, last_list, last_n)
    )
    pay, g = middle(own_counts, sec, part, other, video, target, w_out, o, lse)
    off, mate = from_off(pay), from_mate(pay)
    pair, after = from_pair(pay), from_other(pay)
    dq = query_grad(local, pay, kv, far, p)
    dq, off = lax.optimization_barrier((dq, off))
    near, mates, corners = (pay, pair, after, off), (mate, from_mate(pair), from_mate(after)), (from_pair(off), from_other(off))
    acc, base = key_near(
        near_list, near_n, own_counts, own_q.reshape(tw, tube, feats), near_q.reshape(6 * tw, tube, feats), kv, w, dq, [*near, *mates]
    )
    send, keep = key_last(0, last_list, last_n, own_counts, sec, far_q, kv, w, acc, corners, video, gain, base, g)
    got = lax.ppermute(send, "section", swap)
    return (keep + got.astype(F32)).astype(BF16).reshape(tt, th, tw, tube, width // 2)


def solution(mesh):
    in_specs = (
        P("tm", "height", None, None, None),
        P("tm", "height", None, None, None),
        P(),
        P(None, None, "section"),
        P("section", None),
        P("tm", "height", None, None),
        P("tm", "height", None),
    )
    out_specs = P("tm", "height", None, None, "section")
    return jax.shard_map(
        per_device, mesh=mesh, in_specs=in_specs, out_specs=out_specs, check_vma=False
    )
```

```python
import functools
import math

import jax
import jax.numpy as jnp
from jax import lax
from jax.experimental import pallas as pl
from jax.experimental.pallas import tpu as pltpu
from jax.sharding import PartitionSpec as P

HEAD_DIM = 80
SCALE = HEAD_DIM ** (-0.5)
LOG2_SCALE = SCALE * math.log2(math.e)
BF16 = jnp.bfloat16
F32 = jnp.float32
MIB = 1 << 20
GROUPS = ((0, 3, 0, 256), (3, 2, 128, 384), (5, 3, 384, 256))
NEAR_CHUNK, LAST_CHUNK = 8, 2
STAT_ROWS = 32
BLOCKS = 12
SMALL = pl.CostEstimate(flops=1, bytes_accessed=1, transcendentals=0)
VMEM_LIMIT = 52 * MIB

NT_DIMS = (((1,), (1,)), ((), ()))


def dot(a, b):
    return jnp.dot(a, b, preferred_element_type=F32)


def dot_nt(a, b):
    return lax.dot_general(a, b, NT_DIMS, preferred_element_type=F32)


def head_row(head, first_lane, lanes):
    lane = lax.broadcasted_iota(jnp.int32, (1, lanes), 1) + first_lane
    return jnp.where((lane >= head * HEAD_DIM) & (lane < (head + 1) * HEAD_DIM), 1.0, 0.0).astype(F32)


def spread(x, group):
    h0, nh, l0, wd = group
    out = []
    for h in range(h0, h0 + nh):
        mask = jnp.broadcast_to(head_row(h, l0, wd), (16, wd)).astype(BF16)
        out += [x[r : r + 16] * mask for r in range(0, x.shape[0], 16)]
    return jnp.concatenate(out, axis=0)


def gather_heads(y, group, rows):
    h0, nh, l0, wd = group
    total = y[:rows] * head_row(h0, l0, wd)
    for k in range(1, nh):
        total = total + y[k * rows : (k + 1) * rows] * head_row(h0 + k, l0, wd)
    return total


def add_group(ref, rows, value, group):
    h0, nh, l0, wd = group
    ref[rows, l0 : l0 + wd] = ref[rows, l0 : l0 + wd] + value


def gain_of(gain_ref):
    return gain_ref[...].reshape(1, -1)


def normalize(x):
    centred = x - jnp.mean(x, axis=-1, keepdims=True)
    inverse = lax.rsqrt(jnp.mean(centred * centred, axis=-1, keepdims=True) + 1e-06)
    return centred * inverse, inverse


def project_near_body(n, *refs):
    xs = refs[:n]
    gain_ref, w_ref = refs[n : n + 2]
    kv_ref, x_scr = refs[n + 3 :]
    rows = xs[0].shape[0]

    @pl.when(pl.program_id(0) == 0)
    def _():
        for k in range(n):
            x_scr[k * rows : (k + 1) * rows] = (normalize(xs[k][...].astype(F32))[0] * gain_of(gain_ref)).astype(BF16)

    kv_ref[...] = dot(x_scr[...], w_ref[...]).astype(BF16).reshape(kv_ref.shape)


def whole(a):
    return pl.BlockSpec(a.shape, lambda i: (0,) * a.ndim)


def project_near(blocks, first, gain, w, buf):
    n = len(blocks)
    rows, width = blocks[0].shape
    feats = w.shape[2]
    return pl.pallas_call(
        functools.partial(project_near_body, n),
        grid=(2,),
        in_specs=[whole(b) for b in blocks]
        + [whole(gain), pl.BlockSpec((pl.squeezed, width, feats), lambda i: (i + 1, 0, 0))]
        + [pl.BlockSpec(memory_space=pl.ANY)],
        out_specs=pl.BlockSpec((n, rows, feats), lambda i: (first // n, 0, i)),
        out_shape=jax.ShapeDtypeStruct(buf.shape, BF16),
        scratch_shapes=[pltpu.VMEM((n * rows, width), BF16)],
        input_output_aliases={n + 2: 0},
        compiler_params=pltpu.CompilerParams(vmem_limit_bytes=VMEM_LIMIT),
        cost_estimate=SMALL,
        name="project_near",
    )(*blocks, gain, w, buf)


def project_own_body(x_ref, gain_ref, w_ref, kv_ref, q_ref, x_scr):
    step = pl.program_id(0)

    @pl.when(step == 0)
    def _():
        x_scr[...] = (normalize(x_ref[...].astype(F32))[0] * gain_of(gain_ref)).astype(BF16)

    @pl.when(step < 2)
    def _():
        kv_ref[0] = dot(x_scr[...], w_ref[...]).astype(BF16)

    @pl.when(step == 2)
    def _():
        q_ref[...] = dot(x_scr[...], w_ref[...]).astype(BF16)


def project_own(x, gain, w):
    rows, width = x.shape
    feats = w.shape[2]
    return pl.pallas_call(
        project_own_body,
        grid=(3,),
        in_specs=[whole(x), whole(gain), pl.BlockSpec((pl.squeezed, width, feats), lambda i: ((i + 1) % 3, 0, 0))],
        out_specs=[
            pl.BlockSpec((1, rows, feats), lambda i: (0, 0, jnp.minimum(i, 1))),
            pl.BlockSpec((rows, feats), lambda i: (0, 0)),
        ],
        out_shape=[
            jax.ShapeDtypeStruct((BLOCKS, rows, 2 * feats), BF16),
            jax.ShapeDtypeStruct((rows, feats), BF16),
        ],
        scratch_shapes=[pltpu.VMEM((rows, width), BF16)],
        compiler_params=pltpu.CompilerParams(vmem_limit_bytes=VMEM_LIMIT),
        cost_estimate=SMALL,
        name="project_own",
    )(x, gain, w)


def project_queries_body(n, *refs):
    xs = refs[:n]
    gain_ref, w_ref, out_ref, x_scr = refs[n:]
    step = pl.program_id(0)
    for k in range(n):

        @pl.when(step == k)
        def _():
            x_scr[...] = xs[k][...]

    normed = (normalize(x_scr[...].astype(F32))[0] * gain_of(gain_ref)).astype(BF16)
    out_ref[0] = dot(normed, w_ref[...]).astype(BF16)


def project_queries(blocks, gain, w):
    n = len(blocks)
    rows, width = blocks[0].shape
    feats = w.shape[2]
    return pl.pallas_call(
        functools.partial(project_queries_body, n),
        grid=(n,),
        in_specs=[whole(b) for b in blocks] + [whole(gain), pl.BlockSpec((pl.squeezed, width, feats), lambda i: (0, 0, 0))],
        out_specs=pl.BlockSpec((1, rows, feats), lambda i: (i, 0, 0)),
        out_shape=jax.ShapeDtypeStruct((n, rows, feats), BF16),
        scratch_shapes=[pltpu.VMEM((rows, width), BF16)],
        compiler_params=pltpu.CompilerParams(vmem_limit_bytes=VMEM_LIMIT),
        cost_estimate=SMALL,
        name="project_queries",
    )(*blocks, gain, w)


def lay_out_keys(local_ref, all_scr, kv_scr, i):
    nb = kv_scr.shape[1] // 64
    for n in range(nb):
        kv_scr[i, n * 64 : (n + 1) * 64, :] = all_scr[local_ref[i, n]]


def forward_body(
    local_ref, count_ref, x0_ref, x1_ref, gain_ref, w_ref, kv_ref, q_ref, w_out_ref,
    part_ref, o_ref, lse_ref, p_ref, far_ref,
    n_scr, w_scr, wo_scr, q_scr, all_scr, kv_scr, p_scr, sem, p_sem,
):
    tubes, keys, feats2 = kv_scr.shape
    feats = feats2 // 2
    nb = keys // 64
    rows = tubes * 64
    copies = [
        pltpu.make_async_copy(w_ref.at[1], w_scr.at[0], sem.at[2]),
        pltpu.make_async_copy(w_ref.at[2], w_scr.at[1], sem.at[3]),
        pltpu.make_async_copy(q_ref, q_scr, sem.at[4]),
        pltpu.make_async_copy(w_out_ref, wo_scr, sem.at[5]),
        pltpu.make_async_copy(kv_ref.at[:tubes], all_scr.at[:tubes], sem.at[6]),
        pltpu.make_async_copy(kv_ref.at[6 * tubes :], all_scr.at[tubes : 7 * tubes], sem.at[7]),
    ]
    for k in (0, 1, 4, 5, 2, 3):
        copies[k].start()
    for k, x_ref in enumerate((x0_ref, x1_ref)):
        n_scr[k * rows : (k + 1) * rows] = (normalize(x_ref[...].astype(F32))[0] * gain_of(gain_ref)).astype(BF16)
    for k in range(2):
        copies[k].wait()
        out = dot(n_scr[...], w_scr[k]).astype(BF16).reshape(2 * tubes, 64, feats)
        all_scr[7 * tubes :, :, k * feats : (k + 1) * feats] = out
    far_copy = pltpu.make_async_copy(all_scr.at[7 * tubes :], far_ref, sem.at[8])
    far_copy.start()
    for k in (4, 5, 2):
        copies[k].wait()
    lane = lax.broadcasted_iota(jnp.int32, (1, keys), 1)
    slot, place = lane // 64, lane % 64
    pick = lax.broadcasted_iota(jnp.int32, (64, 128), 0) == lax.broadcasted_iota(jnp.int32, (64, 128), 1) % 64
    o_ref[...] = jnp.zeros_like(o_ref)

    def tube(i):
        limit = jnp.zeros((1, keys), jnp.int32)
        for n in range(nb):
            limit = jnp.where(slot == n, count_ref[local_ref[i, n] // tubes, local_ref[i, n] % tubes], limit)
        live = place < limit
        here = slice(i * 64, (i + 1) * 64)
        lay_out_keys(local_ref, all_scr, kv_scr, i)
        for group in GROUPS:
            h0, nh, l0, wd = group
            window = slice(l0, l0 + wd)
            q = spread(q_scr[here, window], group)
            s = dot_nt(q, kv_scr[i, :, window]) * LOG2_SCALE
            s = jnp.where(live, s, -1e30)
            top = jnp.max(s, axis=-1, keepdims=True)
            e = jnp.exp2(s - top)
            total = jnp.sum(e, axis=-1, keepdims=True)
            p = (e * (1.0 / total)).astype(BF16)
            p_scr[i, h0 * 64 : (h0 + nh) * 64, :] = p
            o = dot(p, kv_scr[i, :, feats + l0 : feats + l0 + wd])
            o_ref[here, window] += gather_heads(o, group, 64)
            lse = top + jnp.log2(total)
            for k in range(nh):
                column = jnp.broadcast_to(lse[k * 64 : (k + 1) * 64], (64, 128))
                lse_ref[i, h0 + k : h0 + k + 1, :] = jnp.sum(jnp.where(pick, column, 0.0), axis=0, keepdims=True)
        pltpu.make_async_copy(p_scr.at[i], p_ref.at[i], p_sem.at[i]).start()

    for i in range(tubes):
        tube(i)
    copies[3].wait()
    part_ref[...] = dot(o_ref[...].astype(BF16), wo_scr[...]).astype(BF16)
    far_copy.wait()
    for i in range(tubes):
        pltpu.make_async_copy(p_scr.at[i], p_ref.at[i], p_sem.at[i]).wait()


def attend_forward(local, counts, x0, x1, gain, w, kv, q, w_out):
    rows, feats = q.shape
    tubes = rows // 64
    keys = local.shape[1] * 64
    heads = feats // HEAD_DIM
    width = w_out.shape[1]
    vmem = pl.BlockSpec(memory_space=pltpu.VMEM)
    smem = pl.BlockSpec(memory_space=pltpu.SMEM)
    hbm = pl.BlockSpec(memory_space=pl.ANY)
    return pl.pallas_call(
        forward_body,
        in_specs=[smem, smem, vmem, vmem, vmem, hbm, hbm, hbm, hbm],
        out_specs=[vmem, vmem, vmem, hbm, hbm],
        out_shape=[
            jax.ShapeDtypeStruct((rows, width), BF16),
            jax.ShapeDtypeStruct((rows, feats), F32),
            jax.ShapeDtypeStruct((tubes, heads, 128), F32),
            jax.ShapeDtypeStruct((tubes, heads * 64, keys), BF16),
            jax.ShapeDtypeStruct((2 * tubes, 64, 2 * feats), BF16),
        ],
        scratch_shapes=[
            pltpu.VMEM((2 * rows, width), BF16),
            pltpu.VMEM((2, width, feats), BF16),
            pltpu.VMEM((feats, width), BF16),
            pltpu.VMEM((rows, feats), BF16),
            pltpu.VMEM((9 * tubes, 64, 2 * feats), BF16),
            pltpu.VMEM((tubes, keys, 2 * feats), BF16),
            pltpu.VMEM((tubes, heads * 64, keys), BF16),
            pltpu.SemaphoreType.DMA((9,)),
            pltpu.SemaphoreType.DMA((tubes,)),
        ],
        compiler_params=pltpu.CompilerParams(vmem_limit_bytes=VMEM_LIMIT),
        cost_estimate=SMALL,
        name="attend_forward",
    )(local, counts, x0, x1, gain, w, kv, q, w_out)


def parts_of(x, n):
    out = []
    for _ in range(n):
        piece = x.astype(BF16)
        out.append(piece)
        x = x - piece.astype(F32)
    return out


def middle_body(
    count_ref, sec_ref, mine_hbm, other_ref, video_hbm, target_hbm, w_out_hbm, o_hbm, lse_ref, pay_ref, g_ref,
    mine_ref, video_ref, target_ref, w_out_ref, o_ref, sem,
):
    rows, width = video_ref.shape
    feats = w_out_ref.shape[0]
    pairs = [
        (mine_hbm, mine_ref),
        (video_hbm, video_ref),
        (target_hbm, target_ref),
        (w_out_hbm, w_out_ref),
        (o_hbm, o_ref),
    ]
    copies = [pltpu.make_async_copy(*pair, sem.at[k]) for k, pair in enumerate(pairs)]
    for c in copies:
        c.start()
    heads = feats // HEAD_DIM
    tubes = rows // 64
    row = lax.broadcasted_iota(jnp.int32, (rows, 1), 0)
    limit = jnp.zeros((rows, 1), jnp.int32)
    for i in range(tubes):
        limit = jnp.where(row // 64 == i, count_ref[i], limit)
    valid = row % 64 < limit
    for c in copies[:3]:
        c.wait()
    mixed = mine_ref[...].astype(F32) + other_ref[...].astype(F32)
    g = jnp.where(valid, 2.0 * (video_ref[...].astype(F32) + mixed - target_ref[...].astype(F32)), 0.0)
    half = width // 2
    g_ref[...] = jnp.where(sec_ref[0] == 0, g[:, :half], g[:, half:])
    copies[3].wait()
    d_att = dot_nt(g.astype(BF16), w_out_ref[...]).astype(BF16)
    copies[4].wait()
    pay_ref[:rows] = d_att
    prod = d_att.astype(F32) * o_ref[...]
    head = lax.broadcasted_iota(jnp.int32, (heads, feats), 0)
    lane = lax.broadcasted_iota(jnp.int32, (heads, feats), 1)
    ones = ((lane >= head * HEAD_DIM) & (lane < (head + 1) * HEAD_DIM)).astype(F32)
    inner = []
    for i in range(tubes):
        one = prod[i * 64 : (i + 1) * 64]
        inner.append(
            lax.dot_general(
                ones,
                jnp.concatenate([one, one], axis=0),
                NT_DIMS,
                precision=lax.Precision.HIGHEST,
                preferred_element_type=F32,
            )
        )
    inner = jnp.concatenate(inner, axis=0)
    lse = lse_ref[...].reshape(tubes * heads, 128)
    for k, piece in enumerate(parts_of(lse, 3) + parts_of(inner, 2)):
        pay_ref[rows:, k * 128 : (k + 1) * 128] = piece


def middle(counts, sec, mine, other, video, target, w_out, o, lse):
    rows, width = video.shape
    feats = w_out.shape[0]
    vmem = pl.BlockSpec(memory_space=pltpu.VMEM)
    smem = pl.BlockSpec(memory_space=pltpu.SMEM)
    return pl.pallas_call(
        middle_body,
        in_specs=[smem, smem] + [pl.BlockSpec(memory_space=pl.ANY), vmem] + [pl.BlockSpec(memory_space=pl.ANY)] * 4 + [vmem],
        out_specs=[vmem, vmem],
        out_shape=[
            jax.ShapeDtypeStruct((rows + STAT_ROWS, feats), BF16),
            jax.ShapeDtypeStruct((rows, width // 2), F32),
        ],
        scratch_shapes=[pltpu.VMEM((rows, width), BF16)] * 3
        + [pltpu.VMEM((feats, width), BF16), pltpu.VMEM((rows, feats), F32), pltpu.SemaphoreType.DMA((5,))],
        compiler_params=pltpu.CompilerParams(vmem_limit_bytes=VMEM_LIMIT),
        cost_estimate=SMALL,
        name="middle",
    )(counts, sec, mine, other, video, target, w_out, o, lse)


def key_pass(
    list_ref, count_ref, q_scr, kv_scr, pay_scr, lse_scr, inner_scr, qc_scr, dc_scr, km_scr, vm_scr, dk_scr, dv_scr, grad_scr
):
    tubes = kv_scr.shape[0]
    size = qc_scr.shape[0] // 64
    feats = q_scr.shape[2]
    most = list_ref.shape[1] - 1
    low = lax.broadcasted_iota(jnp.int32, (8, 128), 1) < 64
    key_row = lax.broadcasted_iota(jnp.int32, (64, 1), 0)

    def tube(j, carry):
        alive = key_row < count_ref[j]
        block = pl.ds(pl.multiple_of(j * 64, 64), 64)
        for group in GROUPS:
            h0, nh, l0, wd = group
            these = slice(h0 * 64, (h0 + nh) * 64)
            km_scr[these, :wd] = spread(kv_scr[j, :, l0 : l0 + wd], group)
            vm_scr[these, :wd] = spread(kv_scr[j, :, feats + l0 : feats + l0 + wd], group)
        dk_scr[...] = jnp.zeros_like(dk_scr)
        dv_scr[...] = jnp.zeros_like(dv_scr)

        def chunk(c, carry):
            lses, inners = [], []
            for t in range(size):
                place = c * size + t
                i = list_ref[j, jnp.minimum(place, most - 1)]
                slot, w = i // tubes, i % tubes
                qc_scr[t * 64 : (t + 1) * 64, :] = q_scr[i]
                dc_scr[t * 64 : (t + 1) * 64, :] = pay_scr[slot, pl.ds(pl.multiple_of(w * 64, 64), 64), :]
                lses.append(jnp.where(place < list_ref[j, most], lse_scr[i], 1e30))
                inners.append(inner_scr[i])
            lse = jnp.concatenate([jnp.where(low, lses[t], lses[t + 1]) for t in range(0, size, 2)], axis=1)
            inner = jnp.concatenate([jnp.where(low, inners[t], inners[t + 1]) for t in range(0, size, 2)], axis=1)
            for group in GROUPS:
                h0, nh, l0, wd = group
                window = slice(l0, l0 + wd)
                these = slice(h0 * 64, (h0 + nh) * 64)
                qc, dc = qc_scr[:, window], dc_scr[:, window]
                s = dot_nt(km_scr[these, :wd], qc)
                d_prob = dot_nt(vm_scr[these, :wd], dc)
                p, d_score = [], []
                for m in range(nh):
                    part = slice(m * 64, (m + 1) * 64)
                    head = slice(h0 + m, h0 + m + 1)
                    one = jnp.where(alive, jnp.exp2(s[part] * LOG2_SCALE - lse[head]), 0.0)
                    p.append(one.astype(BF16))
                    d_score.append((one * (d_prob[part] - inner[head])).astype(BF16))
                dk_scr[these, :wd] += dot(jnp.concatenate(d_score, axis=0), qc)
                dv_scr[these, :wd] += dot(jnp.concatenate(p, axis=0), dc)
            return carry

        lax.fori_loop(0, (list_ref[j, most] + size - 1) // size, chunk, carry)
        for group in GROUPS:
            h0, nh, l0, wd = group
            these = slice(h0 * 64, (h0 + nh) * 64)
            grad_scr[block, l0 : l0 + wd] += gather_heads(dk_scr[these, :wd], group, 64) * SCALE
            grad_scr[block, feats + l0 : feats + l0 + wd] += gather_heads(dv_scr[these, :wd], group, 64)
        return carry

    lax.fori_loop(0, tubes, tube, 0)


def stats_of(pay_scr, k, rows, tubes, lse_scr, inner_scr):
    parts = [pay_scr[k, rows:, j * 128 : (j + 1) * 128].astype(F32) for j in range(5)]
    lse_scr[k * tubes : (k + 1) * tubes] = (parts[0] + parts[1] + parts[2]).reshape(tubes, -1, 128)
    inner_scr[k * tubes : (k + 1) * tubes] = (parts[3] + parts[4]).reshape(tubes, -1, 128)


def query_body(local_ref, pay_ref, kv_ref, far_ref, p_ref, dq_ref, all_scr, kv_scr, p_scr, pay_scr, dq_scr, sem, p_sem):
    tubes, keys, feats2 = kv_scr.shape
    feats = feats2 // 2
    pay_copy = pltpu.make_async_copy(pay_ref, pay_scr, sem.at[0])
    p_copies = [pltpu.make_async_copy(p_ref.at[i], p_scr.at[i], p_sem.at[i]) for i in range(tubes)]
    copies = [
        pltpu.make_async_copy(kv_ref.at[:tubes], all_scr.at[:tubes], sem.at[1]),
        pltpu.make_async_copy(kv_ref.at[6 * tubes :], all_scr.at[tubes : 7 * tubes], sem.at[2]),
        pltpu.make_async_copy(far_ref, all_scr.at[7 * tubes :], sem.at[3]),
    ]
    for c in copies + [pay_copy] + p_copies:
        c.start()
    for c in copies:
        c.wait()
    dq_scr[...] = jnp.zeros_like(dq_scr)
    pay_copy.wait()
    for i in range(tubes):
        here = slice(i * 64, (i + 1) * 64)
        lay_out_keys(local_ref, all_scr, kv_scr, i)
        p_copies[i].wait()
        for group in GROUPS:
            h0, nh, l0, wd = group
            window = slice(l0, l0 + wd)
            d_att = spread(pay_scr[here, window], group)
            d_prob = dot_nt(d_att, kv_scr[i, :, feats + l0 : feats + l0 + wd])
            p = p_scr[i, h0 * 64 : (h0 + nh) * 64, :].astype(F32)
            inner = jnp.sum(d_prob * p, axis=-1, keepdims=True)
            d_score = (p * (d_prob - inner)).astype(BF16)
            dq_scr[here, window] += gather_heads(dot(d_score, kv_scr[i, :, window]), group, 64)
    dq_ref[...] = (dq_scr[...] * SCALE).astype(BF16)


def query_grad(local, pay, kv, far, p):
    feats = pay.shape[1]
    tubes, _, keys = p.shape
    vmem = pl.BlockSpec(memory_space=pltpu.VMEM)
    smem = pl.BlockSpec(memory_space=pltpu.SMEM)
    hbm = pl.BlockSpec(memory_space=pl.ANY)
    return pl.pallas_call(
        query_body,
        in_specs=[smem] + [hbm] * 4,
        out_specs=vmem,
        out_shape=jax.ShapeDtypeStruct((tubes * 64, feats), BF16),
        scratch_shapes=[
            pltpu.VMEM((9 * tubes, 64, 2 * feats), BF16),
            pltpu.VMEM((tubes, keys, 2 * feats), BF16),
            pltpu.VMEM(p.shape, BF16),
            pltpu.VMEM(pay.shape, BF16),
            pltpu.VMEM((tubes * 64, feats), F32),
            pltpu.SemaphoreType.DMA((4,)),
            pltpu.SemaphoreType.DMA((tubes,)),
        ],
        compiler_params=pltpu.CompilerParams(vmem_limit_bytes=VMEM_LIMIT),
        cost_estimate=SMALL,
        name="query_grad",
    )(local, pay, kv, far, p)


def key_near_body(n, list_ref, count_ref, own_q_ref, q_ref, kv_ref, w_ref, dq_ref, *rest):
    pays = rest[:n]
    grad_ref, base_ref, w_scr, dq_scr, q_scr, kv_scr, pay_scr, *scr, sem = rest[n:]
    lse_scr, inner_scr = scr[:2]
    tubes = kv_scr.shape[0]
    rows = tubes * 64
    pay_copies = [pltpu.make_async_copy(pays[k], pay_scr.at[k], sem.at[k]) for k in range(n)]
    first = [
        pltpu.make_async_copy(dq_ref, dq_scr, sem.at[n + 4]),
        pltpu.make_async_copy(w_ref.at[0], w_scr, sem.at[n]),
    ]
    copies = [
        pltpu.make_async_copy(own_q_ref, q_scr.at[:tubes], sem.at[n + 1]),
        pltpu.make_async_copy(q_ref.at[: (n - 1) * tubes], q_scr.at[tubes:], sem.at[n + 2]),
        pltpu.make_async_copy(kv_ref.at[:tubes], kv_scr, sem.at[n + 3]),
    ]
    for c in first + pay_copies + copies:
        c.start()
    grad_ref[...] = jnp.zeros_like(grad_ref)
    for c in first:
        c.wait()
    base_ref[...] = dot_nt(dq_scr[...], w_scr[...])
    for k in range(n):
        pay_copies[k].wait()
        stats_of(pay_scr, k, rows, tubes, lse_scr, inner_scr)
    for c in copies:
        c.wait()
    key_pass(list_ref, count_ref, q_scr, kv_scr, pay_scr, *scr, grad_ref)


def key_scratch(n, tubes, feats, size):
    rows = tubes * 64
    heads = feats // HEAD_DIM
    return [
        pltpu.VMEM((n * tubes, 64, feats), BF16),
        pltpu.VMEM((tubes, 64, 2 * feats), BF16),
        pltpu.VMEM((n, rows + STAT_ROWS, feats), BF16),
        pltpu.VMEM((n * tubes, heads, 128), F32),
        pltpu.VMEM((n * tubes, heads, 128), F32),
        pltpu.VMEM((size * 64, feats), BF16),
        pltpu.VMEM((size * 64, feats), BF16),
        pltpu.VMEM((heads * 64, 384), BF16),
        pltpu.VMEM((heads * 64, 384), BF16),
        pltpu.VMEM((heads * 64, 384), F32),
        pltpu.VMEM((heads * 64, 384), F32),
    ]


def key_near(lists, counts, own_q, q, kv, w, dq, pays):
    rows, feats = dq.shape
    width = w.shape[1]
    tubes = rows // 64
    n = len(pays)
    vmem = pl.BlockSpec(memory_space=pltpu.VMEM)
    smem = pl.BlockSpec(memory_space=pltpu.SMEM)
    hbm = pl.BlockSpec(memory_space=pl.ANY)
    return pl.pallas_call(
        functools.partial(key_near_body, n),
        in_specs=[smem] * 2 + [hbm] * 5 + [vmem] * n,
        out_specs=[vmem, vmem],
        out_shape=[
            jax.ShapeDtypeStruct((rows, 2 * feats), F32),
            jax.ShapeDtypeStruct((rows, width), F32),
        ],
        scratch_shapes=[pltpu.VMEM((width, feats), BF16), pltpu.VMEM((rows, feats), BF16)]
        + key_scratch(n, tubes, feats, NEAR_CHUNK)
        + [pltpu.SemaphoreType.DMA((n + 5,))],
        compiler_params=pltpu.CompilerParams(vmem_limit_bytes=VMEM_LIMIT),
        cost_estimate=SMALL,
        name="key_near",
    )(lists, counts, own_q, q, kv, w, dq, *pays)


def key_last_body(n, first, list_ref, count_ref, sec_ref, q_ref, kv_ref, w_ref, acc_ref, *rest):
    pays = rest[:n]
    video_ref, gain_ref, base_ref, g_ref, send_ref, keep_ref = rest[n : n + 6]
    q_scr, kv_scr, pay_scr, *scr, w_scr, grad_scr, x_scr, base_scr, g_scr, sem = rest[n + 6 :]
    lse_scr, inner_scr = scr[:2]
    tubes = kv_scr.shape[0]
    rows = tubes * 64
    feats = q_scr.shape[2]
    q_copy = pltpu.make_async_copy(q_ref.at[first * tubes : (first + n) * tubes], q_scr, sem.at[0])
    kv_copy = pltpu.make_async_copy(kv_ref.at[:tubes], kv_scr, sem.at[1])
    acc_copy = pltpu.make_async_copy(acc_ref, grad_scr, sem.at[2])
    w_copy = pltpu.make_async_copy(w_ref.at[1:], w_scr, sem.at[3])
    x_copy = pltpu.make_async_copy(video_ref, x_scr, sem.at[4])
    base_copy = pltpu.make_async_copy(base_ref, base_scr, sem.at[5])
    g_copy = pltpu.make_async_copy(g_ref, g_scr, sem.at[6])
    pay_copies = [pltpu.make_async_copy(pays[k], pay_scr.at[k], sem.at[7 + k]) for k in range(n)]
    for c in pay_copies + [q_copy, kv_copy, acc_copy, w_copy, x_copy, base_copy, g_copy]:
        c.start()
    for k, c in enumerate(pay_copies):
        c.wait()
        stats_of(pay_scr, k, rows, tubes, lse_scr, inner_scr)
    q_copy.wait()
    kv_copy.wait()
    acc_copy.wait()
    key_pass(list_ref, count_ref, q_scr, kv_scr, pay_scr, *scr, grad_scr)
    d_proj = grad_scr[...].astype(BF16)
    x_copy.wait()
    xhat, inverse = normalize(x_scr[...].astype(F32))
    w_copy.wait()
    base_copy.wait()
    g_copy.wait()
    d_normed = base_scr[...] + dot_nt(d_proj[:, :feats], w_scr[0]) + dot_nt(d_proj[:, feats:], w_scr[1])
    scaled = d_normed * gain_of(gain_ref)
    out = (
        scaled
        - jnp.mean(scaled, axis=-1, keepdims=True)
        - xhat * jnp.mean(scaled * xhat, axis=-1, keepdims=True)
    ) * inverse
    half = out.shape[1] // 2
    lower = sec_ref[0] == 0
    send_ref[...] = jnp.where(lower, out[:, half:], out[:, :half]).astype(BF16)
    keep_ref[...] = jnp.where(lower, out[:, :half], out[:, half:]) + g_scr[...]


def key_last(first, lists, counts, sec, q, kv, w, acc, pays, video, gain, base, g):
    rows, width = video.shape
    feats = q.shape[2]
    tubes = rows // 64
    n = len(pays)
    vmem = pl.BlockSpec(memory_space=pltpu.VMEM)
    smem = pl.BlockSpec(memory_space=pltpu.SMEM)
    hbm = pl.BlockSpec(memory_space=pl.ANY)
    return pl.pallas_call(
        functools.partial(key_last_body, n, first),
        in_specs=[smem] * 3 + [hbm] * 4 + [vmem] * n + [hbm] + [vmem] + [hbm] * 2,
        out_specs=[vmem, vmem],
        out_shape=[
            jax.ShapeDtypeStruct((rows, width // 2), BF16),
            jax.ShapeDtypeStruct((rows, width // 2), F32),
        ],
        scratch_shapes=key_scratch(n, tubes, feats, LAST_CHUNK)
        + [
            pltpu.VMEM((2, width, feats), BF16),
            pltpu.VMEM((rows, 2 * feats), F32),
            pltpu.VMEM((rows, width), BF16),
            pltpu.VMEM((rows, width), F32),
            pltpu.VMEM((rows, width // 2), F32),
            pltpu.SemaphoreType.DMA((7 + n,)),
        ],
        compiler_params=pltpu.CompilerParams(vmem_limit_bytes=VMEM_LIMIT),
        cost_estimate=SMALL,
        name="key_last",
    )(lists, counts, sec, q, kv, w, acc, *pays, video, gain, base, g)


def per_device(video, target, gain, w_qkv, w_out, neighbours, counts):
    tt, th, tw, tube, width = video.shape
    feats = w_qkv.shape[2]
    nb = neighbours.shape[3]
    rows = tt * th * tw * tube
    n_t, n_h = lax.axis_size("tm"), lax.axis_size("height")
    t_here, h_here, sec = lax.axis_index("tm"), lax.axis_index("height"), lax.axis_index("section")
    off_chip = [p for h in range(1, n_h - 1, 2) for p in ((h, h + 1), (h + 1, h))]
    on_chip = [(h, h ^ 1) for h in range(n_h)]
    pair_times = [(t, t ^ 1) for t in range(n_t)]
    other_times = [p for t in range(1, n_t - 1, 2) for p in ((t, t + 1), (t + 1, t))]
    swap = [(0, 1), (1, 0)]

    def from_pair(x):
        return lax.ppermute(x, "tm", pair_times)

    def from_other(x):
        return lax.ppermute(x, "tm", other_times)

    def from_off(x):
        return lax.ppermute(x, "height", off_chip)

    def from_mate(x):
        return lax.ppermute(x, "height", on_chip)

    video = video.reshape(rows, width)
    target = target.reshape(rows, width)
    w = jnp.transpose(w_qkv, (1, 0, 2))

    off, mate, pair, other = from_off(video), from_mate(video), from_pair(video), from_other(video)
    meta = jnp.concatenate(
        [neighbours.reshape(tw, nb) + 1, jnp.pad(counts.reshape(1, tw), ((0, 0), (0, nb - tw)))], axis=0
    )
    own_video, meta, _ = lax.optimization_barrier((video, meta, mate))
    kv, own_q = project_own(own_video, gain, w)
    pair, other, kv = lax.optimization_barrier((pair, other, kv))
    three = jnp.stack([meta, from_pair(meta), from_other(meta)])
    off_meta, mate_meta = from_off(three), from_mate(three)
    off, off_meta, mate_meta, kv = lax.optimization_barrier((off, off_meta, mate_meta, kv))
    corners = from_pair(off), from_other(off)
    mates = mate, from_mate(pair), from_mate(other)
    rest = (pair, other, off, *mates)
    kv = project_near((pair, other, off, *mates), 6, gain, w, kv)
    kv = kv.reshape(BLOCKS * tw, tube, 2 * feats)

    meta = jnp.concatenate([three, off_meta[:1], mate_meta, off_meta[1:]])
    listed = (meta[:, :tw] - 1).reshape(9 * tw, nb)
    count_all = meta[:, tw, :tw]

    ids = neighbours.reshape(tw, nb)
    t_of, h_of, w_of = ids // (n_h * tw), ids // tw % n_h, ids % tw
    step = jnp.where(t_of == t_here, 0, jnp.where(t_of == t_here + 1 - 2 * (t_here % 2), 1, 2))
    slot = jnp.where(
        h_of == h_here,
        step,
        jnp.where(h_of == h_here + 1 - 2 * (h_here % 2), 4 + step, jnp.where(step == 0, 3, 6 + step)),
    )
    local = slot * tw + w_of
    own_ids = (t_here * n_h + h_here) * tw + jnp.arange(tw, dtype=jnp.int32)
    names = jnp.any(listed[None] == own_ids[:, None, None], axis=2)

    def listing(first, last, most):
        named = names[:, first:last]
        where = jnp.arange(last - first, dtype=jnp.int32)
        rank = jnp.sum(named[:, None, :] & (where[None, :] < where[:, None])[None], axis=2)
        hit = named[:, None, :] & (rank[:, None, :] == jnp.arange(most)[None, :, None])
        places = jnp.sum(jnp.where(hit, where, 0), axis=2).astype(jnp.int32)
        return jnp.concatenate([places, jnp.sum(named, axis=1, keepdims=True).astype(jnp.int32)], axis=1)

    near_list = listing(0, 7 * tw, 24)
    last_list = listing(7 * tw, 9 * tw, 8)
    sec = sec.reshape(1).astype(jnp.int32)
    own_counts = counts.reshape(tw)

    part, o, lse, p, far = attend_forward(local, count_all, *corners, gain, w, kv, own_q, w_out)
    other = lax.ppermute(part, "section", swap)
    part, videos = lax.optimization_barrier((part, (*rest, *corners)))
    far_q = project_queries(videos, gain, w).reshape(8 * tw, tube, feats)
    other, far_q, near_list, last_list = lax.optimization_barrier((other, far_q, near_list, last_list))
    pay, g = middle(own_counts, sec, part, other, video, target, w_out, o, lse)
    off, mate = from_off(pay), from_mate(pay)
    pair, after = from_pair(pay), from_other(pay)
    dq = query_grad(local, pay, kv, far, p)
    dq, off = lax.optimization_barrier((dq, off))
    near, mates, corners = (pay, pair, after, off), (mate, from_mate(pair), from_mate(after)), (from_pair(off), from_other(off))
    acc, base = key_near(
        near_list, own_counts, own_q.reshape(tw, tube, feats), far_q, kv, w, dq, [*near, *mates]
    )
    send, keep = key_last(6, last_list, own_counts, sec, far_q, kv, w, acc, corners, video, gain, base, g)
    got = lax.ppermute(send, "section", swap)
    return (keep + got.astype(F32)).astype(BF16).reshape(tt, th, tw, tube, width // 2)


def solution(mesh):
    in_specs = (
        P("tm", "height", None, None, None),
        P("tm", "height", None, None, None),
        P(),
        P(None, None, "section"),
        P("section", None),
        P("tm", "height", None, None),
        P("tm", "height", None),
    )
    out_specs = P("tm", "height", None, None, "section")
    return jax.shard_map(
        per_device, mesh=mesh, in_specs=in_specs, out_specs=out_specs, check_vma=False
    )
```

```python
import functools
import math

import jax
import jax.numpy as jnp
from jax import lax
from jax.experimental import pallas as pl
from jax.experimental.pallas import tpu as pltpu
from jax.sharding import PartitionSpec as P

HEAD_DIM = 80
SCALE = HEAD_DIM ** (-0.5)
LOG2_SCALE = SCALE * math.log2(math.e)
BF16 = jnp.bfloat16
F32 = jnp.float32
MIB = 1 << 20
GROUPS = ((0, 3, 0, 256), (3, 2, 128, 384), (5, 3, 384, 256))
NEAR_CHUNK, LAST_CHUNK = 8, 2
STAT_ROWS = 32
BLOCKS = 12
SMALL = pl.CostEstimate(flops=1, bytes_accessed=1, transcendentals=0)
VMEM_LIMIT = 52 * MIB

NT_DIMS = (((1,), (1,)), ((), ()))


def dot(a, b):
    return jnp.dot(a, b, preferred_element_type=F32)


def dot_nt(a, b):
    return lax.dot_general(a, b, NT_DIMS, preferred_element_type=F32)


def head_row(head, first_lane, lanes):
    lane = lax.broadcasted_iota(jnp.int32, (1, lanes), 1) + first_lane
    return jnp.where((lane >= head * HEAD_DIM) & (lane < (head + 1) * HEAD_DIM), 1.0, 0.0).astype(F32)


def spread(x, group):
    h0, nh, l0, wd = group
    out = []
    for h in range(h0, h0 + nh):
        mask = jnp.broadcast_to(head_row(h, l0, wd), (16, wd)).astype(BF16)
        out += [x[r : r + 16] * mask for r in range(0, x.shape[0], 16)]
    return jnp.concatenate(out, axis=0)


def gather_heads(y, group, rows):
    h0, nh, l0, wd = group
    total = y[:rows] * head_row(h0, l0, wd)
    for k in range(1, nh):
        total = total + y[k * rows : (k + 1) * rows] * head_row(h0 + k, l0, wd)
    return total


def add_group(ref, rows, value, group):
    h0, nh, l0, wd = group
    ref[rows, l0 : l0 + wd] = ref[rows, l0 : l0 + wd] + value


def gain_of(gain_ref):
    return gain_ref[...].reshape(1, -1)


def normalize(x):
    centred = x - jnp.mean(x, axis=-1, keepdims=True)
    inverse = lax.rsqrt(jnp.mean(centred * centred, axis=-1, keepdims=True) + 1e-06)
    return centred * inverse, inverse


def project_near_body(n, *refs):
    xs = refs[:n]
    gain_ref, w_ref = refs[n : n + 2]
    kv_ref, x_scr = refs[n + 3 :]
    rows = xs[0].shape[0]

    @pl.when(pl.program_id(0) == 0)
    def _():
        for k in range(n):
            x_scr[k * rows : (k + 1) * rows] = (normalize(xs[k][...].astype(F32))[0] * gain_of(gain_ref)).astype(BF16)

    kv_ref[...] = dot(x_scr[...], w_ref[...]).astype(BF16).reshape(kv_ref.shape)


def whole(a):
    return pl.BlockSpec(a.shape, lambda i: (0,) * a.ndim)


def project_near(blocks, first, gain, w, buf):
    n = len(blocks)
    rows, width = blocks[0].shape
    feats = w.shape[2]
    return pl.pallas_call(
        functools.partial(project_near_body, n),
        grid=(2,),
        in_specs=[whole(b) for b in blocks]
        + [whole(gain), pl.BlockSpec((pl.squeezed, width, feats), lambda i: (i + 1, 0, 0))]
        + [pl.BlockSpec(memory_space=pl.ANY)],
        out_specs=pl.BlockSpec((n, rows, feats), lambda i: (first // n, 0, i)),
        out_shape=jax.ShapeDtypeStruct(buf.shape, BF16),
        scratch_shapes=[pltpu.VMEM((n * rows, width), BF16)],
        input_output_aliases={n + 2: 0},
        compiler_params=pltpu.CompilerParams(vmem_limit_bytes=VMEM_LIMIT),
        cost_estimate=SMALL,
        name="project_near",
    )(*blocks, gain, w, buf)


def project_own_body(x_ref, gain_ref, w_ref, kv_ref, q_ref, x_scr):
    step = pl.program_id(0)

    @pl.when(step == 0)
    def _():
        x_scr[...] = (normalize(x_ref[...].astype(F32))[0] * gain_of(gain_ref)).astype(BF16)

    @pl.when(step < 2)
    def _():
        kv_ref[0] = dot(x_scr[...], w_ref[...]).astype(BF16)

    @pl.when(step == 2)
    def _():
        q_ref[...] = dot(x_scr[...], w_ref[...]).astype(BF16)


def project_own(x, gain, w):
    rows, width = x.shape
    feats = w.shape[2]
    return pl.pallas_call(
        project_own_body,
        grid=(3,),
        in_specs=[whole(x), whole(gain), pl.BlockSpec((pl.squeezed, width, feats), lambda i: ((i + 1) % 3, 0, 0))],
        out_specs=[
            pl.BlockSpec((1, rows, feats), lambda i: (0, 0, jnp.minimum(i, 1))),
            pl.BlockSpec((rows, feats), lambda i: (0, 0)),
        ],
        out_shape=[
            jax.ShapeDtypeStruct((BLOCKS, rows, 2 * feats), BF16),
            jax.ShapeDtypeStruct((rows, feats), BF16),
        ],
        scratch_shapes=[pltpu.VMEM((rows, width), BF16)],
        compiler_params=pltpu.CompilerParams(vmem_limit_bytes=VMEM_LIMIT),
        cost_estimate=SMALL,
        name="project_own",
    )(x, gain, w)


def project_queries_body(n, *refs):
    xs = refs[:n]
    gain_ref, w_ref, out_ref, x_scr = refs[n:]
    step = pl.program_id(0)
    for k in range(n):

        @pl.when(step == k)
        def _():
            x_scr[...] = xs[k][...]

    normed = (normalize(x_scr[...].astype(F32))[0] * gain_of(gain_ref)).astype(BF16)
    out_ref[0] = dot(normed, w_ref[...]).astype(BF16)


def project_queries(blocks, gain, w):
    n = len(blocks)
    rows, width = blocks[0].shape
    feats = w.shape[2]
    return pl.pallas_call(
        functools.partial(project_queries_body, n),
        grid=(n,),
        in_specs=[whole(b) for b in blocks] + [whole(gain), pl.BlockSpec((pl.squeezed, width, feats), lambda i: (0, 0, 0))],
        out_specs=pl.BlockSpec((1, rows, feats), lambda i: (i, 0, 0)),
        out_shape=jax.ShapeDtypeStruct((n, rows, feats), BF16),
        scratch_shapes=[pltpu.VMEM((rows, width), BF16)],
        compiler_params=pltpu.CompilerParams(vmem_limit_bytes=VMEM_LIMIT),
        cost_estimate=SMALL,
        name="project_queries",
    )(*blocks, gain, w)


def lay_out_keys(local_ref, all_scr, kv_scr, i):
    nb = kv_scr.shape[1] // 64
    for n in range(nb):
        kv_scr[i, n * 64 : (n + 1) * 64, :] = all_scr[local_ref[i, n]]


def forward_body(
    local_ref, count_ref, x0_ref, x1_ref, gain_ref, w_ref, kv_ref, q_ref, w_out_ref,
    part_ref, o_ref, lse_ref, p_ref, far_ref,
    n_scr, w_scr, wo_scr, q_scr, all_scr, kv_scr, p_scr, sem, p_sem,
):
    tubes, keys, feats2 = kv_scr.shape
    feats = feats2 // 2
    nb = keys // 64
    rows = tubes * 64
    copies = [
        pltpu.make_async_copy(w_ref.at[1], w_scr.at[0], sem.at[2]),
        pltpu.make_async_copy(w_ref.at[2], w_scr.at[1], sem.at[3]),
        pltpu.make_async_copy(q_ref, q_scr, sem.at[4]),
        pltpu.make_async_copy(w_out_ref, wo_scr, sem.at[5]),
        pltpu.make_async_copy(kv_ref.at[:tubes], all_scr.at[:tubes], sem.at[6]),
        pltpu.make_async_copy(kv_ref.at[6 * tubes :], all_scr.at[tubes : 7 * tubes], sem.at[7]),
    ]
    for k in (0, 1, 4, 5, 2, 3):
        copies[k].start()
    for k, x_ref in enumerate((x0_ref, x1_ref)):
        n_scr[k * rows : (k + 1) * rows] = (normalize(x_ref[...].astype(F32))[0] * gain_of(gain_ref)).astype(BF16)
    for k in range(2):
        copies[k].wait()
        out = dot(n_scr[...], w_scr[k]).astype(BF16).reshape(2 * tubes, 64, feats)
        all_scr[7 * tubes :, :, k * feats : (k + 1) * feats] = out
    far_copy = pltpu.make_async_copy(all_scr.at[7 * tubes :], far_ref, sem.at[8])
    far_copy.start()
    for k in (4, 5, 2):
        copies[k].wait()
    lane = lax.broadcasted_iota(jnp.int32, (1, keys), 1)
    slot, place = lane // 64, lane % 64
    pick = lax.broadcasted_iota(jnp.int32, (64, 128), 0) == lax.broadcasted_iota(jnp.int32, (64, 128), 1) % 64
    o_ref[...] = jnp.zeros_like(o_ref)

    def tube(i):
        limit = jnp.zeros((1, keys), jnp.int32)
        for n in range(nb):
            limit = jnp.where(slot == n, count_ref[local_ref[i, n] // tubes, local_ref[i, n] % tubes], limit)
        live = place < limit
        here = slice(i * 64, (i + 1) * 64)
        lay_out_keys(local_ref, all_scr, kv_scr, i)
        for group in GROUPS:
            h0, nh, l0, wd = group
            window = slice(l0, l0 + wd)
            q = spread(q_scr[here, window], group)
            s = dot_nt(q, kv_scr[i, :, window]) * LOG2_SCALE
            s = jnp.where(live, s, -1e30)
            top = jnp.max(s, axis=-1, keepdims=True)
            e = jnp.exp2(s - top)
            total = jnp.sum(e, axis=-1, keepdims=True)
            p = (e * (1.0 / total)).astype(BF16)
            p_scr[i, h0 * 64 : (h0 + nh) * 64, :] = p
            o = dot(p, kv_scr[i, :, feats + l0 : feats + l0 + wd])
            o_ref[here, window] += gather_heads(o, group, 64)
            lse = top + jnp.log2(total)
            for k in range(nh):
                column = jnp.broadcast_to(lse[k * 64 : (k + 1) * 64], (64, 128))
                lse_ref[i, h0 + k : h0 + k + 1, :] = jnp.sum(jnp.where(pick, column, 0.0), axis=0, keepdims=True)
        pltpu.make_async_copy(p_scr.at[i], p_ref.at[i], p_sem.at[i]).start()

    for i in range(tubes):
        tube(i)
    copies[3].wait()
    part_ref[...] = dot(o_ref[...].astype(BF16), wo_scr[...]).astype(BF16)
    far_copy.wait()
    for i in range(tubes):
        pltpu.make_async_copy(p_scr.at[i], p_ref.at[i], p_sem.at[i]).wait()


def attend_forward(local, counts, x0, x1, gain, w, kv, q, w_out):
    rows, feats = q.shape
    tubes = rows // 64
    keys = local.shape[1] * 64
    heads = feats // HEAD_DIM
    width = w_out.shape[1]
    vmem = pl.BlockSpec(memory_space=pltpu.VMEM)
    smem = pl.BlockSpec(memory_space=pltpu.SMEM)
    hbm = pl.BlockSpec(memory_space=pl.ANY)
    return pl.pallas_call(
        forward_body,
        in_specs=[smem, smem, vmem, vmem, vmem, hbm, hbm, hbm, hbm],
        out_specs=[vmem, vmem, vmem, hbm, hbm],
        out_shape=[
            jax.ShapeDtypeStruct((rows, width), BF16),
            jax.ShapeDtypeStruct((rows, feats), F32),
            jax.ShapeDtypeStruct((tubes, heads, 128), F32),
            jax.ShapeDtypeStruct((tubes, heads * 64, keys), BF16),
            jax.ShapeDtypeStruct((2 * tubes, 64, 2 * feats), BF16),
        ],
        scratch_shapes=[
            pltpu.VMEM((2 * rows, width), BF16),
            pltpu.VMEM((2, width, feats), BF16),
            pltpu.VMEM((feats, width), BF16),
            pltpu.VMEM((rows, feats), BF16),
            pltpu.VMEM((9 * tubes, 64, 2 * feats), BF16),
            pltpu.VMEM((tubes, keys, 2 * feats), BF16),
            pltpu.VMEM((tubes, heads * 64, keys), BF16),
            pltpu.SemaphoreType.DMA((9,)),
            pltpu.SemaphoreType.DMA((tubes,)),
        ],
        compiler_params=pltpu.CompilerParams(vmem_limit_bytes=VMEM_LIMIT),
        cost_estimate=SMALL,
        name="attend_forward",
    )(local, counts, x0, x1, gain, w, kv, q, w_out)


def parts_of(x, n):
    out = []
    for _ in range(n):
        piece = x.astype(BF16)
        out.append(piece)
        x = x - piece.astype(F32)
    return out


def middle_body(
    count_ref, sec_ref, mine_hbm, other_ref, video_hbm, target_hbm, w_out_hbm, o_hbm, lse_ref, pay_ref, g_ref,
    mine_ref, video_ref, target_ref, w_out_ref, o_ref, sem,
):
    rows, width = video_ref.shape
    feats = w_out_ref.shape[0]
    pairs = [
        (mine_hbm, mine_ref),
        (video_hbm, video_ref),
        (target_hbm, target_ref),
        (w_out_hbm, w_out_ref),
        (o_hbm, o_ref),
    ]
    copies = [pltpu.make_async_copy(*pair, sem.at[k]) for k, pair in enumerate(pairs)]
    for c in copies:
        c.start()
    heads = feats // HEAD_DIM
    tubes = rows // 64
    row = lax.broadcasted_iota(jnp.int32, (rows, 1), 0)
    limit = jnp.zeros((rows, 1), jnp.int32)
    for i in range(tubes):
        limit = jnp.where(row // 64 == i, count_ref[i], limit)
    valid = row % 64 < limit
    for c in copies[:3]:
        c.wait()
    mixed = mine_ref[...].astype(F32) + other_ref[...].astype(F32)
    g = jnp.where(valid, 2.0 * (video_ref[...].astype(F32) + mixed - target_ref[...].astype(F32)), 0.0)
    half = width // 2
    g_ref[...] = jnp.where(sec_ref[0] == 0, g[:, :half], g[:, half:])
    copies[3].wait()
    d_att = dot_nt(g.astype(BF16), w_out_ref[...]).astype(BF16)
    copies[4].wait()
    pay_ref[:rows] = d_att
    prod = d_att.astype(F32) * o_ref[...]
    head = lax.broadcasted_iota(jnp.int32, (heads, feats), 0)
    lane = lax.broadcasted_iota(jnp.int32, (heads, feats), 1)
    ones = ((lane >= head * HEAD_DIM) & (lane < (head + 1) * HEAD_DIM)).astype(F32)
    inner = []
    for i in range(tubes):
        one = prod[i * 64 : (i + 1) * 64]
        inner.append(
            lax.dot_general(
                ones,
                jnp.concatenate([one, one], axis=0),
                NT_DIMS,
                precision=lax.Precision.HIGHEST,
                preferred_element_type=F32,
            )
        )
    inner = jnp.concatenate(inner, axis=0)
    lse = lse_ref[...].reshape(tubes * heads, 128)
    for k, piece in enumerate(parts_of(lse, 3) + parts_of(inner, 2)):
        pay_ref[rows:, k * 128 : (k + 1) * 128] = piece


def middle(counts, sec, mine, other, video, target, w_out, o, lse):
    rows, width = video.shape
    feats = w_out.shape[0]
    vmem = pl.BlockSpec(memory_space=pltpu.VMEM)
    smem = pl.BlockSpec(memory_space=pltpu.SMEM)
    return pl.pallas_call(
        middle_body,
        in_specs=[smem, smem] + [pl.BlockSpec(memory_space=pl.ANY), vmem] + [pl.BlockSpec(memory_space=pl.ANY)] * 4 + [vmem],
        out_specs=[vmem, vmem],
        out_shape=[
            jax.ShapeDtypeStruct((rows + STAT_ROWS, feats), BF16),
            jax.ShapeDtypeStruct((rows, width // 2), F32),
        ],
        scratch_shapes=[pltpu.VMEM((rows, width), BF16)] * 3
        + [pltpu.VMEM((feats, width), BF16), pltpu.VMEM((rows, feats), F32), pltpu.SemaphoreType.DMA((5,))],
        compiler_params=pltpu.CompilerParams(vmem_limit_bytes=VMEM_LIMIT),
        cost_estimate=SMALL,
        name="middle",
    )(counts, sec, mine, other, video, target, w_out, o, lse)


def key_pass(
    list_ref, count_ref, q_scr, kv_scr, pay_scr, lse_scr, inner_scr, qc_scr, dc_scr, km_scr, vm_scr, dk_scr, dv_scr, grad_scr
):
    tubes = kv_scr.shape[0]
    size = qc_scr.shape[0] // 64
    feats = q_scr.shape[2]
    most = list_ref.shape[1] - 1
    low = lax.broadcasted_iota(jnp.int32, (8, 128), 1) < 64
    key_row = lax.broadcasted_iota(jnp.int32, (64, 1), 0)

    def tube(j, carry):
        alive = key_row < count_ref[j]
        block = pl.ds(pl.multiple_of(j * 64, 64), 64)
        for group in GROUPS:
            h0, nh, l0, wd = group
            these = slice(h0 * 64, (h0 + nh) * 64)
            km_scr[these, :wd] = spread(kv_scr[j, :, l0 : l0 + wd], group)
            vm_scr[these, :wd] = spread(kv_scr[j, :, feats + l0 : feats + l0 + wd], group)
        dk_scr[...] = jnp.zeros_like(dk_scr)
        dv_scr[...] = jnp.zeros_like(dv_scr)

        def chunk(c, carry):
            lses, inners = [], []
            for t in range(size):
                place = c * size + t
                i = list_ref[j, jnp.minimum(place, most - 1)]
                slot, w = i // tubes, i % tubes
                qc_scr[t * 64 : (t + 1) * 64, :] = q_scr[i]
                dc_scr[t * 64 : (t + 1) * 64, :] = pay_scr[slot, pl.ds(pl.multiple_of(w * 64, 64), 64), :]
                lses.append(jnp.where(place < list_ref[j, most], lse_scr[i], 1e30))
                inners.append(inner_scr[i])
            lse = jnp.concatenate([jnp.where(low, lses[t], lses[t + 1]) for t in range(0, size, 2)], axis=1)
            inner = jnp.concatenate([jnp.where(low, inners[t], inners[t + 1]) for t in range(0, size, 2)], axis=1)
            for group in GROUPS:
                h0, nh, l0, wd = group
                window = slice(l0, l0 + wd)
                these = slice(h0 * 64, (h0 + nh) * 64)
                qc, dc = qc_scr[:, window], dc_scr[:, window]
                s = dot_nt(km_scr[these, :wd], qc)
                d_prob = dot_nt(vm_scr[these, :wd], dc)
                p, d_score = [], []
                for m in range(nh):
                    part = slice(m * 64, (m + 1) * 64)
                    head = slice(h0 + m, h0 + m + 1)
                    one = jnp.where(alive, jnp.exp2(s[part] * LOG2_SCALE - lse[head]), 0.0)
                    p.append(one.astype(BF16))
                    d_score.append((one * (d_prob[part] - inner[head])).astype(BF16))
                dk_scr[these, :wd] += dot(jnp.concatenate(d_score, axis=0), qc)
                dv_scr[these, :wd] += dot(jnp.concatenate(p, axis=0), dc)
            return carry

        lax.fori_loop(0, (list_ref[j, most] + size - 1) // size, chunk, carry)
        for group in GROUPS:
            h0, nh, l0, wd = group
            these = slice(h0 * 64, (h0 + nh) * 64)
            grad_scr[block, l0 : l0 + wd] += gather_heads(dk_scr[these, :wd], group, 64) * SCALE
            grad_scr[block, feats + l0 : feats + l0 + wd] += gather_heads(dv_scr[these, :wd], group, 64)
        return carry

    lax.fori_loop(0, tubes, tube, 0)


def stats_of(pay_scr, k, rows, tubes, lse_scr, inner_scr):
    parts = [pay_scr[k, rows:, j * 128 : (j + 1) * 128].astype(F32) for j in range(5)]
    lse_scr[k * tubes : (k + 1) * tubes] = (parts[0] + parts[1] + parts[2]).reshape(tubes, -1, 128)
    inner_scr[k * tubes : (k + 1) * tubes] = (parts[3] + parts[4]).reshape(tubes, -1, 128)


def query_body(local_ref, pay_ref, kv_ref, far_ref, p_ref, dq_ref, all_scr, kv_scr, p_scr, pay_scr, dq_scr, sem, p_sem):
    tubes, keys, feats2 = kv_scr.shape
    feats = feats2 // 2
    pay_copy = pltpu.make_async_copy(pay_ref, pay_scr, sem.at[0])
    p_copies = [pltpu.make_async_copy(p_ref.at[i], p_scr.at[i], p_sem.at[i]) for i in range(tubes)]
    copies = [
        pltpu.make_async_copy(kv_ref.at[:tubes], all_scr.at[:tubes], sem.at[1]),
        pltpu.make_async_copy(kv_ref.at[6 * tubes :], all_scr.at[tubes : 7 * tubes], sem.at[2]),
        pltpu.make_async_copy(far_ref, all_scr.at[7 * tubes :], sem.at[3]),
    ]
    for c in copies + [pay_copy] + p_copies:
        c.start()
    for c in copies:
        c.wait()
    dq_scr[...] = jnp.zeros_like(dq_scr)
    pay_copy.wait()
    for i in range(tubes):
        here = slice(i * 64, (i + 1) * 64)
        lay_out_keys(local_ref, all_scr, kv_scr, i)
        p_copies[i].wait()
        for group in GROUPS:
            h0, nh, l0, wd = group
            window = slice(l0, l0 + wd)
            d_att = spread(pay_scr[here, window], group)
            d_prob = dot_nt(d_att, kv_scr[i, :, feats + l0 : feats + l0 + wd])
            p = p_scr[i, h0 * 64 : (h0 + nh) * 64, :].astype(F32)
            inner = jnp.sum(d_prob * p, axis=-1, keepdims=True)
            d_score = (p * (d_prob - inner)).astype(BF16)
            dq_scr[here, window] += gather_heads(dot(d_score, kv_scr[i, :, window]), group, 64)
    dq_ref[...] = (dq_scr[...] * SCALE).astype(BF16)


def query_grad(local, pay, kv, far, p):
    feats = pay.shape[1]
    tubes, _, keys = p.shape
    vmem = pl.BlockSpec(memory_space=pltpu.VMEM)
    smem = pl.BlockSpec(memory_space=pltpu.SMEM)
    hbm = pl.BlockSpec(memory_space=pl.ANY)
    return pl.pallas_call(
        query_body,
        in_specs=[smem] + [hbm] * 4,
        out_specs=vmem,
        out_shape=jax.ShapeDtypeStruct((tubes * 64, feats), BF16),
        scratch_shapes=[
            pltpu.VMEM((9 * tubes, 64, 2 * feats), BF16),
            pltpu.VMEM((tubes, keys, 2 * feats), BF16),
            pltpu.VMEM(p.shape, BF16),
            pltpu.VMEM(pay.shape, BF16),
            pltpu.VMEM((tubes * 64, feats), F32),
            pltpu.SemaphoreType.DMA((4,)),
            pltpu.SemaphoreType.DMA((tubes,)),
        ],
        compiler_params=pltpu.CompilerParams(vmem_limit_bytes=VMEM_LIMIT),
        cost_estimate=SMALL,
        name="query_grad",
    )(local, pay, kv, far, p)


def key_near_body(n, list_ref, count_ref, own_q_ref, q_ref, kv_ref, w_ref, dq_ref, *rest):
    pays = rest[:n]
    grad_ref, base_ref, w_scr, dq_scr, q_scr, kv_scr, pay_scr, *scr, sem = rest[n:]
    lse_scr, inner_scr = scr[:2]
    tubes = kv_scr.shape[0]
    rows = tubes * 64
    pay_copies = [pltpu.make_async_copy(pays[k], pay_scr.at[k], sem.at[k]) for k in range(n)]
    first = [
        pltpu.make_async_copy(dq_ref, dq_scr, sem.at[n + 4]),
        pltpu.make_async_copy(w_ref.at[0], w_scr, sem.at[n]),
    ]
    copies = [
        pltpu.make_async_copy(own_q_ref, q_scr.at[:tubes], sem.at[n + 1]),
        pltpu.make_async_copy(q_ref.at[: (n - 1) * tubes], q_scr.at[tubes:], sem.at[n + 2]),
        pltpu.make_async_copy(kv_ref.at[:tubes], kv_scr, sem.at[n + 3]),
    ]
    for c in first + pay_copies + copies:
        c.start()
    grad_ref[...] = jnp.zeros_like(grad_ref)
    for c in first:
        c.wait()
    base_ref[...] = dot_nt(dq_scr[...], w_scr[...])
    for k in range(n):
        pay_copies[k].wait()
        stats_of(pay_scr, k, rows, tubes, lse_scr, inner_scr)
    for c in copies:
        c.wait()
    key_pass(list_ref, count_ref, q_scr, kv_scr, pay_scr, *scr, grad_ref)


def key_scratch(n, tubes, feats, size):
    rows = tubes * 64
    heads = feats // HEAD_DIM
    return [
        pltpu.VMEM((n * tubes, 64, feats), BF16),
        pltpu.VMEM((tubes, 64, 2 * feats), BF16),
        pltpu.VMEM((n, rows + STAT_ROWS, feats), BF16),
        pltpu.VMEM((n * tubes, heads, 128), F32),
        pltpu.VMEM((n * tubes, heads, 128), F32),
        pltpu.VMEM((size * 64, feats), BF16),
        pltpu.VMEM((size * 64, feats), BF16),
        pltpu.VMEM((heads * 64, 384), BF16),
        pltpu.VMEM((heads * 64, 384), BF16),
        pltpu.VMEM((heads * 64, 384), F32),
        pltpu.VMEM((heads * 64, 384), F32),
    ]


def key_near(lists, counts, own_q, q, kv, w, dq, pays):
    rows, feats = dq.shape
    width = w.shape[1]
    tubes = rows // 64
    n = len(pays)
    vmem = pl.BlockSpec(memory_space=pltpu.VMEM)
    smem = pl.BlockSpec(memory_space=pltpu.SMEM)
    hbm = pl.BlockSpec(memory_space=pl.ANY)
    return pl.pallas_call(
        functools.partial(key_near_body, n),
        in_specs=[smem] * 2 + [hbm] * 5 + [vmem] * n,
        out_specs=[vmem, vmem],
        out_shape=[
            jax.ShapeDtypeStruct((rows, 2 * feats), F32),
            jax.ShapeDtypeStruct((rows, width), F32),
        ],
        scratch_shapes=[pltpu.VMEM((width, feats), BF16), pltpu.VMEM((rows, feats), BF16)]
        + key_scratch(n, tubes, feats, NEAR_CHUNK)
        + [pltpu.SemaphoreType.DMA((n + 5,))],
        compiler_params=pltpu.CompilerParams(vmem_limit_bytes=VMEM_LIMIT),
        cost_estimate=SMALL,
        name="key_near",
    )(lists, counts, own_q, q, kv, w, dq, *pays)


def key_last_body(n, first, list_ref, count_ref, sec_ref, q_ref, kv_ref, w_ref, acc_ref, *rest):
    pays = rest[:n]
    video_ref, gain_ref, base_ref, g_ref, send_ref, keep_ref = rest[n : n + 6]
    q_scr, kv_scr, pay_scr, *scr, w_scr, grad_scr, x_scr, base_scr, g_scr, sem = rest[n + 6 :]
    lse_scr, inner_scr = scr[:2]
    tubes = kv_scr.shape[0]
    rows = tubes * 64
    feats = q_scr.shape[2]
    q_copy = pltpu.make_async_copy(q_ref.at[first * tubes : (first + n) * tubes], q_scr, sem.at[0])
    kv_copy = pltpu.make_async_copy(kv_ref.at[:tubes], kv_scr, sem.at[1])
    acc_copy = pltpu.make_async_copy(acc_ref, grad_scr, sem.at[2])
    w_copy = pltpu.make_async_copy(w_ref.at[1:], w_scr, sem.at[3])
    x_copy = pltpu.make_async_copy(video_ref, x_scr, sem.at[4])
    base_copy = pltpu.make_async_copy(base_ref, base_scr, sem.at[5])
    g_copy = pltpu.make_async_copy(g_ref, g_scr, sem.at[6])
    pay_copies = [pltpu.make_async_copy(pays[k], pay_scr.at[k], sem.at[7 + k]) for k in range(n)]
    for c in pay_copies + [q_copy, kv_copy, acc_copy, w_copy, x_copy, base_copy, g_copy]:
        c.start()
    for k, c in enumerate(pay_copies):
        c.wait()
        stats_of(pay_scr, k, rows, tubes, lse_scr, inner_scr)
    q_copy.wait()
    kv_copy.wait()
    acc_copy.wait()
    key_pass(list_ref, count_ref, q_scr, kv_scr, pay_scr, *scr, grad_scr)
    d_proj = grad_scr[...].astype(BF16)
    x_copy.wait()
    xhat, inverse = normalize(x_scr[...].astype(F32))
    w_copy.wait()
    base_copy.wait()
    g_copy.wait()
    d_normed = base_scr[...] + dot_nt(d_proj[:, :feats], w_scr[0]) + dot_nt(d_proj[:, feats:], w_scr[1])
    scaled = d_normed * gain_of(gain_ref)
    out = (
        scaled
        - jnp.mean(scaled, axis=-1, keepdims=True)
        - xhat * jnp.mean(scaled * xhat, axis=-1, keepdims=True)
    ) * inverse
    half = out.shape[1] // 2
    lower = sec_ref[0] == 0
    send_ref[...] = jnp.where(lower, out[:, half:], out[:, :half]).astype(BF16)
    keep_ref[...] = jnp.where(lower, out[:, :half], out[:, half:]) + g_scr[...]


def key_last(first, lists, counts, sec, q, kv, w, acc, pays, video, gain, base, g):
    rows, width = video.shape
    feats = q.shape[2]
    tubes = rows // 64
    n = len(pays)
    vmem = pl.BlockSpec(memory_space=pltpu.VMEM)
    smem = pl.BlockSpec(memory_space=pltpu.SMEM)
    hbm = pl.BlockSpec(memory_space=pl.ANY)
    return pl.pallas_call(
        functools.partial(key_last_body, n, first),
        in_specs=[smem] * 3 + [hbm] * 4 + [vmem] * n + [hbm] + [vmem] + [hbm] * 2,
        out_specs=[vmem, vmem],
        out_shape=[
            jax.ShapeDtypeStruct((rows, width // 2), BF16),
            jax.ShapeDtypeStruct((rows, width // 2), F32),
        ],
        scratch_shapes=key_scratch(n, tubes, feats, LAST_CHUNK)
        + [
            pltpu.VMEM((2, width, feats), BF16),
            pltpu.VMEM((rows, 2 * feats), F32),
            pltpu.VMEM((rows, width), BF16),
            pltpu.VMEM((rows, width), F32),
            pltpu.VMEM((rows, width // 2), F32),
            pltpu.SemaphoreType.DMA((7 + n,)),
        ],
        compiler_params=pltpu.CompilerParams(vmem_limit_bytes=VMEM_LIMIT),
        cost_estimate=SMALL,
        name="key_last",
    )(lists, counts, sec, q, kv, w, acc, *pays, video, gain, base, g)


def per_device(video, target, gain, w_qkv, w_out, neighbours, counts):
    tt, th, tw, tube, width = video.shape
    feats = w_qkv.shape[2]
    nb = neighbours.shape[3]
    rows = tt * th * tw * tube
    n_t, n_h = lax.axis_size("tm"), lax.axis_size("height")
    t_here, h_here, sec = lax.axis_index("tm"), lax.axis_index("height"), lax.axis_index("section")
    off_chip = [p for h in range(1, n_h - 1, 2) for p in ((h, h + 1), (h + 1, h))]
    on_chip = [(h, h ^ 1) for h in range(n_h)]
    pair_times = [(t, t ^ 1) for t in range(n_t)]
    other_times = [p for t in range(1, n_t - 1, 2) for p in ((t, t + 1), (t + 1, t))]
    swap = [(0, 1), (1, 0)]

    def from_pair(x):
        return lax.ppermute(x, "tm", pair_times)

    def from_other(x):
        return lax.ppermute(x, "tm", other_times)

    def from_off(x):
        return lax.ppermute(x, "height", off_chip)

    def from_mate(x):
        return lax.ppermute(x, "height", on_chip)

    video = video.reshape(rows, width)
    target = target.reshape(rows, width)
    w = jnp.transpose(w_qkv, (1, 0, 2))

    off, mate, pair, other = from_off(video), from_mate(video), from_pair(video), from_other(video)
    meta = jnp.concatenate(
        [neighbours.reshape(tw, nb) + 1, jnp.pad(counts.reshape(1, tw), ((0, 0), (0, nb - tw)))], axis=0
    )
    own_video, meta, _ = lax.optimization_barrier((video, meta, mate))
    kv, own_q = project_own(own_video, gain, w)
    pair, other, kv = lax.optimization_barrier((pair, other, kv))
    three = jnp.stack([meta, from_pair(meta), from_other(meta)])
    off_meta, mate_meta = from_off(three), from_mate(three)
    off, off_meta, mate_meta, kv = lax.optimization_barrier((off, off_meta, mate_meta, kv))
    corners = from_pair(off), from_other(off)
    mates = mate, from_mate(pair), from_mate(other)
    rest = (pair, other, off, *mates)
    kv = project_near((pair, other, off, *mates), 6, gain, w, kv)
    kv = kv.reshape(BLOCKS * tw, tube, 2 * feats)

    meta = jnp.concatenate([three, off_meta[:1], mate_meta, off_meta[1:]])
    listed = (meta[:, :tw] - 1).reshape(9 * tw, nb)
    count_all = meta[:, tw, :tw]

    ids = neighbours.reshape(tw, nb)
    t_of, h_of, w_of = ids // (n_h * tw), ids // tw % n_h, ids % tw
    step = jnp.where(t_of == t_here, 0, jnp.where(t_of == t_here + 1 - 2 * (t_here % 2), 1, 2))
    slot = jnp.where(
        h_of == h_here,
        step,
        jnp.where(h_of == h_here + 1 - 2 * (h_here % 2), 4 + step, jnp.where(step == 0, 3, 6 + step)),
    )
    local = slot * tw + w_of
    own_ids = (t_here * n_h + h_here) * tw + jnp.arange(tw, dtype=jnp.int32)
    names = jnp.any(listed[None] == own_ids[:, None, None], axis=2)

    def listing(first, last, most):
        named = names[:, first:last]
        where = jnp.arange(last - first, dtype=jnp.int32)
        rank = jnp.sum(named[:, None, :] & (where[None, :] < where[:, None])[None], axis=2)
        hit = named[:, None, :] & (rank[:, None, :] == jnp.arange(most)[None, :, None])
        places = jnp.sum(jnp.where(hit, where, 0), axis=2).astype(jnp.int32)
        return jnp.concatenate([places, jnp.sum(named, axis=1, keepdims=True).astype(jnp.int32)], axis=1)

    near_list = listing(0, 7 * tw, 24)
    last_list = listing(7 * tw, 9 * tw, 8)
    sec = sec.reshape(1).astype(jnp.int32)
    own_counts = counts.reshape(tw)

    part, o, lse, p, far = attend_forward(local, count_all, *corners, gain, w, kv, own_q, w_out)
    other = lax.ppermute(part, "section", swap)
    part, videos = lax.optimization_barrier((part, (*rest, *corners)))
    far_q = project_queries(videos, gain, w).reshape(8 * tw, tube, feats)
    other, far_q, near_list, last_list = lax.optimization_barrier((other, far_q, near_list, last_list))
    pay, g = middle(own_counts, sec, part, other, video, target, w_out, o, lse)
    off, mate = from_off(pay), from_mate(pay)
    pair, after = from_pair(pay), from_other(pay)
    dq = query_grad(local, pay, kv, far, p)
    dq, off, pair, after = lax.optimization_barrier((dq, off, pair, after))
    near, mates, corners = (pay, pair, after, off), (mate, from_mate(pair), from_mate(after)), (from_pair(off), from_other(off))
    acc, base = key_near(
        near_list, own_counts, own_q.reshape(tw, tube, feats), far_q, kv, w, dq, [*near, *mates]
    )
    send, keep = key_last(6, last_list, own_counts, sec, far_q, kv, w, acc, corners, video, gain, base, g)
    got = lax.ppermute(send, "section", swap)
    return (keep + got.astype(F32)).astype(BF16).reshape(tt, th, tw, tube, width // 2)


def solution(mesh):
    in_specs = (
        P("tm", "height", None, None, None),
        P("tm", "height", None, None, None),
        P(),
        P(None, None, "section"),
        P("section", None),
        P("tm", "height", None, None),
        P("tm", "height", None),
    )
    out_specs = P("tm", "height", None, None, "section")
    return jax.shard_map(
        per_device, mesh=mesh, in_specs=in_specs, out_specs=out_specs, check_vma=False
    )
```

```python
import functools
import math

import jax
import jax.numpy as jnp
from jax import lax
from jax.experimental import pallas as pl
from jax.experimental.pallas import tpu as pltpu
from jax.sharding import PartitionSpec as P

HEAD_DIM = 80
SCALE = HEAD_DIM ** (-0.5)
LOG2_SCALE = SCALE * math.log2(math.e)
BF16 = jnp.bfloat16
F32 = jnp.float32
MIB = 1 << 20
GROUPS = ((0, 3, 0, 256), (3, 2, 128, 384), (5, 3, 384, 256))
NEAR_CHUNK, LAST_CHUNK = 8, 2
STAT_ROWS = 32
BLOCKS = 12
SMALL = pl.CostEstimate(flops=1, bytes_accessed=1, transcendentals=0)
VMEM_LIMIT = 52 * MIB

NT_DIMS = (((1,), (1,)), ((), ()))


def dot(a, b):
    return jnp.dot(a, b, preferred_element_type=F32)


def dot_nt(a, b):
    return lax.dot_general(a, b, NT_DIMS, preferred_element_type=F32)


def head_row(head, first_lane, lanes):
    lane = lax.broadcasted_iota(jnp.int32, (1, lanes), 1) + first_lane
    return jnp.where((lane >= head * HEAD_DIM) & (lane < (head + 1) * HEAD_DIM), 1.0, 0.0).astype(F32)


def spread(x, group):
    h0, nh, l0, wd = group
    out = []
    for h in range(h0, h0 + nh):
        mask = jnp.broadcast_to(head_row(h, l0, wd), (16, wd)).astype(BF16)
        out += [x[r : r + 16] * mask for r in range(0, x.shape[0], 16)]
    return jnp.concatenate(out, axis=0)


def gather_heads(y, group, rows):
    h0, nh, l0, wd = group
    total = y[:rows] * head_row(h0, l0, wd)
    for k in range(1, nh):
        total = total + y[k * rows : (k + 1) * rows] * head_row(h0 + k, l0, wd)
    return total


def add_group(ref, rows, value, group):
    h0, nh, l0, wd = group
    ref[rows, l0 : l0 + wd] = ref[rows, l0 : l0 + wd] + value


def gain_of(gain_ref):
    return gain_ref[...].reshape(1, -1)


def normalize(x):
    centred = x - jnp.mean(x, axis=-1, keepdims=True)
    inverse = lax.rsqrt(jnp.mean(centred * centred, axis=-1, keepdims=True) + 1e-06)
    return centred * inverse, inverse


def project_near_body(n, *refs):
    xs = refs[:n]
    gain_ref, w_ref = refs[n : n + 2]
    kv_ref, x_scr = refs[n + 3 :]
    rows = xs[0].shape[0]

    @pl.when(pl.program_id(0) == 0)
    def _():
        for k in range(n):
            x_scr[k * rows : (k + 1) * rows] = (normalize(xs[k][...].astype(F32))[0] * gain_of(gain_ref)).astype(BF16)

    kv_ref[...] = dot(x_scr[...], w_ref[...]).astype(BF16).reshape(kv_ref.shape)


def whole(a):
    return pl.BlockSpec(a.shape, lambda i: (0,) * a.ndim)


def project_near(blocks, first, gain, w, buf):
    n = len(blocks)
    rows, width = blocks[0].shape
    feats = w.shape[2]
    return pl.pallas_call(
        functools.partial(project_near_body, n),
        grid=(2,),
        in_specs=[whole(b) for b in blocks]
        + [whole(gain), pl.BlockSpec((pl.squeezed, width, feats), lambda i: (i + 1, 0, 0))]
        + [pl.BlockSpec(memory_space=pl.ANY)],
        out_specs=pl.BlockSpec((n, rows, feats), lambda i: (first // n, 0, i)),
        out_shape=jax.ShapeDtypeStruct(buf.shape, BF16),
        scratch_shapes=[pltpu.VMEM((n * rows, width), BF16)],
        input_output_aliases={n + 2: 0},
        compiler_params=pltpu.CompilerParams(vmem_limit_bytes=VMEM_LIMIT),
        cost_estimate=SMALL,
        name="project_near",
    )(*blocks, gain, w, buf)


def project_own_body(x_ref, gain_ref, w_ref, kv_ref, q_ref, x_scr):
    step = pl.program_id(0)

    @pl.when(step == 0)
    def _():
        x_scr[...] = (normalize(x_ref[...].astype(F32))[0] * gain_of(gain_ref)).astype(BF16)

    @pl.when(step < 2)
    def _():
        kv_ref[0] = dot(x_scr[...], w_ref[...]).astype(BF16)

    @pl.when(step == 2)
    def _():
        q_ref[...] = dot(x_scr[...], w_ref[...]).astype(BF16)


def project_own(x, gain, w):
    rows, width = x.shape
    feats = w.shape[2]
    return pl.pallas_call(
        project_own_body,
        grid=(3,),
        in_specs=[whole(x), whole(gain), pl.BlockSpec((pl.squeezed, width, feats), lambda i: ((i + 1) % 3, 0, 0))],
        out_specs=[
            pl.BlockSpec((1, rows, feats), lambda i: (0, 0, jnp.minimum(i, 1))),
            pl.BlockSpec((rows, feats), lambda i: (0, 0)),
        ],
        out_shape=[
            jax.ShapeDtypeStruct((BLOCKS, rows, 2 * feats), BF16),
            jax.ShapeDtypeStruct((rows, feats), BF16),
        ],
        scratch_shapes=[pltpu.VMEM((rows, width), BF16)],
        compiler_params=pltpu.CompilerParams(vmem_limit_bytes=VMEM_LIMIT),
        cost_estimate=SMALL,
        name="project_own",
    )(x, gain, w)


def project_queries_body(n, *refs):
    xs = refs[:n]
    gain_ref, w_ref, out_ref, x_scr = refs[n:]
    step = pl.program_id(0)
    for k in range(n):

        @pl.when(step == k)
        def _():
            x_scr[...] = xs[k][...]

    normed = (normalize(x_scr[...].astype(F32))[0] * gain_of(gain_ref)).astype(BF16)
    out_ref[0] = dot(normed, w_ref[...]).astype(BF16)


def project_queries(blocks, gain, w):
    n = len(blocks)
    rows, width = blocks[0].shape
    feats = w.shape[2]
    return pl.pallas_call(
        functools.partial(project_queries_body, n),
        grid=(n,),
        in_specs=[whole(b) for b in blocks] + [whole(gain), pl.BlockSpec((pl.squeezed, width, feats), lambda i: (0, 0, 0))],
        out_specs=pl.BlockSpec((1, rows, feats), lambda i: (i, 0, 0)),
        out_shape=jax.ShapeDtypeStruct((n, rows, feats), BF16),
        scratch_shapes=[pltpu.VMEM((rows, width), BF16)],
        compiler_params=pltpu.CompilerParams(vmem_limit_bytes=VMEM_LIMIT),
        cost_estimate=SMALL,
        name="project_queries",
    )(*blocks, gain, w)


def lay_out_keys(local_ref, all_scr, kv_scr, i):
    nb = kv_scr.shape[1] // 64
    for n in range(nb):
        kv_scr[i, n * 64 : (n + 1) * 64, :] = all_scr[local_ref[i, n]]


def forward_body(
    local_ref, count_ref, x0_ref, x1_ref, gain_ref, w_ref, kv_ref, q_ref, w_out_ref,
    part_ref, o_ref, lse_ref, p_ref, far_ref,
    n_scr, w_scr, wo_scr, q_scr, all_scr, kv_scr, p_scr, sem, p_sem,
):
    tubes, keys, feats2 = kv_scr.shape
    feats = feats2 // 2
    nb = keys // 64
    rows = tubes * 64
    copies = [
        pltpu.make_async_copy(w_ref.at[1], w_scr.at[0], sem.at[2]),
        pltpu.make_async_copy(w_ref.at[2], w_scr.at[1], sem.at[3]),
        pltpu.make_async_copy(q_ref, q_scr, sem.at[4]),
        pltpu.make_async_copy(w_out_ref, wo_scr, sem.at[5]),
        pltpu.make_async_copy(kv_ref.at[:tubes], all_scr.at[:tubes], sem.at[6]),
        pltpu.make_async_copy(kv_ref.at[6 * tubes :], all_scr.at[tubes : 7 * tubes], sem.at[7]),
    ]
    for k in (0, 1, 4, 5, 2, 3):
        copies[k].start()
    for k, x_ref in enumerate((x0_ref, x1_ref)):
        n_scr[k * rows : (k + 1) * rows] = (normalize(x_ref[...].astype(F32))[0] * gain_of(gain_ref)).astype(BF16)
    for k in range(2):
        copies[k].wait()
        out = dot(n_scr[...], w_scr[k]).astype(BF16).reshape(2 * tubes, 64, feats)
        all_scr[7 * tubes :, :, k * feats : (k + 1) * feats] = out
    far_copy = pltpu.make_async_copy(all_scr.at[7 * tubes :], far_ref, sem.at[8])
    far_copy.start()
    for k in (4, 5, 2):
        copies[k].wait()
    lane = lax.broadcasted_iota(jnp.int32, (1, keys), 1)
    slot, place = lane // 64, lane % 64
    pick = lax.broadcasted_iota(jnp.int32, (64, 128), 0) == lax.broadcasted_iota(jnp.int32, (64, 128), 1) % 64
    o_ref[...] = jnp.zeros_like(o_ref)

    def tube(i):
        limit = jnp.zeros((1, keys), jnp.int32)
        for n in range(nb):
            limit = jnp.where(slot == n, count_ref[local_ref[i, n] // tubes, local_ref[i, n] % tubes], limit)
        live = place < limit
        here = slice(i * 64, (i + 1) * 64)
        lay_out_keys(local_ref, all_scr, kv_scr, i)
        for group in GROUPS:
            h0, nh, l0, wd = group
            window = slice(l0, l0 + wd)
            q = spread(q_scr[here, window], group)
            s = dot_nt(q, kv_scr[i, :, window]) * LOG2_SCALE
            s = jnp.where(live, s, -1e30)
            top = jnp.max(s, axis=-1, keepdims=True)
            e = jnp.exp2(s - top)
            total = jnp.sum(e, axis=-1, keepdims=True)
            p = (e * (1.0 / total)).astype(BF16)
            p_scr[i, h0 * 64 : (h0 + nh) * 64, :] = p
            o = dot(p, kv_scr[i, :, feats + l0 : feats + l0 + wd])
            o_ref[here, window] += gather_heads(o, group, 64)
            lse = top + jnp.log2(total)
            for k in range(nh):
                column = jnp.broadcast_to(lse[k * 64 : (k + 1) * 64], (64, 128))
                lse_ref[i, h0 + k : h0 + k + 1, :] = jnp.sum(jnp.where(pick, column, 0.0), axis=0, keepdims=True)
        pltpu.make_async_copy(p_scr.at[i], p_ref.at[i], p_sem.at[i]).start()

    for i in range(tubes):
        tube(i)
    copies[3].wait()
    part_ref[...] = dot(o_ref[...].astype(BF16), wo_scr[...]).astype(BF16)
    far_copy.wait()
    for i in range(tubes):
        pltpu.make_async_copy(p_scr.at[i], p_ref.at[i], p_sem.at[i]).wait()


def attend_forward(local, counts, x0, x1, gain, w, kv, q, w_out):
    rows, feats = q.shape
    tubes = rows // 64
    keys = local.shape[1] * 64
    heads = feats // HEAD_DIM
    width = w_out.shape[1]
    vmem = pl.BlockSpec(memory_space=pltpu.VMEM)
    smem = pl.BlockSpec(memory_space=pltpu.SMEM)
    hbm = pl.BlockSpec(memory_space=pl.ANY)
    return pl.pallas_call(
        forward_body,
        in_specs=[smem, smem, vmem, vmem, vmem, hbm, hbm, hbm, hbm],
        out_specs=[vmem, vmem, vmem, hbm, hbm],
        out_shape=[
            jax.ShapeDtypeStruct((rows, width), BF16),
            jax.ShapeDtypeStruct((rows, feats), F32),
            jax.ShapeDtypeStruct((tubes, heads, 128), F32),
            jax.ShapeDtypeStruct((tubes, heads * 64, keys), BF16),
            jax.ShapeDtypeStruct((2 * tubes, 64, 2 * feats), BF16),
        ],
        scratch_shapes=[
            pltpu.VMEM((2 * rows, width), BF16),
            pltpu.VMEM((2, width, feats), BF16),
            pltpu.VMEM((feats, width), BF16),
            pltpu.VMEM((rows, feats), BF16),
            pltpu.VMEM((9 * tubes, 64, 2 * feats), BF16),
            pltpu.VMEM((tubes, keys, 2 * feats), BF16),
            pltpu.VMEM((tubes, heads * 64, keys), BF16),
            pltpu.SemaphoreType.DMA((9,)),
            pltpu.SemaphoreType.DMA((tubes,)),
        ],
        compiler_params=pltpu.CompilerParams(vmem_limit_bytes=VMEM_LIMIT),
        cost_estimate=SMALL,
        name="attend_forward",
    )(local, counts, x0, x1, gain, w, kv, q, w_out)


def parts_of(x, n):
    out = []
    for _ in range(n):
        piece = x.astype(BF16)
        out.append(piece)
        x = x - piece.astype(F32)
    return out


def middle_body(
    count_ref, sec_ref, mine_hbm, other_ref, video_hbm, target_hbm, w_out_hbm, o_hbm, lse_ref, pay_ref, g_ref,
    mine_ref, video_ref, target_ref, w_out_ref, o_ref, sem,
):
    rows, width = video_ref.shape
    feats = w_out_ref.shape[0]
    pairs = [
        (mine_hbm, mine_ref),
        (video_hbm, video_ref),
        (target_hbm, target_ref),
        (w_out_hbm, w_out_ref),
        (o_hbm, o_ref),
    ]
    copies = [pltpu.make_async_copy(*pair, sem.at[k]) for k, pair in enumerate(pairs)]
    for c in copies:
        c.start()
    heads = feats // HEAD_DIM
    tubes = rows // 64
    row = lax.broadcasted_iota(jnp.int32, (rows, 1), 0)
    limit = jnp.zeros((rows, 1), jnp.int32)
    for i in range(tubes):
        limit = jnp.where(row // 64 == i, count_ref[i], limit)
    valid = row % 64 < limit
    for c in copies[:3]:
        c.wait()
    mixed = mine_ref[...].astype(F32) + other_ref[...].astype(F32)
    g = jnp.where(valid, 2.0 * (video_ref[...].astype(F32) + mixed - target_ref[...].astype(F32)), 0.0)
    half = width // 2
    g_ref[...] = jnp.where(sec_ref[0] == 0, g[:, :half], g[:, half:])
    copies[3].wait()
    d_att = dot_nt(g.astype(BF16), w_out_ref[...]).astype(BF16)
    copies[4].wait()
    pay_ref[:rows] = d_att
    prod = d_att.astype(F32) * o_ref[...]
    head = lax.broadcasted_iota(jnp.int32, (heads, feats), 0)
    lane = lax.broadcasted_iota(jnp.int32, (heads, feats), 1)
    ones = ((lane >= head * HEAD_DIM) & (lane < (head + 1) * HEAD_DIM)).astype(F32)
    inner = []
    for i in range(tubes):
        one = prod[i * 64 : (i + 1) * 64]
        inner.append(
            lax.dot_general(
                ones,
                jnp.concatenate([one, one], axis=0),
                NT_DIMS,
                precision=lax.Precision.HIGHEST,
                preferred_element_type=F32,
            )
        )
    inner = jnp.concatenate(inner, axis=0)
    lse = lse_ref[...].reshape(tubes * heads, 128)
    for k, piece in enumerate(parts_of(lse, 3) + parts_of(inner, 2)):
        pay_ref[rows:, k * 128 : (k + 1) * 128] = piece


def middle(counts, sec, mine, other, video, target, w_out, o, lse):
    rows, width = video.shape
    feats = w_out.shape[0]
    vmem = pl.BlockSpec(memory_space=pltpu.VMEM)
    smem = pl.BlockSpec(memory_space=pltpu.SMEM)
    return pl.pallas_call(
        middle_body,
        in_specs=[smem, smem] + [pl.BlockSpec(memory_space=pl.ANY), vmem] + [pl.BlockSpec(memory_space=pl.ANY)] * 4 + [vmem],
        out_specs=[vmem, vmem],
        out_shape=[
            jax.ShapeDtypeStruct((rows + STAT_ROWS, feats), BF16),
            jax.ShapeDtypeStruct((rows, width // 2), F32),
        ],
        scratch_shapes=[pltpu.VMEM((rows, width), BF16)] * 3
        + [pltpu.VMEM((feats, width), BF16), pltpu.VMEM((rows, feats), F32), pltpu.SemaphoreType.DMA((5,))],
        compiler_params=pltpu.CompilerParams(vmem_limit_bytes=VMEM_LIMIT),
        cost_estimate=SMALL,
        name="middle",
    )(counts, sec, mine, other, video, target, w_out, o, lse)


def key_pass(
    list_ref, count_ref, q_scr, kv_scr, pay_scr, lse_scr, inner_scr, qc_scr, dc_scr, km_scr, vm_scr, dk_scr, dv_scr, grad_scr
):
    tubes = kv_scr.shape[0]
    size = qc_scr.shape[0] // 64
    feats = q_scr.shape[2]
    most = list_ref.shape[1] - 1
    low = lax.broadcasted_iota(jnp.int32, (8, 128), 1) < 64
    key_row = lax.broadcasted_iota(jnp.int32, (64, 1), 0)

    def tube(j, carry):
        alive = key_row < count_ref[j]
        block = pl.ds(pl.multiple_of(j * 64, 64), 64)
        for group in GROUPS:
            h0, nh, l0, wd = group
            these = slice(h0 * 64, (h0 + nh) * 64)
            km_scr[these, :wd] = spread(kv_scr[j, :, l0 : l0 + wd], group)
            vm_scr[these, :wd] = spread(kv_scr[j, :, feats + l0 : feats + l0 + wd], group)
        dk_scr[...] = jnp.zeros_like(dk_scr)
        dv_scr[...] = jnp.zeros_like(dv_scr)

        def chunk(c, carry):
            lses, inners = [], []
            for t in range(size):
                place = c * size + t
                i = list_ref[j, jnp.minimum(place, most - 1)]
                slot, w = i // tubes, i % tubes
                qc_scr[t * 64 : (t + 1) * 64, :] = q_scr[i]
                dc_scr[t * 64 : (t + 1) * 64, :] = pay_scr[slot, pl.ds(pl.multiple_of(w * 64, 64), 64), :]
                lses.append(jnp.where(place < list_ref[j, most], lse_scr[i], 1e30))
                inners.append(inner_scr[i])
            lse = jnp.concatenate([jnp.where(low, lses[t], lses[t + 1]) for t in range(0, size, 2)], axis=1)
            inner = jnp.concatenate([jnp.where(low, inners[t], inners[t + 1]) for t in range(0, size, 2)], axis=1)
            for group in GROUPS:
                h0, nh, l0, wd = group
                window = slice(l0, l0 + wd)
                these = slice(h0 * 64, (h0 + nh) * 64)
                qc, dc = qc_scr[:, window], dc_scr[:, window]
                s = dot_nt(km_scr[these, :wd], qc)
                d_prob = dot_nt(vm_scr[these, :wd], dc)
                p, d_score = [], []
                for m in range(nh):
                    part = slice(m * 64, (m + 1) * 64)
                    head = slice(h0 + m, h0 + m + 1)
                    one = jnp.where(alive, jnp.exp2(s[part] * LOG2_SCALE - lse[head]), 0.0)
                    p.append(one.astype(BF16))
                    d_score.append((one * (d_prob[part] - inner[head])).astype(BF16))
                dk_scr[these, :wd] += dot(jnp.concatenate(d_score, axis=0), qc)
                dv_scr[these, :wd] += dot(jnp.concatenate(p, axis=0), dc)
            return carry

        lax.fori_loop(0, (list_ref[j, most] + size - 1) // size, chunk, carry)
        for group in GROUPS:
            h0, nh, l0, wd = group
            these = slice(h0 * 64, (h0 + nh) * 64)
            grad_scr[block, l0 : l0 + wd] += gather_heads(dk_scr[these, :wd], group, 64) * SCALE
            grad_scr[block, feats + l0 : feats + l0 + wd] += gather_heads(dv_scr[these, :wd], group, 64)
        return carry

    lax.fori_loop(0, tubes, tube, 0)


def stats_of(pay_scr, k, rows, tubes, lse_scr, inner_scr):
    parts = [pay_scr[k, rows:, j * 128 : (j + 1) * 128].astype(F32) for j in range(5)]
    lse_scr[k * tubes : (k + 1) * tubes] = (parts[0] + parts[1] + parts[2]).reshape(tubes, -1, 128)
    inner_scr[k * tubes : (k + 1) * tubes] = (parts[3] + parts[4]).reshape(tubes, -1, 128)


def query_body(local_ref, pay_ref, kv_ref, far_ref, p_ref, dq_ref, all_scr, kv_scr, p_scr, pay_scr, dq_scr, sem, p_sem):
    tubes, keys, feats2 = kv_scr.shape
    feats = feats2 // 2
    pay_copy = pltpu.make_async_copy(pay_ref, pay_scr, sem.at[0])
    p_copies = [pltpu.make_async_copy(p_ref.at[i], p_scr.at[i], p_sem.at[i]) for i in range(tubes)]
    copies = [
        pltpu.make_async_copy(kv_ref.at[:tubes], all_scr.at[:tubes], sem.at[1]),
        pltpu.make_async_copy(kv_ref.at[6 * tubes :], all_scr.at[tubes : 7 * tubes], sem.at[2]),
        pltpu.make_async_copy(far_ref, all_scr.at[7 * tubes :], sem.at[3]),
    ]
    for c in copies + [pay_copy] + p_copies:
        c.start()
    for c in copies:
        c.wait()
    dq_scr[...] = jnp.zeros_like(dq_scr)
    pay_copy.wait()
    for i in range(tubes):
        here = slice(i * 64, (i + 1) * 64)
        lay_out_keys(local_ref, all_scr, kv_scr, i)
        p_copies[i].wait()
        for group in GROUPS:
            h0, nh, l0, wd = group
            window = slice(l0, l0 + wd)
            d_att = spread(pay_scr[here, window], group)
            d_prob = dot_nt(d_att, kv_scr[i, :, feats + l0 : feats + l0 + wd])
            p = p_scr[i, h0 * 64 : (h0 + nh) * 64, :].astype(F32)
            inner = jnp.sum(d_prob * p, axis=-1, keepdims=True)
            d_score = (p * (d_prob - inner)).astype(BF16)
            dq_scr[here, window] += gather_heads(dot(d_score, kv_scr[i, :, window]), group, 64)
    dq_ref[...] = (dq_scr[...] * SCALE).astype(BF16)


def query_grad(local, pay, kv, far, p):
    feats = pay.shape[1]
    tubes, _, keys = p.shape
    vmem = pl.BlockSpec(memory_space=pltpu.VMEM)
    smem = pl.BlockSpec(memory_space=pltpu.SMEM)
    hbm = pl.BlockSpec(memory_space=pl.ANY)
    return pl.pallas_call(
        query_body,
        in_specs=[smem] + [hbm] * 4,
        out_specs=vmem,
        out_shape=jax.ShapeDtypeStruct((tubes * 64, feats), BF16),
        scratch_shapes=[
            pltpu.VMEM((9 * tubes, 64, 2 * feats), BF16),
            pltpu.VMEM((tubes, keys, 2 * feats), BF16),
            pltpu.VMEM(p.shape, BF16),
            pltpu.VMEM(pay.shape, BF16),
            pltpu.VMEM((tubes * 64, feats), F32),
            pltpu.SemaphoreType.DMA((4,)),
            pltpu.SemaphoreType.DMA((tubes,)),
        ],
        compiler_params=pltpu.CompilerParams(vmem_limit_bytes=VMEM_LIMIT),
        cost_estimate=SMALL,
        name="query_grad",
    )(local, pay, kv, far, p)


def key_near_body(n, list_ref, count_ref, own_q_ref, q_ref, kv_ref, *rest):
    pays = rest[:n]
    grad_ref, q_scr, kv_scr, pay_scr, *scr, sem = rest[n:]
    lse_scr, inner_scr = scr[:2]
    tubes = kv_scr.shape[0]
    rows = tubes * 64
    pay_copies = [pltpu.make_async_copy(pays[k], pay_scr.at[k], sem.at[k]) for k in range(n)]
    copies = [
        pltpu.make_async_copy(own_q_ref, q_scr.at[:tubes], sem.at[n]),
        pltpu.make_async_copy(q_ref.at[: (n - 1) * tubes], q_scr.at[tubes:], sem.at[n + 1]),
        pltpu.make_async_copy(kv_ref.at[:tubes], kv_scr, sem.at[n + 2]),
    ]
    for c in pay_copies + copies:
        c.start()
    grad_ref[...] = jnp.zeros_like(grad_ref)
    for k in range(n):
        pay_copies[k].wait()
        stats_of(pay_scr, k, rows, tubes, lse_scr, inner_scr)
    for c in copies:
        c.wait()
    key_pass(list_ref, count_ref, q_scr, kv_scr, pay_scr, *scr, grad_ref)


def key_scratch(n, tubes, feats, size):
    rows = tubes * 64
    heads = feats // HEAD_DIM
    return [
        pltpu.VMEM((n * tubes, 64, feats), BF16),
        pltpu.VMEM((tubes, 64, 2 * feats), BF16),
        pltpu.VMEM((n, rows + STAT_ROWS, feats), BF16),
        pltpu.VMEM((n * tubes, heads, 128), F32),
        pltpu.VMEM((n * tubes, heads, 128), F32),
        pltpu.VMEM((size * 64, feats), BF16),
        pltpu.VMEM((size * 64, feats), BF16),
        pltpu.VMEM((heads * 64, 384), BF16),
        pltpu.VMEM((heads * 64, 384), BF16),
        pltpu.VMEM((heads * 64, 384), F32),
        pltpu.VMEM((heads * 64, 384), F32),
    ]


def key_near(lists, counts, own_q, q, kv, pays):
    tubes, _, feats = own_q.shape
    rows = tubes * 64
    n = len(pays)
    vmem = pl.BlockSpec(memory_space=pltpu.VMEM)
    smem = pl.BlockSpec(memory_space=pltpu.SMEM)
    hbm = pl.BlockSpec(memory_space=pl.ANY)
    return pl.pallas_call(
        functools.partial(key_near_body, n),
        in_specs=[smem] * 2 + [hbm] * 3 + [vmem] * n,
        out_specs=vmem,
        out_shape=jax.ShapeDtypeStruct((rows, 2 * feats), F32),
        scratch_shapes=key_scratch(n, tubes, feats, NEAR_CHUNK) + [pltpu.SemaphoreType.DMA((n + 3,))],
        compiler_params=pltpu.CompilerParams(vmem_limit_bytes=VMEM_LIMIT),
        cost_estimate=SMALL,
        name="key_near",
    )(lists, counts, own_q, q, kv, *pays)


def key_last_body(n, first, list_ref, count_ref, sec_ref, q_ref, kv_ref, w_ref, acc_ref, *rest):
    pays = rest[:n]
    video_ref, gain_ref, dq_ref, g_ref, send_ref, keep_ref = rest[n : n + 6]
    q_scr, kv_scr, pay_scr, *scr, w_scr, grad_scr, x_scr, dq_scr, g_scr, sem = rest[n + 6 :]
    lse_scr, inner_scr = scr[:2]
    tubes = kv_scr.shape[0]
    rows = tubes * 64
    feats = q_scr.shape[2]
    q_copy = pltpu.make_async_copy(q_ref.at[first * tubes : (first + n) * tubes], q_scr, sem.at[0])
    kv_copy = pltpu.make_async_copy(kv_ref.at[:tubes], kv_scr, sem.at[1])
    acc_copy = pltpu.make_async_copy(acc_ref, grad_scr, sem.at[2])
    w_copy = pltpu.make_async_copy(w_ref, w_scr, sem.at[3])
    x_copy = pltpu.make_async_copy(video_ref, x_scr, sem.at[4])
    dq_copy = pltpu.make_async_copy(dq_ref, dq_scr, sem.at[5])
    g_copy = pltpu.make_async_copy(g_ref, g_scr, sem.at[6])
    pay_copies = [pltpu.make_async_copy(pays[k], pay_scr.at[k], sem.at[7 + k]) for k in range(n)]
    for c in pay_copies + [q_copy, kv_copy, acc_copy, w_copy, x_copy, dq_copy, g_copy]:
        c.start()
    for k, c in enumerate(pay_copies):
        c.wait()
        stats_of(pay_scr, k, rows, tubes, lse_scr, inner_scr)
    q_copy.wait()
    kv_copy.wait()
    acc_copy.wait()
    key_pass(list_ref, count_ref, q_scr, kv_scr, pay_scr, *scr, grad_scr)
    d_proj = grad_scr[...].astype(BF16)
    x_copy.wait()
    xhat, inverse = normalize(x_scr[...].astype(F32))
    w_copy.wait()
    dq_copy.wait()
    g_copy.wait()
    d_normed = dot_nt(dq_scr[...], w_scr[0]) + dot_nt(d_proj[:, :feats], w_scr[1]) + dot_nt(d_proj[:, feats:], w_scr[2])
    scaled = d_normed * gain_of(gain_ref)
    out = (
        scaled
        - jnp.mean(scaled, axis=-1, keepdims=True)
        - xhat * jnp.mean(scaled * xhat, axis=-1, keepdims=True)
    ) * inverse
    half = out.shape[1] // 2
    lower = sec_ref[0] == 0
    send_ref[...] = jnp.where(lower, out[:, half:], out[:, :half]).astype(BF16)
    keep_ref[...] = jnp.where(lower, out[:, :half], out[:, half:]) + g_scr[...]


def key_last(first, lists, counts, sec, q, kv, w, acc, pays, video, gain, dq, g):
    rows, width = video.shape
    feats = q.shape[2]
    tubes = rows // 64
    n = len(pays)
    vmem = pl.BlockSpec(memory_space=pltpu.VMEM)
    smem = pl.BlockSpec(memory_space=pltpu.SMEM)
    hbm = pl.BlockSpec(memory_space=pl.ANY)
    return pl.pallas_call(
        functools.partial(key_last_body, n, first),
        in_specs=[smem] * 3 + [hbm] * 4 + [vmem] * n + [hbm] + [vmem] + [hbm] * 2,
        out_specs=[vmem, vmem],
        out_shape=[
            jax.ShapeDtypeStruct((rows, width // 2), BF16),
            jax.ShapeDtypeStruct((rows, width // 2), F32),
        ],
        scratch_shapes=key_scratch(n, tubes, feats, LAST_CHUNK)
        + [
            pltpu.VMEM((3, width, feats), BF16),
            pltpu.VMEM((rows, 2 * feats), F32),
            pltpu.VMEM((rows, width), BF16),
            pltpu.VMEM((rows, feats), BF16),
            pltpu.VMEM((rows, width // 2), F32),
            pltpu.SemaphoreType.DMA((7 + n,)),
        ],
        compiler_params=pltpu.CompilerParams(vmem_limit_bytes=VMEM_LIMIT),
        cost_estimate=SMALL,
        name="key_last",
    )(lists, counts, sec, q, kv, w, acc, *pays, video, gain, dq, g)


def per_device(video, target, gain, w_qkv, w_out, neighbours, counts):
    tt, th, tw, tube, width = video.shape
    feats = w_qkv.shape[2]
    nb = neighbours.shape[3]
    rows = tt * th * tw * tube
    n_t, n_h = lax.axis_size("tm"), lax.axis_size("height")
    t_here, h_here, sec = lax.axis_index("tm"), lax.axis_index("height"), lax.axis_index("section")
    off_chip = [p for h in range(1, n_h - 1, 2) for p in ((h, h + 1), (h + 1, h))]
    on_chip = [(h, h ^ 1) for h in range(n_h)]
    pair_times = [(t, t ^ 1) for t in range(n_t)]
    other_times = [p for t in range(1, n_t - 1, 2) for p in ((t, t + 1), (t + 1, t))]
    swap = [(0, 1), (1, 0)]

    def from_pair(x):
        return lax.ppermute(x, "tm", pair_times)

    def from_other(x):
        return lax.ppermute(x, "tm", other_times)

    def from_off(x):
        return lax.ppermute(x, "height", off_chip)

    def from_mate(x):
        return lax.ppermute(x, "height", on_chip)

    video = video.reshape(rows, width)
    target = target.reshape(rows, width)
    w = jnp.transpose(w_qkv, (1, 0, 2))

    off, mate, pair, other = from_off(video), from_mate(video), from_pair(video), from_other(video)
    meta = jnp.concatenate(
        [neighbours.reshape(tw, nb) + 1, jnp.pad(counts.reshape(1, tw), ((0, 0), (0, nb - tw)))], axis=0
    )
    own_video, meta, _ = lax.optimization_barrier((video, meta, mate))
    kv, own_q = project_own(own_video, gain, w)
    pair, other, kv = lax.optimization_barrier((pair, other, kv))
    three = jnp.stack([meta, from_pair(meta), from_other(meta)])
    off_meta, mate_meta = from_off(three), from_mate(three)
    off, off_meta, mate_meta, kv = lax.optimization_barrier((off, off_meta, mate_meta, kv))
    corners = from_pair(off), from_other(off)
    mates = mate, from_mate(pair), from_mate(other)
    rest = (pair, other, off, *mates)
    kv = project_near((pair, other, off, *mates), 6, gain, w, kv)
    kv = kv.reshape(BLOCKS * tw, tube, 2 * feats)

    meta = jnp.concatenate([three, off_meta[:1], mate_meta, off_meta[1:]])
    listed = (meta[:, :tw] - 1).reshape(9 * tw, nb)
    count_all = meta[:, tw, :tw]

    ids = neighbours.reshape(tw, nb)
    t_of, h_of, w_of = ids // (n_h * tw), ids // tw % n_h, ids % tw
    step = jnp.where(t_of == t_here, 0, jnp.where(t_of == t_here + 1 - 2 * (t_here % 2), 1, 2))
    slot = jnp.where(
        h_of == h_here,
        step,
        jnp.where(h_of == h_here + 1 - 2 * (h_here % 2), 4 + step, jnp.where(step == 0, 3, 6 + step)),
    )
    local = slot * tw + w_of
    own_ids = (t_here * n_h + h_here) * tw + jnp.arange(tw, dtype=jnp.int32)
    names = jnp.any(listed[None] == own_ids[:, None, None], axis=2)

    def listing(first, last, most):
        named = names[:, first:last]
        where = jnp.arange(last - first, dtype=jnp.int32)
        rank = jnp.sum(named[:, None, :] & (where[None, :] < where[:, None])[None], axis=2)
        hit = named[:, None, :] & (rank[:, None, :] == jnp.arange(most)[None, :, None])
        places = jnp.sum(jnp.where(hit, where, 0), axis=2).astype(jnp.int32)
        return jnp.concatenate([places, jnp.sum(named, axis=1, keepdims=True).astype(jnp.int32)], axis=1)

    near_list = listing(0, 7 * tw, 24)
    last_list = listing(7 * tw, 9 * tw, 8)
    sec = sec.reshape(1).astype(jnp.int32)
    own_counts = counts.reshape(tw)

    part, o, lse, p, far = attend_forward(local, count_all, *corners, gain, w, kv, own_q, w_out)
    other = lax.ppermute(part, "section", swap)
    part, videos = lax.optimization_barrier((part, (*rest, *corners)))
    far_q = project_queries(videos, gain, w).reshape(8 * tw, tube, feats)
    other, far_q, near_list, last_list = lax.optimization_barrier((other, far_q, near_list, last_list))
    pay, g = middle(own_counts, sec, part, other, video, target, w_out, o, lse)
    off, mate = from_off(pay), from_mate(pay)
    pair, after = from_pair(pay), from_other(pay)
    dq = query_grad(local, pay, kv, far, p)
    dq, off, pair, after = lax.optimization_barrier((dq, off, pair, after))
    near, mates, corners = (pay, pair, after, off), (mate, from_mate(pair), from_mate(after)), (from_pair(off), from_other(off))
    acc = key_near(near_list, own_counts, own_q.reshape(tw, tube, feats), far_q, kv, [*near, *mates])
    send, keep = key_last(6, last_list, own_counts, sec, far_q, kv, w, acc, corners, video, gain, dq, g)
    got = lax.ppermute(send, "section", swap)
    return (keep + got.astype(F32)).astype(BF16).reshape(tt, th, tw, tube, width // 2)


def solution(mesh):
    in_specs = (
        P("tm", "height", None, None, None),
        P("tm", "height", None, None, None),
        P(),
        P(None, None, "section"),
        P("section", None),
        P("tm", "height", None, None),
        P("tm", "height", None),
    )
    out_specs = P("tm", "height", None, None, "section")
    return jax.shard_map(
        per_device, mesh=mesh, in_specs=in_specs, out_specs=out_specs, check_vma=False
    )
```

```python
import functools
import math

import jax
import jax.numpy as jnp
from jax import lax
from jax.experimental import pallas as pl
from jax.experimental.pallas import tpu as pltpu
from jax.sharding import PartitionSpec as P

HEAD_DIM = 80
SCALE = HEAD_DIM ** (-0.5)
LOG2_SCALE = SCALE * math.log2(math.e)
BF16 = jnp.bfloat16
F32 = jnp.float32
MIB = 1 << 20
GROUPS = ((0, 3, 0, 256), (3, 2, 128, 384), (5, 3, 384, 256))
NEAR_CHUNK, LAST_CHUNK = 8, 2
STAT_ROWS = 32
BLOCKS = 12
SMALL = pl.CostEstimate(flops=1, bytes_accessed=1, transcendentals=0)
VMEM_LIMIT = 52 * MIB

NT_DIMS = (((1,), (1,)), ((), ()))


def dot(a, b):
    return jnp.dot(a, b, preferred_element_type=F32)


def dot_nt(a, b):
    return lax.dot_general(a, b, NT_DIMS, preferred_element_type=F32)


def head_row(head, first_lane, lanes):
    lane = lax.broadcasted_iota(jnp.int32, (1, lanes), 1) + first_lane
    return jnp.where((lane >= head * HEAD_DIM) & (lane < (head + 1) * HEAD_DIM), 1.0, 0.0).astype(F32)


def spread(x, group):
    h0, nh, l0, wd = group
    out = []
    for h in range(h0, h0 + nh):
        mask = jnp.broadcast_to(head_row(h, l0, wd), (16, wd)).astype(BF16)
        out += [x[r : r + 16] * mask for r in range(0, x.shape[0], 16)]
    return jnp.concatenate(out, axis=0)


def gather_heads(y, group, rows):
    h0, nh, l0, wd = group
    total = y[:rows] * head_row(h0, l0, wd)
    for k in range(1, nh):
        total = total + y[k * rows : (k + 1) * rows] * head_row(h0 + k, l0, wd)
    return total


def add_group(ref, rows, value, group):
    h0, nh, l0, wd = group
    ref[rows, l0 : l0 + wd] = ref[rows, l0 : l0 + wd] + value


def gain_of(gain_ref):
    return gain_ref[...].reshape(1, -1)


def normalize(x):
    centred = x - jnp.mean(x, axis=-1, keepdims=True)
    inverse = lax.rsqrt(jnp.mean(centred * centred, axis=-1, keepdims=True) + 1e-06)
    return centred * inverse, inverse


def project_near_body(n, *refs):
    xs = refs[:n]
    gain_ref, w_ref = refs[n : n + 2]
    kv_ref, x_scr = refs[n + 3 :]
    rows = xs[0].shape[0]

    @pl.when(pl.program_id(0) == 0)
    def _():
        for k in range(n):
            x_scr[k * rows : (k + 1) * rows] = (normalize(xs[k][...].astype(F32))[0] * gain_of(gain_ref)).astype(BF16)

    kv_ref[...] = dot(x_scr[...], w_ref[...]).astype(BF16).reshape(kv_ref.shape)


def whole(a):
    return pl.BlockSpec(a.shape, lambda i: (0,) * a.ndim)


def project_near(blocks, first, gain, w, buf):
    n = len(blocks)
    rows, width = blocks[0].shape
    feats = w.shape[2]
    return pl.pallas_call(
        functools.partial(project_near_body, n),
        grid=(2,),
        in_specs=[whole(b) for b in blocks]
        + [whole(gain), pl.BlockSpec((pl.squeezed, width, feats), lambda i: (i + 1, 0, 0))]
        + [pl.BlockSpec(memory_space=pl.ANY)],
        out_specs=pl.BlockSpec((n, rows, feats), lambda i: (first // n, 0, i)),
        out_shape=jax.ShapeDtypeStruct(buf.shape, BF16),
        scratch_shapes=[pltpu.VMEM((n * rows, width), BF16)],
        input_output_aliases={n + 2: 0},
        compiler_params=pltpu.CompilerParams(vmem_limit_bytes=VMEM_LIMIT),
        cost_estimate=SMALL,
        name="project_near",
    )(*blocks, gain, w, buf)


def project_own_body(x_ref, gain_ref, w_ref, kv_ref, q_ref, x_scr):
    step = pl.program_id(0)

    @pl.when(step == 0)
    def _():
        x_scr[...] = (normalize(x_ref[...].astype(F32))[0] * gain_of(gain_ref)).astype(BF16)

    @pl.when(step < 2)
    def _():
        kv_ref[0] = dot(x_scr[...], w_ref[...]).astype(BF16)

    @pl.when(step == 2)
    def _():
        q_ref[...] = dot(x_scr[...], w_ref[...]).astype(BF16)


def project_own(x, gain, w):
    rows, width = x.shape
    feats = w.shape[2]
    return pl.pallas_call(
        project_own_body,
        grid=(3,),
        in_specs=[whole(x), whole(gain), pl.BlockSpec((pl.squeezed, width, feats), lambda i: ((i + 1) % 3, 0, 0))],
        out_specs=[
            pl.BlockSpec((1, rows, feats), lambda i: (0, 0, jnp.minimum(i, 1))),
            pl.BlockSpec((rows, feats), lambda i: (0, 0)),
        ],
        out_shape=[
            jax.ShapeDtypeStruct((BLOCKS, rows, 2 * feats), BF16),
            jax.ShapeDtypeStruct((rows, feats), BF16),
        ],
        scratch_shapes=[pltpu.VMEM((rows, width), BF16)],
        compiler_params=pltpu.CompilerParams(vmem_limit_bytes=VMEM_LIMIT),
        cost_estimate=SMALL,
        name="project_own",
    )(x, gain, w)


def project_queries_body(n, *refs):
    xs = refs[:n]
    gain_ref, w_ref, out_ref, x_scr = refs[n:]
    step = pl.program_id(0)
    for k in range(n):

        @pl.when(step == k)
        def _():
            x_scr[...] = xs[k][...]

    normed = (normalize(x_scr[...].astype(F32))[0] * gain_of(gain_ref)).astype(BF16)
    out_ref[0] = dot(normed, w_ref[...]).astype(BF16)


def project_queries(blocks, gain, w):
    n = len(blocks)
    rows, width = blocks[0].shape
    feats = w.shape[2]
    return pl.pallas_call(
        functools.partial(project_queries_body, n),
        grid=(n,),
        in_specs=[whole(b) for b in blocks] + [whole(gain), pl.BlockSpec((pl.squeezed, width, feats), lambda i: (0, 0, 0))],
        out_specs=pl.BlockSpec((1, rows, feats), lambda i: (i, 0, 0)),
        out_shape=jax.ShapeDtypeStruct((n, rows, feats), BF16),
        scratch_shapes=[pltpu.VMEM((rows, width), BF16)],
        compiler_params=pltpu.CompilerParams(vmem_limit_bytes=VMEM_LIMIT),
        cost_estimate=SMALL,
        name="project_queries",
    )(*blocks, gain, w)


def lay_out_keys(local_ref, all_scr, kv_scr, i):
    nb = kv_scr.shape[1] // 64
    for n in range(nb):
        kv_scr[i, n * 64 : (n + 1) * 64, :] = all_scr[local_ref[i, n]]


def forward_body(
    local_ref, count_ref, x0_ref, x1_ref, gain_ref, w_ref, kv_ref, q_ref, w_out_ref,
    part_ref, o_ref, lse_ref, p_ref, far_ref,
    n_scr, w_scr, wo_scr, q_scr, all_scr, kv_scr, p_scr, sem, p_sem,
):
    tubes, keys, feats2 = kv_scr.shape
    feats = feats2 // 2
    nb = keys // 64
    rows = tubes * 64
    copies = [
        pltpu.make_async_copy(w_ref.at[1], w_scr.at[0], sem.at[2]),
        pltpu.make_async_copy(w_ref.at[2], w_scr.at[1], sem.at[3]),
        pltpu.make_async_copy(q_ref, q_scr, sem.at[4]),
        pltpu.make_async_copy(w_out_ref, wo_scr, sem.at[5]),
        pltpu.make_async_copy(kv_ref.at[:tubes], all_scr.at[:tubes], sem.at[6]),
        pltpu.make_async_copy(kv_ref.at[6 * tubes :], all_scr.at[tubes : 7 * tubes], sem.at[7]),
    ]
    for k in (0, 1, 4, 5, 2, 3):
        copies[k].start()
    for k, x_ref in enumerate((x0_ref, x1_ref)):
        n_scr[k * rows : (k + 1) * rows] = (normalize(x_ref[...].astype(F32))[0] * gain_of(gain_ref)).astype(BF16)
    for k in range(2):
        copies[k].wait()
        out = dot(n_scr[...], w_scr[k]).astype(BF16).reshape(2 * tubes, 64, feats)
        all_scr[7 * tubes :, :, k * feats : (k + 1) * feats] = out
    far_copy = pltpu.make_async_copy(all_scr.at[7 * tubes :], far_ref, sem.at[8])
    far_copy.start()
    for k in (4, 5, 2):
        copies[k].wait()
    lane = lax.broadcasted_iota(jnp.int32, (1, keys), 1)
    slot, place = lane // 64, lane % 64
    pick = lax.broadcasted_iota(jnp.int32, (64, 128), 0) == lax.broadcasted_iota(jnp.int32, (64, 128), 1) % 64
    o_ref[...] = jnp.zeros_like(o_ref)

    def tube(i):
        limit = jnp.zeros((1, keys), jnp.int32)
        for n in range(nb):
            limit = jnp.where(slot == n, count_ref[local_ref[i, n] // tubes, local_ref[i, n] % tubes], limit)
        live = place < limit
        here = slice(i * 64, (i + 1) * 64)
        lay_out_keys(local_ref, all_scr, kv_scr, i)
        for group in GROUPS:
            h0, nh, l0, wd = group
            window = slice(l0, l0 + wd)
            q = spread(q_scr[here, window], group)
            s = dot_nt(q, kv_scr[i, :, window]) * LOG2_SCALE
            s = jnp.where(live, s, -1e30)
            top = jnp.max(s, axis=-1, keepdims=True)
            e = jnp.exp2(s - top)
            total = jnp.sum(e, axis=-1, keepdims=True)
            p = (e * (1.0 / total)).astype(BF16)
            p_scr[i, h0 * 64 : (h0 + nh) * 64, :] = p
            o = dot(p, kv_scr[i, :, feats + l0 : feats + l0 + wd])
            o_ref[here, window] += gather_heads(o, group, 64)
            lse = top + jnp.log2(total)
            for k in range(nh):
                column = jnp.broadcast_to(lse[k * 64 : (k + 1) * 64], (64, 128))
                lse_ref[i, h0 + k : h0 + k + 1, :] = jnp.sum(jnp.where(pick, column, 0.0), axis=0, keepdims=True)
        pltpu.make_async_copy(p_scr.at[i], p_ref.at[i], p_sem.at[i]).start()

    for i in range(tubes):
        tube(i)
    copies[3].wait()
    part_ref[...] = dot(o_ref[...].astype(BF16), wo_scr[...]).astype(BF16)
    far_copy.wait()
    for i in range(tubes):
        pltpu.make_async_copy(p_scr.at[i], p_ref.at[i], p_sem.at[i]).wait()


def attend_forward(local, counts, x0, x1, gain, w, kv, q, w_out):
    rows, feats = q.shape
    tubes = rows // 64
    keys = local.shape[1] * 64
    heads = feats // HEAD_DIM
    width = w_out.shape[1]
    vmem = pl.BlockSpec(memory_space=pltpu.VMEM)
    smem = pl.BlockSpec(memory_space=pltpu.SMEM)
    hbm = pl.BlockSpec(memory_space=pl.ANY)
    return pl.pallas_call(
        forward_body,
        in_specs=[smem, smem, vmem, vmem, vmem, hbm, hbm, hbm, hbm],
        out_specs=[vmem, vmem, vmem, hbm, hbm],
        out_shape=[
            jax.ShapeDtypeStruct((rows, width), BF16),
            jax.ShapeDtypeStruct((rows, feats), F32),
            jax.ShapeDtypeStruct((tubes, heads, 128), F32),
            jax.ShapeDtypeStruct((tubes, heads * 64, keys), BF16),
            jax.ShapeDtypeStruct((2 * tubes, 64, 2 * feats), BF16),
        ],
        scratch_shapes=[
            pltpu.VMEM((2 * rows, width), BF16),
            pltpu.VMEM((2, width, feats), BF16),
            pltpu.VMEM((feats, width), BF16),
            pltpu.VMEM((rows, feats), BF16),
            pltpu.VMEM((9 * tubes, 64, 2 * feats), BF16),
            pltpu.VMEM((tubes, keys, 2 * feats), BF16),
            pltpu.VMEM((tubes, heads * 64, keys), BF16),
            pltpu.SemaphoreType.DMA((9,)),
            pltpu.SemaphoreType.DMA((tubes,)),
        ],
        compiler_params=pltpu.CompilerParams(vmem_limit_bytes=VMEM_LIMIT),
        cost_estimate=SMALL,
        name="attend_forward",
    )(local, counts, x0, x1, gain, w, kv, q, w_out)


def parts_of(x, n):
    out = []
    for _ in range(n):
        piece = x.astype(BF16)
        out.append(piece)
        x = x - piece.astype(F32)
    return out


def middle_body(
    count_ref, sec_ref, mine_hbm, other_ref, video_hbm, target_hbm, w_out_hbm, o_hbm, lse_ref, pay_ref, g_ref,
    mine_ref, video_ref, target_ref, w_out_ref, o_ref, sem,
):
    rows, width = video_ref.shape
    feats = w_out_ref.shape[0]
    pairs = [
        (mine_hbm, mine_ref),
        (video_hbm, video_ref),
        (target_hbm, target_ref),
        (w_out_hbm, w_out_ref),
        (o_hbm, o_ref),
    ]
    copies = [pltpu.make_async_copy(*pair, sem.at[k]) for k, pair in enumerate(pairs)]
    for c in copies:
        c.start()
    heads = feats // HEAD_DIM
    tubes = rows // 64
    row = lax.broadcasted_iota(jnp.int32, (rows, 1), 0)
    limit = jnp.zeros((rows, 1), jnp.int32)
    for i in range(tubes):
        limit = jnp.where(row // 64 == i, count_ref[i], limit)
    valid = row % 64 < limit
    for c in copies[:3]:
        c.wait()
    mixed = mine_ref[...].astype(F32) + other_ref[...].astype(F32)
    g = jnp.where(valid, 2.0 * (video_ref[...].astype(F32) + mixed - target_ref[...].astype(F32)), 0.0)
    half = width // 2
    g_ref[...] = jnp.where(sec_ref[0] == 0, g[:, :half], g[:, half:])
    copies[3].wait()
    d_att = dot_nt(g.astype(BF16), w_out_ref[...]).astype(BF16)
    copies[4].wait()
    pay_ref[:rows] = d_att
    prod = d_att.astype(F32) * o_ref[...]
    head = lax.broadcasted_iota(jnp.int32, (heads, feats), 0)
    lane = lax.broadcasted_iota(jnp.int32, (heads, feats), 1)
    ones = ((lane >= head * HEAD_DIM) & (lane < (head + 1) * HEAD_DIM)).astype(F32)
    inner = []
    for i in range(tubes):
        one = prod[i * 64 : (i + 1) * 64]
        inner.append(
            lax.dot_general(
                ones,
                jnp.concatenate([one, one], axis=0),
                NT_DIMS,
                precision=lax.Precision.HIGHEST,
                preferred_element_type=F32,
            )
        )
    inner = jnp.concatenate(inner, axis=0)
    lse = lse_ref[...].reshape(tubes * heads, 128)
    for k, piece in enumerate(parts_of(lse, 3) + parts_of(inner, 2)):
        pay_ref[rows:, k * 128 : (k + 1) * 128] = piece


def middle(counts, sec, mine, other, video, target, w_out, o, lse):
    rows, width = video.shape
    feats = w_out.shape[0]
    vmem = pl.BlockSpec(memory_space=pltpu.VMEM)
    smem = pl.BlockSpec(memory_space=pltpu.SMEM)
    return pl.pallas_call(
        middle_body,
        in_specs=[smem, smem] + [pl.BlockSpec(memory_space=pl.ANY), vmem] + [pl.BlockSpec(memory_space=pl.ANY)] * 4 + [vmem],
        out_specs=[vmem, vmem],
        out_shape=[
            jax.ShapeDtypeStruct((rows + STAT_ROWS, feats), BF16),
            jax.ShapeDtypeStruct((rows, width // 2), F32),
        ],
        scratch_shapes=[pltpu.VMEM((rows, width), BF16)] * 3
        + [pltpu.VMEM((feats, width), BF16), pltpu.VMEM((rows, feats), F32), pltpu.SemaphoreType.DMA((5,))],
        compiler_params=pltpu.CompilerParams(vmem_limit_bytes=VMEM_LIMIT),
        cost_estimate=SMALL,
        name="middle",
    )(counts, sec, mine, other, video, target, w_out, o, lse)


def key_pass(
    list_ref, count_ref, q_scr, kv_scr, pay_scr, lse_scr, inner_scr, qc_scr, dc_scr, km_scr, vm_scr, dk_scr, dv_scr, grad_scr
):
    tubes = kv_scr.shape[0]
    size = qc_scr.shape[0] // 64
    feats = q_scr.shape[2]
    most = list_ref.shape[1] - 1
    low = lax.broadcasted_iota(jnp.int32, (8, 128), 1) < 64
    key_row = lax.broadcasted_iota(jnp.int32, (64, 1), 0)

    def tube(j, carry):
        alive = key_row < count_ref[j]
        block = pl.ds(pl.multiple_of(j * 64, 64), 64)
        for group in GROUPS:
            h0, nh, l0, wd = group
            these = slice(h0 * 64, (h0 + nh) * 64)
            km_scr[these, :wd] = spread(kv_scr[j, :, l0 : l0 + wd], group)
            vm_scr[these, :wd] = spread(kv_scr[j, :, feats + l0 : feats + l0 + wd], group)
        dk_scr[...] = jnp.zeros_like(dk_scr)
        dv_scr[...] = jnp.zeros_like(dv_scr)

        def chunk(c, carry):
            lses, inners = [], []
            for t in range(size):
                place = c * size + t
                i = list_ref[j, jnp.minimum(place, most - 1)]
                slot, w = i // tubes, i % tubes
                qc_scr[t * 64 : (t + 1) * 64, :] = q_scr[i]
                dc_scr[t * 64 : (t + 1) * 64, :] = pay_scr[slot, pl.ds(pl.multiple_of(w * 64, 64), 64), :]
                lses.append(jnp.where(place < list_ref[j, most], lse_scr[i], 1e30))
                inners.append(inner_scr[i])
            lse = jnp.concatenate([jnp.where(low, lses[t], lses[t + 1]) for t in range(0, size, 2)], axis=1)
            inner = jnp.concatenate([jnp.where(low, inners[t], inners[t + 1]) for t in range(0, size, 2)], axis=1)
            for group in GROUPS:
                h0, nh, l0, wd = group
                window = slice(l0, l0 + wd)
                these = slice(h0 * 64, (h0 + nh) * 64)
                qc, dc = qc_scr[:, window], dc_scr[:, window]
                s = dot_nt(km_scr[these, :wd], qc)
                d_prob = dot_nt(vm_scr[these, :wd], dc)
                p, d_score = [], []
                for m in range(nh):
                    part = slice(m * 64, (m + 1) * 64)
                    head = slice(h0 + m, h0 + m + 1)
                    one = jnp.where(alive, jnp.exp2(s[part] * LOG2_SCALE - lse[head]), 0.0)
                    p.append(one.astype(BF16))
                    d_score.append((one * (d_prob[part] - inner[head])).astype(BF16))
                dk_scr[these, :wd] += dot(jnp.concatenate(d_score, axis=0), qc)
                dv_scr[these, :wd] += dot(jnp.concatenate(p, axis=0), dc)
            return carry

        lax.fori_loop(0, (list_ref[j, most] + size - 1) // size, chunk, carry)
        for group in GROUPS:
            h0, nh, l0, wd = group
            these = slice(h0 * 64, (h0 + nh) * 64)
            grad_scr[block, l0 : l0 + wd] += gather_heads(dk_scr[these, :wd], group, 64) * SCALE
            grad_scr[block, feats + l0 : feats + l0 + wd] += gather_heads(dv_scr[these, :wd], group, 64)
        return carry

    lax.fori_loop(0, tubes, tube, 0)


def stats_of(pay_scr, k, rows, tubes, lse_scr, inner_scr):
    parts = [pay_scr[k, rows:, j * 128 : (j + 1) * 128].astype(F32) for j in range(5)]
    lse_scr[k * tubes : (k + 1) * tubes] = (parts[0] + parts[1] + parts[2]).reshape(tubes, -1, 128)
    inner_scr[k * tubes : (k + 1) * tubes] = (parts[3] + parts[4]).reshape(tubes, -1, 128)


def query_body(local_ref, pay_ref, kv_ref, far_ref, p_ref, dq_ref, all_scr, kv_scr, p_scr, pay_scr, dq_scr, sem, p_sem):
    tubes, keys, feats2 = kv_scr.shape
    feats = feats2 // 2
    pay_copy = pltpu.make_async_copy(pay_ref, pay_scr, sem.at[0])
    p_copies = [pltpu.make_async_copy(p_ref.at[i], p_scr.at[i], p_sem.at[i]) for i in range(tubes)]
    copies = [
        pltpu.make_async_copy(kv_ref.at[:tubes], all_scr.at[:tubes], sem.at[1]),
        pltpu.make_async_copy(kv_ref.at[6 * tubes :], all_scr.at[tubes : 7 * tubes], sem.at[2]),
        pltpu.make_async_copy(far_ref, all_scr.at[7 * tubes :], sem.at[3]),
    ]
    for c in copies + [pay_copy] + p_copies:
        c.start()
    for c in copies:
        c.wait()
    dq_scr[...] = jnp.zeros_like(dq_scr)
    pay_copy.wait()
    for i in range(tubes):
        here = slice(i * 64, (i + 1) * 64)
        lay_out_keys(local_ref, all_scr, kv_scr, i)
        p_copies[i].wait()
        for group in GROUPS:
            h0, nh, l0, wd = group
            window = slice(l0, l0 + wd)
            d_att = spread(pay_scr[here, window], group)
            d_prob = dot_nt(d_att, kv_scr[i, :, feats + l0 : feats + l0 + wd])
            p = p_scr[i, h0 * 64 : (h0 + nh) * 64, :].astype(F32)
            inner = jnp.sum(d_prob * p, axis=-1, keepdims=True)
            d_score = (p * (d_prob - inner)).astype(BF16)
            dq_scr[here, window] += gather_heads(dot(d_score, kv_scr[i, :, window]), group, 64)
    dq_ref[...] = (dq_scr[...] * SCALE).astype(BF16)


def query_grad(local, pay, kv, far, p):
    feats = pay.shape[1]
    tubes, _, keys = p.shape
    vmem = pl.BlockSpec(memory_space=pltpu.VMEM)
    smem = pl.BlockSpec(memory_space=pltpu.SMEM)
    hbm = pl.BlockSpec(memory_space=pl.ANY)
    return pl.pallas_call(
        query_body,
        in_specs=[smem] + [hbm] * 4,
        out_specs=vmem,
        out_shape=jax.ShapeDtypeStruct((tubes * 64, feats), BF16),
        scratch_shapes=[
            pltpu.VMEM((9 * tubes, 64, 2 * feats), BF16),
            pltpu.VMEM((tubes, keys, 2 * feats), BF16),
            pltpu.VMEM(p.shape, BF16),
            pltpu.VMEM(pay.shape, BF16),
            pltpu.VMEM((tubes * 64, feats), F32),
            pltpu.SemaphoreType.DMA((4,)),
            pltpu.SemaphoreType.DMA((tubes,)),
        ],
        compiler_params=pltpu.CompilerParams(vmem_limit_bytes=VMEM_LIMIT),
        cost_estimate=SMALL,
        name="query_grad",
    )(local, pay, kv, far, p)


def key_near_body(n, list_ref, count_ref, own_q_ref, q_ref, kv_ref, w_ref, dq_ref, *rest):
    pays = rest[:n]
    grad_ref, base_ref, w_scr, dq_scr, q_scr, kv_scr, pay_scr, *scr, sem = rest[n:]
    lse_scr, inner_scr = scr[:2]
    tubes = kv_scr.shape[0]
    rows = tubes * 64
    pay_copies = [pltpu.make_async_copy(pays[k], pay_scr.at[k], sem.at[k]) for k in range(n)]
    first = [
        pltpu.make_async_copy(dq_ref, dq_scr, sem.at[n + 4]),
        pltpu.make_async_copy(w_ref.at[0], w_scr, sem.at[n]),
    ]
    copies = [
        pltpu.make_async_copy(own_q_ref, q_scr.at[:tubes], sem.at[n + 1]),
        pltpu.make_async_copy(q_ref.at[: (n - 1) * tubes], q_scr.at[tubes:], sem.at[n + 2]),
        pltpu.make_async_copy(kv_ref.at[:tubes], kv_scr, sem.at[n + 3]),
    ]
    for c in first + pay_copies + copies:
        c.start()
    grad_ref[...] = jnp.zeros_like(grad_ref)
    for c in first:
        c.wait()
    base_ref[...] = dot_nt(dq_scr[...], w_scr[...])
    for k in range(n):
        pay_copies[k].wait()
        stats_of(pay_scr, k, rows, tubes, lse_scr, inner_scr)
    for c in copies:
        c.wait()
    key_pass(list_ref, count_ref, q_scr, kv_scr, pay_scr, *scr, grad_ref)


def key_scratch(n, tubes, feats, size):
    rows = tubes * 64
    heads = feats // HEAD_DIM
    return [
        pltpu.VMEM((n * tubes, 64, feats), BF16),
        pltpu.VMEM((tubes, 64, 2 * feats), BF16),
        pltpu.VMEM((n, rows + STAT_ROWS, feats), BF16),
        pltpu.VMEM((n * tubes, heads, 128), F32),
        pltpu.VMEM((n * tubes, heads, 128), F32),
        pltpu.VMEM((size * 64, feats), BF16),
        pltpu.VMEM((size * 64, feats), BF16),
        pltpu.VMEM((heads * 64, 384), BF16),
        pltpu.VMEM((heads * 64, 384), BF16),
        pltpu.VMEM((heads * 64, 384), F32),
        pltpu.VMEM((heads * 64, 384), F32),
    ]


def key_near(lists, counts, own_q, q, kv, w, dq, pays):
    rows, feats = dq.shape
    width = w.shape[1]
    tubes = rows // 64
    n = len(pays)
    vmem = pl.BlockSpec(memory_space=pltpu.VMEM)
    smem = pl.BlockSpec(memory_space=pltpu.SMEM)
    hbm = pl.BlockSpec(memory_space=pl.ANY)
    return pl.pallas_call(
        functools.partial(key_near_body, n),
        in_specs=[smem] * 2 + [hbm] * 5 + [vmem] * n,
        out_specs=[vmem, vmem],
        out_shape=[
            jax.ShapeDtypeStruct((rows, 2 * feats), F32),
            jax.ShapeDtypeStruct((rows, width), F32),
        ],
        scratch_shapes=[pltpu.VMEM((width, feats), BF16), pltpu.VMEM((rows, feats), BF16)]
        + key_scratch(n, tubes, feats, NEAR_CHUNK)
        + [pltpu.SemaphoreType.DMA((n + 5,))],
        compiler_params=pltpu.CompilerParams(vmem_limit_bytes=VMEM_LIMIT),
        cost_estimate=SMALL,
        name="key_near",
    )(lists, counts, own_q, q, kv, w, dq, *pays)


def key_last_body(n, first, list_ref, count_ref, sec_ref, q_ref, kv_ref, w_ref, acc_ref, *rest):
    pays = rest[:n]
    video_ref, gain_ref, base_ref, g_ref, send_ref, keep_ref = rest[n : n + 6]
    q_scr, kv_scr, pay_scr, *scr, w_scr, grad_scr, x_scr, base_scr, g_scr, sem = rest[n + 6 :]
    lse_scr, inner_scr = scr[:2]
    tubes = kv_scr.shape[0]
    rows = tubes * 64
    feats = q_scr.shape[2]
    q_copy = pltpu.make_async_copy(q_ref.at[first * tubes : (first + n) * tubes], q_scr, sem.at[0])
    kv_copy = pltpu.make_async_copy(kv_ref.at[:tubes], kv_scr, sem.at[1])
    acc_copy = pltpu.make_async_copy(acc_ref, grad_scr, sem.at[2])
    w_copy = pltpu.make_async_copy(w_ref.at[1:], w_scr, sem.at[3])
    x_copy = pltpu.make_async_copy(video_ref, x_scr, sem.at[4])
    base_copy = pltpu.make_async_copy(base_ref, base_scr, sem.at[5])
    g_copy = pltpu.make_async_copy(g_ref, g_scr, sem.at[6])
    pay_copies = [pltpu.make_async_copy(pays[k], pay_scr.at[k], sem.at[7 + k]) for k in range(n)]
    for c in pay_copies + [q_copy, kv_copy, acc_copy, w_copy, x_copy, base_copy, g_copy]:
        c.start()
    for k, c in enumerate(pay_copies):
        c.wait()
        stats_of(pay_scr, k, rows, tubes, lse_scr, inner_scr)
    q_copy.wait()
    kv_copy.wait()
    acc_copy.wait()
    key_pass(list_ref, count_ref, q_scr, kv_scr, pay_scr, *scr, grad_scr)
    d_proj = grad_scr[...].astype(BF16)
    x_copy.wait()
    xhat, inverse = normalize(x_scr[...].astype(F32))
    w_copy.wait()
    base_copy.wait()
    g_copy.wait()
    d_normed = base_scr[...] + dot_nt(d_proj[:, :feats], w_scr[0]) + dot_nt(d_proj[:, feats:], w_scr[1])
    scaled = d_normed * gain_of(gain_ref)
    out = (
        scaled
        - jnp.mean(scaled, axis=-1, keepdims=True)
        - xhat * jnp.mean(scaled * xhat, axis=-1, keepdims=True)
    ) * inverse
    half = out.shape[1] // 2
    lower = sec_ref[0] == 0
    send_ref[...] = jnp.where(lower, out[:, half:], out[:, :half]).astype(BF16)
    keep_ref[...] = jnp.where(lower, out[:, :half], out[:, half:]) + g_scr[...]


def key_last(first, lists, counts, sec, q, kv, w, acc, pays, video, gain, base, g):
    rows, width = video.shape
    feats = q.shape[2]
    tubes = rows // 64
    n = len(pays)
    vmem = pl.BlockSpec(memory_space=pltpu.VMEM)
    smem = pl.BlockSpec(memory_space=pltpu.SMEM)
    hbm = pl.BlockSpec(memory_space=pl.ANY)
    return pl.pallas_call(
        functools.partial(key_last_body, n, first),
        in_specs=[smem] * 3 + [hbm] * 4 + [vmem] * n + [hbm] + [vmem] + [hbm] * 2,
        out_specs=[vmem, vmem],
        out_shape=[
            jax.ShapeDtypeStruct((rows, width // 2), BF16),
            jax.ShapeDtypeStruct((rows, width // 2), F32),
        ],
        scratch_shapes=key_scratch(n, tubes, feats, LAST_CHUNK)
        + [
            pltpu.VMEM((2, width, feats), BF16),
            pltpu.VMEM((rows, 2 * feats), F32),
            pltpu.VMEM((rows, width), BF16),
            pltpu.VMEM((rows, width), F32),
            pltpu.VMEM((rows, width // 2), F32),
            pltpu.SemaphoreType.DMA((7 + n,)),
        ],
        compiler_params=pltpu.CompilerParams(vmem_limit_bytes=VMEM_LIMIT),
        cost_estimate=SMALL,
        name="key_last",
    )(lists, counts, sec, q, kv, w, acc, *pays, video, gain, base, g)


def per_device(video, target, gain, w_qkv, w_out, neighbours, counts):
    tt, th, tw, tube, width = video.shape
    feats = w_qkv.shape[2]
    nb = neighbours.shape[3]
    rows = tt * th * tw * tube
    n_t, n_h = lax.axis_size("tm"), lax.axis_size("height")
    t_here, h_here, sec = lax.axis_index("tm"), lax.axis_index("height"), lax.axis_index("section")
    off_chip = [p for h in range(1, n_h - 1, 2) for p in ((h, h + 1), (h + 1, h))]
    on_chip = [(h, h ^ 1) for h in range(n_h)]
    pair_times = [(t, t ^ 1) for t in range(n_t)]
    other_times = [p for t in range(1, n_t - 1, 2) for p in ((t, t + 1), (t + 1, t))]
    swap = [(0, 1), (1, 0)]

    def from_pair(x):
        return lax.ppermute(x, "tm", pair_times)

    def from_other(x):
        return lax.ppermute(x, "tm", other_times)

    def from_off(x):
        return lax.ppermute(x, "height", off_chip)

    def from_mate(x):
        return lax.ppermute(x, "height", on_chip)

    video = video.reshape(rows, width)
    target = target.reshape(rows, width)
    w = jnp.transpose(w_qkv, (1, 0, 2))

    off, mate, pair, other = from_off(video), from_mate(video), from_pair(video), from_other(video)
    meta = jnp.concatenate(
        [neighbours.reshape(tw, nb) + 1, jnp.pad(counts.reshape(1, tw), ((0, 0), (0, nb - tw)))], axis=0
    )
    own_video, meta, _ = lax.optimization_barrier((video, meta, mate))
    kv, own_q = project_own(own_video, gain, w)
    pair, other, kv = lax.optimization_barrier((pair, other, kv))
    three = jnp.stack([meta, from_pair(meta), from_other(meta)])
    off, kv, three = lax.optimization_barrier((off, kv, three))
    off_meta, mate_meta = from_off(three), from_mate(three)
    corners = from_pair(off), from_other(off)
    mates = mate, from_mate(pair), from_mate(other)
    rest = (pair, other, off, *mates)
    kv = project_near((pair, other, off, *mates), 6, gain, w, kv)
    kv = kv.reshape(BLOCKS * tw, tube, 2 * feats)

    meta = jnp.concatenate([three, off_meta[:1], mate_meta, off_meta[1:]])
    listed = (meta[:, :tw] - 1).reshape(9 * tw, nb)
    count_all = meta[:, tw, :tw]

    ids = neighbours.reshape(tw, nb)
    t_of, h_of, w_of = ids // (n_h * tw), ids // tw % n_h, ids % tw
    step = jnp.where(t_of == t_here, 0, jnp.where(t_of == t_here + 1 - 2 * (t_here % 2), 1, 2))
    slot = jnp.where(
        h_of == h_here,
        step,
        jnp.where(h_of == h_here + 1 - 2 * (h_here % 2), 4 + step, jnp.where(step == 0, 3, 6 + step)),
    )
    local = slot * tw + w_of
    own_ids = (t_here * n_h + h_here) * tw + jnp.arange(tw, dtype=jnp.int32)
    names = jnp.any(listed[None] == own_ids[:, None, None], axis=2)

    def listing(first, last, most):
        named = names[:, first:last]
        where = jnp.arange(last - first, dtype=jnp.int32)
        rank = jnp.sum(named[:, None, :] & (where[None, :] < where[:, None])[None], axis=2)
        hit = named[:, None, :] & (rank[:, None, :] == jnp.arange(most)[None, :, None])
        places = jnp.sum(jnp.where(hit, where, 0), axis=2).astype(jnp.int32)
        return jnp.concatenate([places, jnp.sum(named, axis=1, keepdims=True).astype(jnp.int32)], axis=1)

    near_list = listing(0, 7 * tw, 24)
    last_list = listing(7 * tw, 9 * tw, 8)
    sec = sec.reshape(1).astype(jnp.int32)
    own_counts = counts.reshape(tw)

    part, o, lse, p, far = attend_forward(local, count_all, *corners, gain, w, kv, own_q, w_out)
    other = lax.ppermute(part, "section", swap)
    part, videos = lax.optimization_barrier((part, (*rest, *corners)))
    far_q = project_queries(videos, gain, w).reshape(8 * tw, tube, feats)
    other, far_q, near_list, last_list = lax.optimization_barrier((other, far_q, near_list, last_list))
    pay, g = middle(own_counts, sec, part, other, video, target, w_out, o, lse)
    off, mate = from_off(pay), from_mate(pay)
    pair, after = from_pair(pay), from_other(pay)
    dq = query_grad(local, pay, kv, far, p)
    dq, off, pair, after = lax.optimization_barrier((dq, off, pair, after))
    near, mates, corners = (pay, pair, after, off), (mate, from_mate(pair), from_mate(after)), (from_pair(off), from_other(off))
    acc, base = key_near(
        near_list, own_counts, own_q.reshape(tw, tube, feats), far_q, kv, w, dq, [*near, *mates]
    )
    send, keep = key_last(6, last_list, own_counts, sec, far_q, kv, w, acc, corners, video, gain, base, g)
    got = lax.ppermute(send, "section", swap)
    return (keep + got.astype(F32)).astype(BF16).reshape(tt, th, tw, tube, width // 2)


def solution(mesh):
    in_specs = (
        P("tm", "height", None, None, None),
        P("tm", "height", None, None, None),
        P(),
        P(None, None, "section"),
        P("section", None),
        P("tm", "height", None, None),
        P("tm", "height", None),
    )
    out_specs = P("tm", "height", None, None, "section")
    return jax.shard_map(
        per_device, mesh=mesh, in_specs=in_specs, out_specs=out_specs, check_vma=False
    )
```
